32 devices in a mesh: img: 8 (over z, x), blk: 4 (over y, core).
Axes of the slice: x: 2, y: 2, z: 4, core: 2. Of those that a mesh axis runs over, the one named last changes fastest.
Arguments:
- x_large: bfloat16 [128, 14, 14, 1024], P(('img', 'blk')), may hold values from -18 to 18
- x_small: bfloat16 [256, 6, 6, 1024], P(('img', 'blk')), may hold values from -18 to 18
- large_image: int32 [128], P(('img', 'blk')), may hold values from 0 to 63, as said below
- small_image: int32 [256], P(('img', 'blk')), may hold values from 0 to 63, as said below
- first_reduce: bfloat16 [1024, 512], P('img'), may hold values from -0.1875 to 0.1875
- first_spatial: bfloat16 [3, 3, 512, 512], P(None, None, 'img'), may hold values from -0.09375 to 0.09375
- first_expand: bfloat16 [512, 2048], P('img'), may hold values from -0.25 to 0.25
- first_short: bfloat16 [1024, 2048], P('img'), may hold values from -0.1875 to 0.1875
- second_reduce: bfloat16 [2048, 512], P('img'), may hold values from -0.125 to 0.125
- second_spatial: bfloat16 [3, 3, 512, 512], P(None, None, 'img'), may hold values from -0.09375 to 0.09375
- second_expand: bfloat16 [512, 2048], P('img'), may hold values from -0.25 to 0.25
- head_hidden: bfloat16 [2048, 2048], P('img'), may hold values from -0.125 to 0.125
- head_embed: bfloat16 [2048, 128], P('img'), may hold values from -0.125 to 0.125
- norm_gain: float32 [10240], replicated, may hold values from 0.5 to 1.5
- norm_shift: float32 [10240], replicated, may hold values from -0.5 to 0.5
Outputs:
- loss: float32 [], replicated
- grad_large: bfloat16 [128, 14, 14, 1024], P(('img', 'blk'))
- grad_small: bfloat16 [256, 6, 6, 1024], P(('img', 'blk'))
- first_reduce_grad: float32 [1024, 512], P('img')
- first_spatial_grad: float32 [3, 3, 512, 512], P(None, None, 'img')
- first_expand_grad: float32 [512, 2048], P('img')
- first_short_grad: float32 [1024, 2048], P('img')
- second_reduce_grad: float32 [2048, 512], P('img')
- second_spatial_grad: float32 [3, 3, 512, 512], P(None, None, 'img')
- second_expand_grad: float32 [512, 2048], P('img')
- head_hidden_grad: float32 [2048, 2048], P('img')
- head_embed_grad: float32 [2048, 128], P('img')
- norm_gain_grad: float32 [10240], replicated
- norm_shift_grad: float32 [10240], replicated
The draws below stay inside these ranges and needn't reach their ends.
Inputs may be any that keep to these rules, and one draw needn't show every extreme that they name: `large_image`: the images fall into groups of 2 in a row; the d-th aligned block of 4 entries holds each image of one group exactly 2 times, in an order drawn from the seed, and which group each block holds is a permutation of the groups drawn from the seed. `small_image`: the d-th aligned block of 8 entries holds each image of the group of the large views' block (d + 16) modulo 64 / 2 exactly 4 times, in an order drawn from the seed.
All inputs are finite; a program needn't handle non-finite values.
Results may differ from the reference program's by a relative error of at most 0.024.
Values may be sent and summed in bfloat16 or wider, within the bound.
No kernel may reach another device: no remote copies, remote signals or barrier semaphores. Data moves between devices by JAX's collectives and lax.ppermute only.
A program may use at most 192 MiB of HBM per device.

```python
import jax
import jax.numpy as jnp
from jax import lax

C_IN = 1024
MID = 512
C_OUT = 2048
PROJ = 2048
EMB = 128
LARGE_SIDE = 14
SMALL_SIDE = 6
LARGE_VIEWS = 2
SMALL_VIEWS = 4
IMG_DEV = 2
IMAGES = 64
POSITIVES = 5
NORM_WIDTH = 10240
N_BLK = 4


def group_order(key):
    groups = IMAGES // IMG_DEV
    return jax.random.permutation(jax.random.fold_in(key, 30), jnp.arange(groups, dtype=jnp.int32)).astype(jnp.int32)


def view_images(key, order, per_image, turn):
    groups = IMAGES // IMG_DEV
    owners = order[(jnp.arange(groups, dtype=jnp.int32) + turn) % groups]
    rows = owners[:, None] * IMG_DEV + jnp.repeat(jnp.arange(IMG_DEV, dtype=jnp.int32), per_image)[None, :]
    row_keys = jax.random.split(key, groups)
    shuffled = jax.vmap(jax.random.permutation)(row_keys, rows)
    return shuffled.reshape(-1).astype(jnp.int32)


def large_labels(key):
    return view_images(jax.random.fold_in(key, 31), group_order(key), LARGE_VIEWS, 0)


def small_labels(key):
    return view_images(jax.random.fold_in(key, 32), group_order(key), SMALL_VIEWS, IMAGES // IMG_DEV // 2)


def normal_field(key, labels, breadth, common):
    number = labels.shape[0]
    layout = (number, breadth, breadth, C_IN)
    groups = IMAGES // IMG_DEV
    block_place = (labels // IMG_DEV).astype(jnp.float32) / groups
    weight_share = 0.95 * (1.0 - block_place)
    rest_share = jnp.sqrt(1.0 - weight_share * weight_share)
    noise = jnp.clip(jax.random.normal(key, layout, jnp.float32), -6.0, 6.0)
    mixed = weight_share[:, None, None, None] * common[labels][:, None, None, :] + rest_share[:, None, None, None] * noise
    mixed = jnp.clip(mixed, -6.0, 6.0)
    position = jnp.arange(number, dtype=jnp.float32) / number
    factor = 3.0 ** position
    return (mixed * factor[:, None, None, None]).astype(jnp.bfloat16)


def common_normal(key):
    return jnp.clip(jax.random.normal(jax.random.fold_in(key, 41), (IMAGES, C_IN), jnp.float32), -6.0, 6.0)


def draw_x_large(key, part):
    labels = large_labels(key)
    return normal_field(jax.random.fold_in(key, 11), labels, LARGE_SIDE, common_normal(key))


def draw_x_small(key, part):
    labels = small_labels(key)
    return normal_field(jax.random.fold_in(key, 12), labels, SMALL_SIDE, common_normal(key))


def draw_large_image(key, part):
    return large_labels(key)


def draw_small_image(key, part):
    return small_labels(key)


def block_scale(key, shape, cuts, smallest, high):
    gain = 1.0
    for dim, shards_of in cuts:
        steps = jax.random.uniform(jax.random.fold_in(jax.random.fold_in(key, 6), dim), (shards_of,), jnp.float32, smallest / len(cuts), high / len(cuts))
        gain = gain * jnp.repeat(jnp.exp(steps), shape[dim] // shards_of).reshape((-1,) + (1,) * (len(shape) - 1 - dim))
    return gain


def normal_values(own_key, extent, scale, most, cuts=(), kind=jnp.bfloat16):
    result = scale * jax.random.normal(own_key, extent, jnp.float32)
    if cuts:
        result = result * block_scale(own_key, extent, cuts, -0.22, 0.18)
    return jnp.clip(result, -most, most).astype(kind)


def setup_inputs(seed: int = 0) -> dict:
    arg_keys = jax.random.split(jax.random.key(seed), 16)
    return {
        "x_large": draw_x_large(jax.random.fold_in(arg_keys[15], 71), 0),
        "x_small": draw_x_small(jax.random.fold_in(arg_keys[15], 71), 0),
        "large_image": draw_large_image(jax.random.fold_in(arg_keys[15], 71), 0),
        "small_image": draw_small_image(jax.random.fold_in(arg_keys[15], 71), 0),
        "first_reduce": normal_values(arg_keys[4], (C_IN, MID), C_IN ** -0.5, 0.1875, ((0, 8),)),
        "first_spatial": normal_values(arg_keys[5], (3, 3, MID, MID), (9 * MID) ** -0.5, 0.09375, ((2, 8),)),
        "first_expand": normal_values(arg_keys[6], (MID, C_OUT), MID ** -0.5, 0.25, ((0, 8),)),
        "first_short": normal_values(arg_keys[7], (C_IN, C_OUT), C_IN ** -0.5, 0.1875, ((0, 8),)),
        "second_reduce": normal_values(arg_keys[8], (C_OUT, MID), C_OUT ** -0.5, 0.125, ((0, 8),)),
        "second_spatial": normal_values(arg_keys[9], (3, 3, MID, MID), (9 * MID) ** -0.5, 0.09375, ((2, 8),)),
        "second_expand": normal_values(arg_keys[10], (MID, C_OUT), MID ** -0.5, 0.25, ((0, 8),)),
        "head_hidden": normal_values(arg_keys[11], (C_OUT, PROJ), C_OUT ** -0.5, 0.125, ((0, 8),)),
        "head_embed": normal_values(arg_keys[12], (PROJ, EMB), PROJ ** -0.5, 0.125, ((0, 8),)),
        "norm_gain": jnp.clip(1.0 + 0.1 * jax.random.normal(arg_keys[13], (NORM_WIDTH,), jnp.float32), 0.5, 1.5),
        "norm_shift": jnp.clip(jax.random.uniform(arg_keys[14], (NORM_WIDTH,), jnp.float32, -0.5, 0.5), -0.5, 0.5),
    }


EPSILON = 1e-05
NORM_EPSILON = 1e-06
SOFTMAX_TEMP = 0.1
MASKED = -1e+30
FULL_PRECISION = lax.Precision.HIGHEST

@jax.custom_vjp
def low(v):
    return lax.optimization_barrier(v.astype(jnp.bfloat16)).astype(jnp.float32)

@jax.custom_vjp
def low_back(v):
    return v

def low_keep(v):
    return (low(v), None)

def low_pass(kept, grad):
    return (grad,)

def back_keep(v):
    return (v, None)

def back_low(kept, grad):
    return (low(grad),)
low.defvjp(low_keep, low_pass)
low_back.defvjp(back_keep, back_low)

def batch_norm(members, gain_vector, shift_vector):
    reduced = tuple(range(members[0].ndim - 1))
    number = sum((member.size // member.shape[-1] for member in members))
    center = sum((lax.optimization_barrier(jnp.sum(member, reduced)) for member in members)) / number
    spread = sum((lax.optimization_barrier(jnp.sum(jnp.square(member - center), reduced)) for member in members)) / number
    factor = lax.rsqrt(spread + EPSILON) * gain_vector
    return [(member - center) * factor + shift_vector for member in members]

def pointwise(frames, weight):
    return jnp.einsum('nhwc,cd->nhwd', frames, weight, precision=FULL_PRECISION)

def spatial(frames, weight, stride):
    return lax.conv_general_dilated(frames, weight, (stride, stride), ((1, 1), (1, 1)), dimension_numbers=('NHWC', 'HWIO', 'NHWC'), precision=FULL_PRECISION)

def smooth_all(members):
    return [jax.nn.silu(member) for member in members]

def forward(x_large, x_small, first_reduce, first_spatial, first_expand, first_short, second_reduce, second_spatial, second_expand, head_hidden, head_embed, norm_gain, norm_shift, labels):
    widths = [MID, MID, C_OUT, C_OUT, MID, MID, C_OUT, PROJ]
    starts = [sum(widths[:layer_index]) for layer_index in range(8)]

    def normalize(layer_index, members):
        begin = starts[layer_index]
        finish = begin + widths[layer_index]
        return batch_norm(members, norm_gain[begin:finish], norm_shift[begin:finish])
    inputs = [x_large, x_small]
    reduced = [low_back(pointwise(member, first_reduce)) for member in inputs]
    reduced_low = [low(member) for member in smooth_all(normalize(0, reduced))]
    turned = [low_back(spatial(member, first_spatial, 2)) for member in reduced_low]
    turned_low = [low(member) for member in smooth_all(normalize(1, turned))]
    expanded = [low_back(pointwise(member, first_expand)) for member in turned_low]
    skipped = [low_back(pointwise(member[:, ::2, ::2], first_short)) for member in inputs]
    branch = normalize(2, expanded)
    shortcut = normalize(3, skipped)
    block_out = [jax.nn.silu(first_term + second_term) for first_term, second_term in zip(branch, shortcut)]
    block_low = [low(member) for member in block_out]
    mixing = [low_back(pointwise(member, second_reduce)) for member in block_low]
    mixing_low = [low(member) for member in smooth_all(normalize(4, mixing))]
    rotated = [low_back(spatial(member, second_spatial, 1)) for member in mixing_low]
    rotated_low = [low(member) for member in smooth_all(normalize(5, rotated))]
    widened = [low_back(pointwise(member, second_expand)) for member in rotated_low]
    grown_out = normalize(6, widened)
    final_out = [jax.nn.silu(first_term + second_term) for first_term, second_term in zip(grown_out, block_out)]
    pooled = jnp.concatenate([lax.optimization_barrier(jnp.mean(member, (1, 2))) for member in final_out], 0)
    head_linear = low_back(jnp.dot(low(pooled), head_hidden, precision=FULL_PRECISION))
    head_low = low(jax.nn.silu(normalize(7, [head_linear])[0]))
    embedding = low_back(jnp.dot(head_low, head_embed, precision=FULL_PRECISION))
    unit_rows = embedding * lax.rsqrt(lax.optimization_barrier(jnp.sum(jnp.square(embedding), 1, keepdims=True)) + NORM_EPSILON)
    unit_lowered = low(unit_rows)
    anchors = jnp.arange(unit_lowered.shape[0], dtype=jnp.int32)
    block_rows = (POSITIVES + 1) * IMG_DEV * N_BLK

    def block_loss(block_inputs):
        block_of_rows, label_block, index_block = block_inputs
        similarity_scores = low_back(jnp.dot(block_of_rows, unit_lowered.T, precision=FULL_PRECISION) / SOFTMAX_TEMP)
        itself = index_block[:, None] == anchors[None, :]
        paired = (label_block[:, None] == labels[None, :]) & jnp.logical_not(itself)
        masked = jnp.where(itself, MASKED, similarity_scores)
        highest = lax.optimization_barrier(jnp.max(masked, 1, keepdims=True))
        log_total = highest[:, 0] + jnp.log(lax.optimization_barrier(jnp.sum(jnp.where(itself, 0.0, jnp.exp(masked - highest)), 1)))
        positive = lax.optimization_barrier(jnp.sum(jnp.where(paired, similarity_scores, 0.0), 1))
        return jnp.sum(log_total - positive / POSITIVES)
    losses = lax.map(jax.checkpoint(block_loss), (unit_lowered.reshape(-1, block_rows, unit_lowered.shape[1]), labels.reshape(-1, block_rows), anchors.reshape(-1, block_rows)))
    return jnp.sum(losses) / unit_lowered.shape[0]

def reference(x_large, x_small, large_image, small_image, first_reduce, first_spatial, first_expand, first_short, second_reduce, second_spatial, second_expand, head_hidden, head_embed, norm_gain, norm_shift):
    labels = jnp.concatenate([large_image, small_image], 0).astype(jnp.int32)
    floats = [array_in.astype(jnp.float32) for array_in in (x_large, x_small, first_reduce, first_spatial, first_expand, first_short, second_reduce, second_spatial, second_expand, head_hidden, head_embed, norm_gain, norm_shift)]
    loss_value, pullback = jax.vjp(lambda *arrays: forward(*arrays, labels), *floats)
    gradients = pullback(jnp.ones_like(loss_value))
    return (loss_value, gradients[0].astype(jnp.bfloat16), gradients[1].astype(jnp.bfloat16), gradients[2], gradients[3], gradients[4], gradients[5], gradients[6], gradients[7], gradients[8], gradients[9], gradients[10], gradients[11], gradients[12])
```

```python
import functools

import jax
import jax.numpy as jnp
import numpy as np
from jax import lax
from jax.experimental import pallas as pl
from jax.experimental.pallas import tpu as pltpu
from jax.sharding import PartitionSpec as P

POSITIVES = 5
EPSILON = 1e-05
NORM_EPSILON = 1e-06
SOFTMAX_TEMP = 0.1
MASKED = -1e30
GUARD = 16
SLOT = 16
VMEM_LIMIT = 56 * 1024 * 1024
AXES = ("img", "blk")
F32 = jnp.float32
BF16 = jnp.bfloat16

NN = (((1,), (0,)), ((), ()))
NT = (((1,), (1,)), ((), ()))
TN = (((0,), (0,)), ((), ()))


def dot(left, right, dims=NN):
    return lax.dot_general(left, right, dims, preferred_element_type=F32)


def call(kernel, grid, inputs, outputs, scratch=(), flops=0):
    moved = sum(a.size * a.dtype.itemsize for a, _, _ in inputs)
    moved += sum(int(np.prod(s)) * jnp.dtype(d).itemsize for s, d, _, _ in outputs)
    return pl.pallas_call(
        kernel,
        grid=grid,
        in_specs=[pl.BlockSpec(b, m) for _, b, m in inputs],
        out_specs=[pl.BlockSpec(b, m) for _, _, b, m in outputs],
        out_shape=[jax.ShapeDtypeStruct(s, d) for s, d, _, _ in outputs],
        scratch_shapes=list(scratch),
        compiler_params=pltpu.CompilerParams(vmem_limit_bytes=VMEM_LIMIT),
        cost_estimate=pl.CostEstimate(flops=flops, bytes_accessed=moved, transcendentals=0),
    )(*[a for a, _, _ in inputs])


def whole(a):
    return (a, a.shape, lambda *_: (0,) * a.ndim)


def cols(a, width):
    return (a, a.shape[:-1] + (width,), lambda i: (0,) * (a.ndim - 1) + (i,))


def rows(a, height):
    return (a, (height,) + a.shape[1:], lambda i: (i,) + (0,) * (a.ndim - 1))


def out_whole(shape, dtype):
    return (shape, dtype, shape, lambda *_: (0,) * len(shape))


def out_cols(shape, dtype, width):
    return (shape, dtype, shape[:-1] + (width,), lambda i: (0,) * (len(shape) - 1) + (i,))


def sigmoid(v):
    return 1.0 / (1.0 + jnp.exp(-v))


def spread(mask, width):
    return jnp.concatenate([mask] * (width // mask.shape[1]), 1)


def column_sum(v):
    return jnp.sum(v, 0, keepdims=True)


class Frames:
    def __init__(self, large, small):
        self.large, self.small = large.shape[0], small.shape[0]
        self.large_in, self.small_in = large.shape[1], small.shape[1]
        self.lo, self.so = self.large_in // 2, self.small_in // 2
        self.lp, self.sp = self.lo + 1, self.so + 1
        self.lrows, self.srows = self.large * self.lp**2, self.small * self.sp**2
        self.rows = self.lrows + self.srows
        self.valid = self.large * self.lo**2 + self.small * self.so**2
        self.views = self.large + self.small

    def mask(self):
        def grid(number, out):
            g = np.zeros((number, out + 1, out + 1), np.float32)
            g[:, :out, :out] = 1
            return g.reshape(-1)

        m = np.concatenate([grid(self.large, self.lo), grid(self.small, self.so)])
        return jnp.asarray(np.repeat(m[:, None], 128, 1))

    def cells(self):
        c = np.zeros((SLOT, 1), np.float32)
        c[: self.large] = 1.0 / self.lo**2
        c[self.large : self.views] = 1.0 / self.so**2
        return c

    def shifted(self, ref, row, col):
        a = GUARD + row * self.lp + col
        b = GUARD + self.lrows + row * self.sp + col
        return jnp.concatenate([ref[a : a + self.lrows, :], ref[b : b + self.srows, :]], 0)

    def per_view(self, v):
        w = v.shape[1]
        large = jnp.sum(v[: self.lrows].reshape(self.large, -1, w), 1)
        small = jnp.sum(v[self.lrows :].reshape(self.small, -1, w), 1)
        return large, small

    def to_rows(self, v):
        w = v.shape[1]
        large = jnp.broadcast_to(
            v[: self.large][:, None, :], (self.large, self.lp**2, w)
        ).reshape(self.lrows, w)
        small = jnp.broadcast_to(
            v[self.large : self.views][:, None, :], (self.small, self.sp**2, w)
        ).reshape(self.srows, w)
        return jnp.concatenate([large, small], 0)


class Norm:
    def __init__(self, stats, affine, count):
        self.center = stats[0:1, :]
        self.factor = lax.rsqrt(stats[1:2, :] / count + EPSILON)
        self.gain = affine[0:1, :]
        self.offset = affine[1:2, :]
        self.count = count

    def hat(self, v):
        return (v - self.center) * self.factor

    def scaled(self, hat):
        return hat * self.gain + self.offset

    def backward(self, d, hat, sums):
        return (self.gain * self.factor) * (
            d - sums[0:1, :] / self.count - hat * (sums[1:2, :] / self.count)
        )


def slope(v):
    s = sigmoid(v)
    return s * (1.0 + v * (1.0 - s))


def store_stats(ref, blocks, mask, count):
    center = sum(column_sum(b[...] * mask) for b in blocks) / count
    square = sum(column_sum(jnp.square((b[...] - center) * mask)) for b in blocks)
    ref[0:1, :] = center
    ref[1:2, :] = square


def lanes(width):
    return [slice(at, at + 128) for at in range(0, width, 128)]


def parity_pieces(f):
    for large, number, out, pitch, base in (
        (True, f.large, f.lo, f.lp, 0),
        (False, f.small, f.so, f.sp, f.lrows),
    ):
        for n in range(number):
            for i in range(out):
                for ph in range(2):
                    for pw in range(2):
                        at = (2 * ph + pw) * f.rows + base + n * pitch**2 + i * pitch
                        yield large, n, 2 * i + ph, pw, at, pitch


def split_kernel(f, large_ref, small_ref, out_ref, lt, st, acc):
    acc[...] = jnp.zeros_like(acc)
    for k, lane in enumerate(lanes(out_ref.shape[1])):
        for t, ref, side in ((lt, large_ref, f.large_in), (st, small_ref, f.small_in)):
            t[k] = jnp.zeros_like(t[k])
            t[k, :, :, 0:side, :] = ref[:, :, :, lane].astype(F32)
        for large, n, row, pw, at, pitch in parity_pieces(f):
            t = lt if large else st
            acc[at : at + pitch, lane] = t[k, n, row, pl.ds(pw, pitch, stride=2), :]
    out_ref[...] = acc[...].astype(BF16)


def parity_scratch(f, width):
    return [
        pltpu.VMEM((width // 128, f.large, f.large_in, 2 * f.lp, 128), F32),
        pltpu.VMEM((width // 128, f.small, f.small_in, 2 * f.sp, 128), F32),
        pltpu.VMEM((4 * f.rows, width), F32),
    ]


def split_cells(f, large, small, width=256):
    c = large.shape[3]
    return call(
        functools.partial(split_kernel, f),
        (c // width,),
        [cols(large, width), cols(small, width)],
        [out_cols((4 * f.rows, c), BF16, width)],
        parity_scratch(f, width),
    )[0]


def linear_kernel(f, count, x_ref, w_ref, mask_ref, out_ref, stats_ref):
    width = out_ref.shape[1]
    mask = spread(mask_ref[...], width)
    blocks = []
    for at in range(0, out_ref.shape[0], f.rows):
        block = out_ref.at[at : at + f.rows, :]
        block[...] = dot(x_ref[at : at + f.rows, :], w_ref[...])
        blocks.append(block)
    store_stats(stats_ref, blocks, mask, count)


def linear(f, x, w, mask, phases, width):
    n = w.shape[1]
    x_in = (x, (phases * f.rows, x.shape[1]), lambda i: (0, 0))
    return call(
        functools.partial(linear_kernel, f, phases * f.valid),
        (n // width,),
        [x_in, cols(w, width), whole(mask)],
        [out_cols((phases * f.rows, n), F32, width), out_cols((2, n), F32, width)],
        flops=2 * phases * f.rows * w.size,
    )


TAPS = [(p, q) for p in range(3) for q in range(3)]


def conv_kernel(
    f, stride, count, pre_ref, stats_ref, affine_ref, w_ref, mask_ref,
    patch_ref, out_ref, new_ref, act,
):
    width = pre_ref.shape[1]

    @pl.when(pl.program_id(0) == 0)
    def _():
        norm = Norm(stats_ref, affine_ref, count)
        mask = spread(mask_ref[...], width)
        for phase in range(act.shape[0]):
            act[phase, 0:GUARD, :] = jnp.zeros((GUARD, width), F32)
            act[phase, GUARD + f.rows :, :] = jnp.zeros((GUARD, width), F32)
            v = norm.scaled(norm.hat(pre_ref[phase * f.rows : (phase + 1) * f.rows, :]))
            act[phase, GUARD : GUARD + f.rows, :] = v * sigmoid(v) * mask
        for tap, (p, q) in enumerate(TAPS):
            if stride == 2:
                phase = 2 * (p != 1) + (q != 1)
                step = (-(p == 0), -(q == 0))
            else:
                phase, step = 0, (p - 1, q - 1)
            patch_ref[:, tap * width : (tap + 1) * width] = f.shifted(
                act.at[phase], *step
            ).astype(BF16)

    out_ref[...] = dot(patch_ref[...], w_ref[...])
    store_stats(new_ref, [out_ref], spread(mask_ref[...], out_ref.shape[1]), f.valid)


def conv(f, stride, count, pre, stats, affine, w, mask, tile=256):
    c, n = pre.shape[1], w.shape[1]
    phases = stride * stride
    return call(
        functools.partial(conv_kernel, f, stride, count),
        (n // tile,),
        [whole(pre), whole(stats), whole(affine), cols(w, tile), whole(mask)],
        [
            out_whole((f.rows, 9 * c), BF16),
            out_cols((f.rows, n), F32, tile),
            out_cols((2, n), F32, tile),
        ],
        [pltpu.VMEM((phases, f.rows + 2 * GUARD, c), F32)],
        flops=2 * f.rows * w.size,
    )


def expand_kernel(f, count, pre_ref, stats_ref, affine_ref, w_ref, mask_ref, low_ref, out_ref, new_ref):
    @pl.when(pl.program_id(0) == 0)
    def _():
        norm = Norm(stats_ref, affine_ref, count)
        v = norm.scaled(norm.hat(pre_ref[...]))
        low_ref[...] = (v * sigmoid(v) * spread(mask_ref[...], v.shape[1])).astype(BF16)

    out_ref[...] = dot(low_ref[...], w_ref[...])
    store_stats(new_ref, [out_ref], spread(mask_ref[...], out_ref.shape[1]), f.valid)


def expand(f, count, pre, stats, affine, w, mask, tile=512):
    c, n = w.shape
    return call(
        functools.partial(expand_kernel, f, count),
        (n // tile,),
        [whole(pre), whole(stats), whole(affine), cols(w, tile), whole(mask)],
        [
            out_whole((f.rows, c), BF16),
            out_cols((f.rows, n), F32, tile),
            out_cols((2, n), F32, tile),
        ],
        flops=2 * f.rows * w.size,
    )


def mix_kernel(
    f, count, exp_ref, skip_ref, stats_a, affine_a, stats_b, affine_b, w_ref, mask_ref,
    low_ref, pre_ref, out_ref, new_ref,
):
    step = pl.program_id(0)
    mask = spread(mask_ref[...], exp_ref.shape[1])
    first = Norm(stats_a, affine_a, count)
    second = Norm(stats_b, affine_b, count)
    v = first.scaled(first.hat(exp_ref[...])) + second.scaled(second.hat(skip_ref[...]))
    pre_ref[...] = v
    low = (v * sigmoid(v) * mask).astype(BF16)
    low_ref[...] = low
    part = dot(low, w_ref[...])

    @pl.when(step == 0)
    def _():
        out_ref[...] = part

    @pl.when(step > 0)
    def _():
        out_ref[...] += part

    @pl.when(step == pl.num_programs(0) - 1)
    def _():
        store_stats(new_ref, [out_ref], spread(mask_ref[...], out_ref.shape[1]), f.valid)


def mix(f, count, expanded, skipped, stats_a, affine_a, stats_b, affine_b, w, mask, tile=512):
    k, n = w.shape
    return call(
        functools.partial(mix_kernel, f, count),
        (k // tile,),
        [cols(a, tile) for a in (expanded, skipped, stats_a, affine_a, stats_b, affine_b)]
        + [rows(w, tile), whole(mask)],
        [
            out_cols((f.rows, k), BF16, tile),
            out_cols((f.rows, k), F32, tile),
            out_whole((f.rows, n), F32),
            out_whole((2, n), F32),
        ],
        flops=2 * f.rows * w.size,
    )


def pool_kernel(
    f, count, wide_ref, pre_ref, stats_ref, affine_ref, mask_ref,
    pooled_ref, slope_ref, view_ref,
):
    mask = spread(mask_ref[...], wide_ref.shape[1])
    norm = Norm(stats_ref, affine_ref, count)
    hat = norm.hat(wide_ref[...])
    before = pre_ref[...]
    v = norm.scaled(hat) + before * sigmoid(before)
    s = sigmoid(v)
    d = s * (1.0 + v * (1.0 - s)) * mask
    slope_ref[...] = d

    def put(ref, at, pair, scale=(1.0, 1.0)):
        ref[at : at + f.large, :] = pair[0] * scale[0]
        ref[at + f.large : at + f.views, :] = pair[1] * scale[1]
        if f.views < SLOT:
            ref[at + f.views : at + SLOT, :] = jnp.zeros((SLOT - f.views, ref.shape[1]), F32)

    put(pooled_ref, 0, f.per_view(v * s * mask), (1.0 / f.lo**2, 1.0 / f.so**2))
    put(view_ref, 0, f.per_view(d))
    put(view_ref, SLOT, f.per_view(d * hat))


def pool(f, count, wide, pre, stats, affine, mask, tile=512):
    n = wide.shape[1]
    return call(
        functools.partial(pool_kernel, f, count),
        (n // tile,),
        [cols(a, tile) for a in (wide, pre, stats, affine)] + [whole(mask)],
        [
            out_cols((SLOT, n), F32, tile),
            out_cols((f.rows, n), F32, tile),
            out_cols((2 * SLOT, n), F32, tile),
        ],
        flops=20 * wide.size,
    )


def head_kernel(
    f, devices, shard, place_ref, p_ref, h_ref, e_ref, affine_ref, label_col, label_row,
    view_ref, cells_ref,
    loss_ref, hidden_ref, embed_ref, gain_ref, back_ref, sums_ref,
    hat, low, emb, grad, own, factors, pooled_grad,
):
    step = pl.program_id(0)
    tiles = pl.num_programs(0) // 2
    v = p_ref.shape[0]
    tile = h_ref.shape[1]
    number = devices * f.views
    row_id = lax.broadcasted_iota(jnp.int32, (v, 128), 0)
    row_ok = (row_id % SLOT < f.views).astype(F32)
    mask = spread(row_ok, tile)
    gain, offset = affine_ref[0:1, :], affine_ref[1:2, :]

    @pl.when(step < tiles)
    def _():
        t = dot(p_ref[...], h_ref[...])
        center = column_sum(t * mask) / number
        t = (t - center) * mask
        factor = lax.rsqrt(column_sum(t * t) / number + EPSILON)
        t = t * factor
        hat[step] = t
        factors[step, 0:1, :] = factor
        t = t * gain + offset
        lowered = (t * sigmoid(t) * mask).astype(BF16)
        low[step] = lowered
        part = dot(lowered, e_ref[...])

        @pl.when(step == 0)
        def _():
            emb[...] = part

        @pl.when(step > 0)
        def _():
            emb[...] += part

    @pl.when(step == tiles - 1)
    def _():
        e = emb[...]
        inverse = lax.rsqrt(jnp.sum(e * e, 1, keepdims=True) + NORM_EPSILON)
        unit = e * inverse
        lowered = unit.astype(BF16)
        scores = dot(lowered, lowered, NT) / SOFTMAX_TEMP
        i = lax.broadcasted_iota(jnp.int32, (v, v), 0)
        j = lax.broadcasted_iota(jnp.int32, (v, v), 1)
        i_ok = i % SLOT < f.views
        j_ok = j % SLOT < f.views
        use = (i != j) & i_ok & j_ok
        paired = use & (label_col[:, 0:1] == label_row[0:1, :])
        weight = paired.astype(F32) / POSITIVES
        masked = jnp.where(use, scores, MASKED)

        def log_total(axis):
            top = jnp.max(masked, axis, keepdims=True)
            terms = jnp.where(use, jnp.exp(masked - top), 0.0)
            total = jnp.sum(terms, axis, keepdims=True)
            return top + jnp.log(jnp.where(total > 0.0, total, 1.0))

        by_row = log_total(1)
        by_col = log_total(0)
        positive = jnp.sum(jnp.where(paired, scores, 0.0), 1, keepdims=True)
        fine = lax.broadcasted_iota(jnp.int32, (v, 1), 0) % SLOT < f.views
        per_row = jnp.where(fine, by_row - positive / POSITIVES, 0.0)
        loss_ref[...] = jnp.broadcast_to(
            jnp.sum(per_row, 0, keepdims=True) / number, loss_ref.shape
        )

        def pair_grad(logs):
            chance = jnp.where(use, jnp.exp(masked - logs), 0.0)
            return ((chance - weight) / number).astype(BF16)

        unit_grad = (dot(pair_grad(by_row), lowered) + dot(pair_grad(by_col), lowered)) / SOFTMAX_TEMP
        along = jnp.sum(unit * unit_grad, 1, keepdims=True)
        g = inverse * (unit_grad - unit * along)
        grad[...] = jnp.where(fine, g, 0.0).astype(BF16)

    @pl.when(step >= tiles)
    def _():
        now = step - tiles
        t = hat[now]
        d = dot(grad[...], e_ref[...], NT) * slope(t * gain + offset)
        shift_grad = column_sum(d)
        gain_grad = column_sum(d * t)
        gain_ref[0:1, :] = gain_grad
        gain_ref[1:2, :] = shift_grad
        d = (factors[now, 0:1, :] * gain) * (d - shift_grad / number - t * (gain_grad / number))
        lowered = (d * mask).astype(BF16)
        own[...] = lowered
        mine = pl.multiple_of(place_ref[0] * shard, 128)
        hidden_ref[...] = dot(p_ref[:, pl.ds(mine, shard)], lowered, TN)
        here = pl.multiple_of(place_ref[1] * SLOT, SLOT)
        part = dot(own[pl.ds(here, SLOT), :], h_ref[...], NT)

        @pl.when(now == 0)
        def _():
            pooled_grad[...] = part

        @pl.when(now > 0)
        def _():
            pooled_grad[...] += part

    @pl.when(step == 2 * tiles - 1)
    def _():
        per = tile // shard if tile > shard else 1
        at = place_ref[0] // per
        inner = pl.multiple_of((place_ref[0] % per) * shard, 128)
        embed_ref[...] = dot(low[at, :, pl.ds(inner, shard)], grad[...], TN)
        b = pooled_grad[...] * cells_ref[...]
        back_ref[...] = b
        sums_ref[0:1, :] = column_sum(b * view_ref[0:SLOT, :])
        sums_ref[1:2, :] = column_sum(b * view_ref[SLOT:, :])


def head(f, devices, shard, place, pooled, hidden, embed, affine, labels, view_sums, tile=512):
    v, c = pooled.shape
    n, w = embed.shape
    tiles = n // tile
    label_col = jnp.broadcast_to(labels[:, None], (v, 128))
    label_row = jnp.broadcast_to(labels[None, :], (8, v))
    cells = jnp.asarray(np.repeat(f.cells(), c, 1))
    late = lambda i: (0, jnp.maximum(i - tiles, 0))
    inputs = [
        whole(pooled),
        (hidden, (c, tile), lambda i: (0, i % tiles)),
        (embed, (tile, w), lambda i: (i % tiles, 0)),
        (affine, (2, tile), lambda i: (0, i % tiles)),
        whole(label_col),
        whole(label_row),
        whole(view_sums),
        whole(cells),
    ]
    outputs = [
        out_whole((8, 128), F32),
        ((shard, n), F32, (shard, tile), late),
        out_whole((shard, w), F32),
        ((2, n), F32, (2, tile), late),
        out_whole((SLOT, c), F32),
        out_whole((2, c), F32),
    ]
    return pl.pallas_call(
        functools.partial(head_kernel, f, devices, shard),
        grid=(2 * tiles,),
        in_specs=[pl.BlockSpec(memory_space=pltpu.SMEM)] + [pl.BlockSpec(b, m) for _, b, m in inputs],
        out_specs=[pl.BlockSpec(b, m) for _, _, b, m in outputs],
        out_shape=[jax.ShapeDtypeStruct(s, d) for s, d, _, _ in outputs],
        scratch_shapes=[
            pltpu.VMEM((tiles, v, tile), F32),
            pltpu.VMEM((tiles, v, tile), BF16),
            pltpu.VMEM((v, w), F32),
            pltpu.VMEM((v, w), BF16),
            pltpu.VMEM((v, tile), BF16),
            pltpu.VMEM((tiles, 8, tile), F32),
            pltpu.VMEM((SLOT, c), F32),
        ],
        compiler_params=pltpu.CompilerParams(vmem_limit_bytes=VMEM_LIMIT),
        cost_estimate=pl.CostEstimate(
            flops=4 * v * c * n, bytes_accessed=20 * 1024 * 1024, transcendentals=0
        ),
    )(place, *[a for a, _, _ in inputs])


def widen_back_kernel(
    f, count, wide_ref, slope_ref, back_ref, stats_ref, affine_ref, sums_ref, w_ref,
    turn_ref, turn_stats, turn_affine, mask_ref,
    low_ref, out_ref, new_ref,
):
    step = pl.program_id(0)
    norm = Norm(stats_ref, affine_ref, count)
    hat = norm.hat(wide_ref[...])
    d = f.to_rows(back_ref[...]) * slope_ref[...]
    low = (norm.backward(d, hat, sums_ref) * spread(mask_ref[...], hat.shape[1])).astype(BF16)
    low_ref[...] = low
    finish_back(step, dot(low, w_ref[...], NT), turn_ref, turn_stats, turn_affine, count, mask_ref, out_ref, new_ref)


def finish_back(step, part, pre_ref, stats, affine, count, mask_ref, out_ref, new_ref):
    @pl.when(step == 0)
    def _():
        out_ref[...] = part

    @pl.when(step > 0)
    def _():
        out_ref[...] += part

    @pl.when(step == pl.num_programs(0) - 1)
    def _():
        norm = Norm(stats, affine, count)
        hat = norm.hat(pre_ref[...])
        d = out_ref[...] * slope(norm.scaled(hat)) * spread(mask_ref[...], hat.shape[1])
        out_ref[...] = d
        new_ref[0:1, :] = column_sum(d)
        new_ref[1:2, :] = column_sum(d * hat)


def widen_back(f, count, wide, slopes, back, stats, affine, sums, w, turn, tstats, taffine, mask, tile=512):
    c, n = w.shape
    return call(
        functools.partial(widen_back_kernel, f, count),
        (n // tile,),
        [cols(a, tile) for a in (wide, slopes, back, stats, affine, sums, w)]
        + [whole(a) for a in (turn, tstats, taffine, mask)],
        [
            out_cols((f.rows, n), BF16, tile),
            out_whole((f.rows, c), F32),
            out_whole((2, c), F32),
        ],
        flops=2 * f.rows * w.size,
    )


def conv_back_kernel(
    f, stride, count, in_count, d_ref, pre_ref, stats_ref, affine_ref, sums_ref, w_ref,
    in_ref, in_stats, in_affine, mask_ref,
    low_ref, out_ref, new_ref, act, moved,
):
    width = d_ref.shape[1]
    steps = [(a, b) for a in (0, 1) for b in (0, 1)] if stride == 2 else [(1 - p, 1 - q) for p, q in TAPS]

    @pl.when(pl.program_id(0) == 0)
    def _():
        norm = Norm(stats_ref, affine_ref, count)
        hat = norm.hat(pre_ref[...])
        low = (norm.backward(d_ref[...], hat, sums_ref) * spread(mask_ref[...], width)).astype(BF16)
        low_ref[...] = low
        act[0:GUARD, :] = jnp.zeros((GUARD, width), F32)
        act[GUARD + f.rows :, :] = jnp.zeros((GUARD, width), F32)
        act[GUARD : GUARD + f.rows, :] = low.astype(F32)
        for k, step in enumerate(steps):
            moved[k] = f.shifted(act, *step).astype(BF16)

    tile = out_ref.shape[1]
    mask = spread(mask_ref[...], tile)
    norm = Norm(in_stats, in_affine, in_count)
    total = jnp.zeros((1, tile), F32)
    total_hat = jnp.zeros((1, tile), F32)
    for phase in range(stride * stride):
        acc = None
        for tap, (p, q) in enumerate(TAPS):
            if stride == 2:
                if phase != 2 * (p != 1) + (q != 1):
                    continue
                step = (int(p == 0), int(q == 0))
            else:
                step = (1 - p, 1 - q)
            part = dot(moved[steps.index(step)], w_ref[tap], NT)
            acc = part if acc is None else acc + part
        at = phase * f.rows
        hat = norm.hat(in_ref[at : at + f.rows, :])
        d = acc * slope(norm.scaled(hat)) * mask
        out_ref[at : at + f.rows, :] = d
        total += column_sum(d)
        total_hat += column_sum(d * hat)
    new_ref[0:1, :] = total
    new_ref[1:2, :] = total_hat


def conv_back(f, stride, count, in_count, d, pre, stats, affine, sums, w, inside, istats, iaffine, mask, tile=256):
    n = d.shape[1]
    c = w.shape[1]
    phases = stride * stride
    return call(
        functools.partial(conv_back_kernel, f, stride, count, in_count),
        (c // tile,),
        [whole(a) for a in (d, pre, stats, affine, sums)]
        + [(w, (9, tile, n), lambda i: (0, i, 0))]
        + [cols(a, tile) for a in (inside, istats, iaffine)]
        + [whole(mask)],
        [
            out_whole((f.rows, n), BF16),
            out_cols((phases * f.rows, c), F32, tile),
            out_cols((2, c), F32, tile),
        ],
        [
            pltpu.VMEM((f.rows + 2 * GUARD, n), F32),
            pltpu.VMEM((4 if stride == 2 else 9, f.rows, n), BF16),
        ],
        flops=2 * f.rows * w.size,
    )


def mix_back_kernel(
    f, count, d_ref, mix_ref, stats_ref, affine_ref, sums_ref, w_ref, back_ref, slope_ref,
    pre_ref, exp_ref, exp_stats, exp_affine, skip_ref, skip_stats, skip_affine, mask_ref,
    low_ref, out_ref, new_ref,
):
    @pl.when(pl.program_id(0) == 0)
    def _():
        norm = Norm(stats_ref, affine_ref, count)
        hat = norm.hat(mix_ref[...])
        d = norm.backward(d_ref[...], hat, sums_ref)
        low_ref[...] = (d * spread(mask_ref[...], hat.shape[1])).astype(BF16)

    g = f.to_rows(back_ref[...]) * slope_ref[...] + dot(low_ref[...], w_ref[...], NT)
    g = g * slope(pre_ref[...]) * spread(mask_ref[...], g.shape[1])
    out_ref[...] = g
    first = Norm(exp_stats, exp_affine, count)
    second = Norm(skip_stats, skip_affine, count)
    new_ref[0:1, :] = column_sum(g)
    new_ref[1:2, :] = column_sum(g * first.hat(exp_ref[...]))
    new_ref[2:3, :] = column_sum(g * second.hat(skip_ref[...]))


def mix_back(
    f, count, d, mixing, stats, affine, sums, w, back, slopes, pre,
    expanded, estats, eaffine, skipped, sstats, saffine, mask, tile=512,
):
    n, c = w.shape
    return call(
        functools.partial(mix_back_kernel, f, count),
        (n // tile,),
        [whole(a) for a in (d, mixing, stats, affine, sums)]
        + [rows(w, tile)]
        + [cols(a, tile) for a in (back, slopes, pre, expanded, estats, eaffine, skipped, sstats, saffine)]
        + [whole(mask)],
        [
            out_whole((f.rows, c), BF16),
            out_cols((f.rows, n), F32, tile),
            out_cols((3, n), F32, tile),
        ],
        flops=2 * f.rows * w.size,
    )


def block_back_kernel(
    f, count, g_ref, exp_ref, exp_stats, exp_affine, skip_ref, skip_stats, skip_affine,
    sums_ref, w_ref, turn_ref, turn_stats, turn_affine, mask_ref,
    exp_low, skip_low, out_ref, new_ref,
):
    g = g_ref[...]
    mask = spread(mask_ref[...], g.shape[1])
    sums = sums_ref[...]
    first = Norm(exp_stats, exp_affine, count)
    low = (first.backward(g, first.hat(exp_ref[...]), sums[0:2]) * mask).astype(BF16)
    exp_low[...] = low
    second = Norm(skip_stats, skip_affine, count)
    other = jnp.concatenate([sums[0:1], sums[2:3]], 0)
    skip_low[...] = (second.backward(g, second.hat(skip_ref[...]), other) * mask).astype(BF16)
    finish_back(
        pl.program_id(0), dot(low, w_ref[...], NT), turn_ref, turn_stats, turn_affine,
        count, mask_ref, out_ref, new_ref,
    )


def block_back(
    f, count, g, expanded, estats, eaffine, skipped, sstats, saffine, sums, w,
    turned, tstats, taffine, mask, tile=512,
):
    c, n = w.shape
    return call(
        functools.partial(block_back_kernel, f, count),
        (n // tile,),
        [cols(a, tile) for a in (g, expanded, estats, eaffine, skipped, sstats, saffine, sums, w)]
        + [whole(a) for a in (turned, tstats, taffine, mask)],
        [
            out_cols((f.rows, n), BF16, tile),
            out_cols((f.rows, n), BF16, tile),
            out_whole((f.rows, c), F32),
            out_whole((2, c), F32),
        ],
        flops=2 * f.rows * w.size,
    )


def input_back_kernel(
    f, count, d_ref, pre_ref, stats_ref, affine_ref, sums_ref, w_ref, sub_ref, mask_ref,
    low_ref, large_ref, small_ref, lt, st, acc,
):
    @pl.when(pl.program_id(0) == 0)
    def _():
        norm = Norm(stats_ref, affine_ref, count)
        mask = spread(mask_ref[...], d_ref.shape[1])
        for phase in range(4):
            at = phase * f.rows
            hat = norm.hat(pre_ref[at : at + f.rows, :])
            d = norm.backward(d_ref[at : at + f.rows, :], hat, sums_ref)
            low_ref[at : at + f.rows, :] = (d * mask).astype(BF16)

    for phase in range(4):
        at = phase * f.rows
        part = dot(low_ref[at : at + f.rows, :], w_ref[...], NT)
        if phase == 0:
            part = part + sub_ref[...]
        acc[at : at + f.rows, :] = part
    for k, lane in enumerate(lanes(acc.shape[1])):
        for large, n, row, pw, at, pitch in parity_pieces(f):
            t = lt if large else st
            t[k, n, row, pl.ds(pw, pitch, stride=2), :] = acc[at : at + pitch, lane]
        large_ref[:, :, :, lane] = lt[k, :, :, 0 : f.large_in, :].astype(BF16)
        small_ref[:, :, :, lane] = st[k, :, :, 0 : f.small_in, :].astype(BF16)


def input_back(f, count, d, pre, stats, affine, sums, w, sub, mask, tile=256):
    n, c = w.shape
    return call(
        functools.partial(input_back_kernel, f, count),
        (n // tile,),
        [whole(a) for a in (d, pre, stats, affine, sums)]
        + [rows(w, tile), cols(sub, tile), whole(mask)],
        [
            out_whole((4 * f.rows, c), BF16),
            out_cols((f.large, f.large_in, f.large_in, n), BF16, tile),
            out_cols((f.small, f.small_in, f.small_in, n), BF16, tile),
        ],
        parity_scratch(f, tile),
        flops=8 * f.rows * w.size,
    )


class Links:
    def __init__(self):
        self.img, self.blk = lax.axis_size("img"), lax.axis_size("blk")
        self.size = self.img * self.blk
        self.me = lax.axis_index("img") * self.blk + lax.axis_index("blk")
        low, high = self.blk.bit_length() - 1, self.img.bit_length() - 1
        self.low, self.high = low, high

    def swap(self, v, bits):
        return lax.ppermute(v, AXES, [(i, i ^ bits) for i in range(self.size)])

    def stages(self):
        found = []

        def cut(start, number):
            if number % 2 and number > 1:
                found.append([1 << start])
                start, number = start + 1, number - 1
            while number > 0:
                take = min(2, number)
                found.append([1 << (start + k) for k in range(take)])
                start, number = start + take, number - take

        cut(0, self.low)
        cut(self.low, self.high)
        return found

    def partners(self, v, stage):
        if len(stage) == 1:
            return [self.swap(v, stage[0])]
        a, b = stage
        return [self.swap(v, a), self.swap(v, b), self.swap(v, a | b)]

    def total(self, v):
        for stage in self.stages():
            got = self.partners(v, stage)
            if len(got) == 1:
                v = v + got[0]
            else:
                v = (v + got[0]) + (got[1] + got[2])
        return v

    def moments(self, v, count):
        for stage in self.stages():
            got = [v] + self.partners(v, stage)
            if len(got) == 2:
                a, b = got
                center = (a[0] + b[0]) * 0.5
                square = (a[1] + b[1]) + count * (
                    jnp.square(a[0] - center) + jnp.square(b[0] - center)
                )
            else:
                a, b, c, d = got
                center = ((a[0] + b[0]) + (c[0] + d[0])) * 0.25
                square = ((a[1] + b[1]) + (c[1] + d[1])) + count * (
                    (jnp.square(a[0] - center) + jnp.square(b[0] - center))
                    + (jnp.square(c[0] - center) + jnp.square(d[0] - center))
                )
            count = count * len(got)
            v = jnp.stack([center, square])
        return v

    def gather(self, v):
        depth = 0
        for bit in reversed(range(self.low + self.high)):
            got = self.swap(v, 1 << bit)
            upper = (self.me >> bit) & 1
            v = jnp.stack(
                [jnp.where(upper == 0, v, got), jnp.where(upper == 0, got, v)], depth
            )
            depth += 1
        return v.reshape((self.size,) + v.shape[depth:])


def head_plain(f, links, pooled, hidden, embed, affine, labels):
    number = links.size * f.views
    line = dot(pooled, hidden)
    center = lax.psum(jnp.sum(line, 0), AXES) / number
    line = line - center
    factor = lax.rsqrt(lax.psum(jnp.sum(line * line, 0), AXES) / number + EPSILON)
    hat = line * factor
    v = hat * affine[0] + affine[1]
    low = (v * sigmoid(v)).astype(BF16)
    e = dot(low, embed)
    inverse = lax.rsqrt(jnp.sum(e * e, 1, keepdims=True) + NORM_EPSILON)
    unit = e * inverse
    lowered = unit.astype(BF16)
    every = lax.all_gather(lowered, AXES, axis=0, tiled=True)
    every_label = lax.all_gather(labels, AXES, axis=0, tiled=True)
    scores = dot(lowered, every, NT) / SOFTMAX_TEMP
    anchor = links.me * f.views + jnp.arange(f.views, dtype=jnp.int32)
    itself = anchor[:, None] == jnp.arange(number, dtype=jnp.int32)[None, :]
    paired = (labels[:, None] == every_label[None, :]) & jnp.logical_not(itself)
    masked = jnp.where(itself, MASKED, scores)
    top = jnp.max(masked, 1)
    log_total = top + jnp.log(jnp.sum(jnp.where(itself, 0.0, jnp.exp(masked - top[:, None])), 1))
    positive = jnp.sum(jnp.where(paired, scores, 0.0), 1)
    loss = lax.psum(jnp.sum(log_total - positive / POSITIVES), AXES) / number
    every_log = lax.all_gather(log_total, AXES, axis=0, tiled=True)

    def pair_grad(logs):
        chance = jnp.where(itself, 0.0, jnp.exp(scores - logs))
        return ((chance - paired.astype(F32) / POSITIVES) / number).astype(BF16)

    unit_grad = (
        dot(pair_grad(log_total[:, None]), every) + dot(pair_grad(every_log[None, :]), every)
    ) / SOFTMAX_TEMP
    along = jnp.sum(unit * unit_grad, 1, keepdims=True)
    grad = (inverse * (unit_grad - unit * along)).astype(BF16)
    d = dot(grad, embed, NT) * slope(v)
    shift_grad = lax.psum(jnp.sum(d, 0), AXES)
    gain_grad = lax.psum(jnp.sum(d * hat, 0), AXES)
    back = (affine[0] * factor * (d - shift_grad / number - hat * (gain_grad / number))).astype(BF16)
    return loss, dot(pooled, back, TN), dot(low, grad, TN), gain_grad, shift_grad, dot(back, hidden, NT)


def per_device(
    x_large, x_small, large_image, small_image,
    first_reduce, first_spatial, first_expand, first_short,
    second_reduce, second_spatial, second_expand, head_hidden, head_embed,
    norm_gain, norm_shift,
):
    f = Frames(x_large, x_small)
    links = Links()
    mid, wide, proj = first_reduce.shape[1], first_short.shape[1], head_hidden.shape[1]
    widths = [mid, mid, wide, wide, mid, mid, wide, proj]
    starts = np.cumsum([0] + widths)
    both = jnp.stack([norm_gain, norm_shift])
    affine = [both[:, starts[k] : starts[k + 1]] for k in range(8)]
    mask = f.mask()

    def gathered(w, axis=0):
        return lax.all_gather(w, "img", axis=axis, tiled=True)

    w_reduce = gathered(first_reduce)
    w_spatial = gathered(first_spatial, 2).reshape(9, mid, mid)
    w_expand = gathered(first_expand)
    w_short = gathered(first_short)
    w_reduce2 = gathered(second_reduce)
    w_spatial2 = gathered(second_spatial, 2).reshape(9, mid, mid)
    w_expand2 = gathered(second_expand)
    w_hidden = gathered(head_hidden)
    w_embed = gathered(head_embed)

    n_in, n_out = 4 * f.valid, f.valid
    all_in, all_out = n_in * links.size, n_out * links.size

    x = split_cells(f, x_large, x_small)
    reduced, st0 = linear(f, x, w_reduce, mask, 4, 256)
    st0 = links.moments(st0, n_in)
    patch1, turned, st1 = conv(f, 2, all_in, reduced, st0, affine[0], w_spatial.reshape(9 * mid, mid), mask)
    st1 = links.moments(st1, n_out)
    skipped, st3 = linear(f, x, w_short, mask, 1, 512)
    turned_low, expanded, st2 = expand(f, all_out, turned, st1, affine[1], w_expand, mask)
    joint = links.moments(jnp.concatenate([st2, st3], 1), n_out)
    st2, st3 = joint[:, :wide], joint[:, wide:]
    block_low, block_pre, mixing, st4 = mix(
        f, all_out, expanded, skipped, st2, affine[2], st3, affine[3], w_reduce2, mask
    )
    st4 = links.moments(st4, n_out)
    patch2, rotated, st5 = conv(f, 1, all_out, mixing, st4, affine[4], w_spatial2.reshape(9 * mid, mid), mask)
    st5 = links.moments(st5, n_out)
    rotated_low, widened, st6 = expand(f, all_out, rotated, st5, affine[5], w_expand2, mask)
    st6 = links.moments(st6, n_out)
    pooled, slopes, view_sums = pool(f, all_out, widened, block_pre, st6, affine[6], mask)
    pooled = pooled.astype(BF16)
    labels = jnp.concatenate([large_image, small_image], 0)

    shard = head_hidden.shape[0]
    joined = links.size * SLOT <= 512 and shard % 128 == 0
    if joined:
        padded = jnp.concatenate([labels, jnp.full((SLOT - f.views,), -1, jnp.int32)])
        every_label = lax.all_gather(padded, AXES, axis=0, tiled=True)
        every = links.gather(pooled).reshape(links.size * SLOT, wide)
        place = jnp.stack([lax.axis_index("img"), links.me]).astype(jnp.int32)
        loss, hidden_grad, embed_grad, gains7, back, sums6 = head(
            f, links.size, shard, place, every, w_hidden, w_embed, affine[7], every_label, view_sums
        )
        loss = loss[0, 0]
        gain7, shift7 = gains7[0], gains7[1]
    else:
        loss, hidden_part, embed_part, gain7, shift7, back = head_plain(
            f, links, pooled[: f.views], w_hidden, w_embed, affine[7], labels
        )
        back = jnp.pad(back, ((0, SLOT - f.views), (0, 0))) * f.cells()
        sums6 = jnp.stack([jnp.sum(back * view_sums[:SLOT], 0), jnp.sum(back * view_sums[SLOT:], 0)])
    sums6 = links.total(sums6)

    widened_back, d5, sums5 = widen_back(
        f, all_out, widened, slopes, back, st6, affine[6], sums6, w_expand2, rotated, st5, affine[5], mask
    )
    expand2_grad = dot(rotated_low, widened_back, TN).astype(BF16)
    sums5 = links.total(sums5)
    rotated_back, d4, sums4 = conv_back(
        f, 1, all_out, all_out, d5, rotated, st5, affine[5], sums5, w_spatial2, mixing, st4, affine[4], mask
    )
    spatial2_grad = dot(patch2, rotated_back, TN).astype(BF16)
    sums4 = links.total(sums4)
    mixing_back, block_grad, sums23 = mix_back(
        f, all_out, d4, mixing, st4, affine[4], sums4, w_reduce2, back, slopes, block_pre,
        expanded, st2, affine[2], skipped, st3, affine[3], mask,
    )
    reduce2_grad = dot(block_low, mixing_back, TN).astype(BF16)
    sums23 = links.total(sums23)
    expanded_back, skipped_back, d1, sums1 = block_back(
        f, all_out, block_grad, expanded, st2, affine[2], skipped, st3, affine[3], sums23, w_expand,
        turned, st1, affine[1], mask,
    )
    expand_grad = dot(turned_low, expanded_back, TN).astype(BF16)
    short_grad = dot(x[: f.rows], skipped_back, TN).astype(BF16)
    sub = dot(skipped_back, w_short, NT)
    sums1 = links.total(sums1)
    turned_back, d0, sums0 = conv_back(
        f, 2, all_out, all_in, d1, turned, st1, affine[1], sums1, w_spatial, reduced, st0, affine[0], mask
    )
    spatial_grad = dot(patch1, turned_back, TN).astype(BF16)
    sums0 = links.total(sums0)
    reduced_back, grad_large, grad_small = input_back(
        f, all_in, d0, reduced, st0, affine[0], sums0, w_reduce, sub, mask
    )
    reduce_grad = dot(x, reduced_back, TN).astype(BF16)

    def scattered(g, axis=0):
        g = lax.psum_scatter(g, "img", scatter_dimension=axis, tiled=True)
        return lax.psum(g, "blk").astype(F32)

    expand2_grad = scattered(expand2_grad)
    spatial2_grad = scattered(spatial2_grad.reshape(3, 3, mid, mid), 2)
    reduce2_grad = scattered(reduce2_grad)
    expand_grad = scattered(expand_grad)
    short_grad = scattered(short_grad)
    spatial_grad = scattered(spatial_grad.reshape(3, 3, mid, mid), 2)
    reduce_grad = scattered(reduce_grad)
    if not joined:
        hidden_grad = scattered(hidden_part.astype(BF16))
        embed_grad = scattered(embed_part.astype(BF16))

    gain_grads = jnp.concatenate(
        [sums0[1], sums1[1], sums23[1], sums23[2], sums4[1], sums5[1], sums6[1], gain7]
    )
    shift_grads = jnp.concatenate(
        [sums0[0], sums1[0], sums23[0], sums23[0], sums4[0], sums5[0], sums6[0], shift7]
    )
    return (
        loss, grad_large, grad_small, reduce_grad, spatial_grad, expand_grad, short_grad,
        reduce2_grad, spatial2_grad, expand2_grad, hidden_grad, embed_grad, gain_grads, shift_grads,
    )


def solution(mesh):
    image = P(("img", "blk"), None, None, None)
    label = P(("img", "blk"))
    matrix = P("img", None)
    kernel = P(None, None, "img", None)
    weights = (matrix, kernel, matrix, matrix, matrix, kernel, matrix, matrix, matrix)
    return jax.shard_map(
        per_device,
        mesh=mesh,
        in_specs=(image, image, label, label) + weights + (P(), P()),
        out_specs=(P(), image, image) + weights + (P(), P()),
        check_vma=False,
    )
```

```python
import functools

import jax
import jax.numpy as jnp
import numpy as np
from jax import lax
from jax.experimental import pallas as pl
from jax.experimental.pallas import tpu as pltpu
from jax.sharding import PartitionSpec as P

POSITIVES = 5
EPSILON = 1e-05
NORM_EPSILON = 1e-06
SOFTMAX_TEMP = 0.1
MASKED = -1e30
GUARD = 16
SLOT = 16
VMEM_LIMIT = 56 * 1024 * 1024
AXES = ("img", "blk")
F32 = jnp.float32
BF16 = jnp.bfloat16

NN = (((1,), (0,)), ((), ()))
NT = (((1,), (1,)), ((), ()))
TN = (((0,), (0,)), ((), ()))


def dot(left, right, dims=NN):
    return lax.dot_general(left, right, dims, preferred_element_type=F32)


def call(kernel, grid, inputs, outputs, scratch=(), us=6, after=()):
    return pl.pallas_call(
        skipping(kernel, len(inputs), len(after)),
        name=kernel.func.__name__,
        grid=grid,
        in_specs=[pl.BlockSpec(b, m) for _, b, m in inputs] + [IN_PLACE] * len(after),
        out_specs=[pl.BlockSpec(b, m) for _, _, b, m in outputs],
        out_shape=[jax.ShapeDtypeStruct(s, d) for s, d, _, _ in outputs],
        scratch_shapes=list(scratch),
        compiler_params=pltpu.CompilerParams(vmem_limit_bytes=VMEM_LIMIT),
        cost_estimate=cost(us),
    )(*[a for a, _, _ in inputs], *after)


def cost(us):
    return pl.CostEstimate(flops=0, bytes_accessed=int(us * 3.5e6), transcendentals=0)


IN_PLACE = pl.BlockSpec(memory_space=pl.ANY)
IN_SMEM = pl.BlockSpec(memory_space=pltpu.SMEM)


def skipping(kernel, used, unused):
    if not unused:
        return kernel
    return lambda *refs: kernel(*refs[:used], *refs[used + unused :])


def whole(a):
    return (a, a.shape, lambda *_: (0,) * a.ndim)


def cols(a, width):
    return (a, a.shape[:-1] + (width,), lambda i: (0,) * (a.ndim - 1) + (i,))


def rows(a, height):
    return (a, (height,) + a.shape[1:], lambda i: (i,) + (0,) * (a.ndim - 1))


def out_whole(shape, dtype):
    return (shape, dtype, shape, lambda *_: (0,) * len(shape))


def out_cols(shape, dtype, width):
    return (shape, dtype, shape[:-1] + (width,), lambda i: (0,) * (len(shape) - 1) + (i,))


def sigmoid(v):
    return 1.0 / (1.0 + jnp.exp(-v))


def spread(mask, width):
    return jnp.concatenate([mask] * (width // mask.shape[1]), 1)


def column_sum(v):
    return jnp.sum(v, 0, keepdims=True)


class Frames:
    def __init__(self, large, small):
        self.large, self.small = large.shape[0], small.shape[0]
        self.large_in, self.small_in = large.shape[1], small.shape[1]
        self.lo, self.so = self.large_in // 2, self.small_in // 2
        self.lp, self.sp = self.lo + 1, self.so + 1
        self.lrows, self.srows = self.large * self.lp**2, self.small * self.sp**2
        self.rows = self.lrows + self.srows
        self.valid = self.large * self.lo**2 + self.small * self.so**2
        self.views = self.large + self.small

    def mask(self):
        def grid(number, out):
            g = np.zeros((number, out + 1, out + 1), np.float32)
            g[:, :out, :out] = 1
            return g.reshape(-1)

        m = np.concatenate([grid(self.large, self.lo), grid(self.small, self.so)])
        return jnp.asarray(np.repeat(m[:, None], 128, 1))

    def cells(self):
        c = np.zeros((SLOT, 1), np.float32)
        c[: self.large] = 1.0 / self.lo**2
        c[self.large : self.views] = 1.0 / self.so**2
        return c

    def shifted(self, ref, row, col):
        a = GUARD + row * self.lp + col
        b = GUARD + self.lrows + row * self.sp + col
        return jnp.concatenate([ref[a : a + self.lrows, :], ref[b : b + self.srows, :]], 0)

    def per_view(self, v):
        w = v.shape[1]
        large = jnp.sum(v[: self.lrows].reshape(self.large, -1, w), 1)
        small = jnp.sum(v[self.lrows :].reshape(self.small, -1, w), 1)
        return large, small

    def to_rows(self, v):
        w = v.shape[1]
        large = jnp.broadcast_to(
            v[: self.large][:, None, :], (self.large, self.lp**2, w)
        ).reshape(self.lrows, w)
        small = jnp.broadcast_to(
            v[self.large : self.views][:, None, :], (self.small, self.sp**2, w)
        ).reshape(self.srows, w)
        return jnp.concatenate([large, small], 0)


class Norm:
    def __init__(self, stats, affine, count):
        self.center = stats[0:1, :]
        self.factor = lax.rsqrt(stats[1:2, :] / count + EPSILON)
        self.gain = affine[0:1, :]
        self.offset = affine[1:2, :]
        self.count = count

    def hat(self, v):
        return (v - self.center) * self.factor

    def scaled(self, hat):
        return hat * self.gain + self.offset

    def backward(self, d, hat, sums):
        return (self.gain * self.factor) * (
            d - sums[0:1, :] / self.count - hat * (sums[1:2, :] / self.count)
        )


def slope(v):
    s = sigmoid(v)
    return s * (1.0 + v * (1.0 - s))


def store_stats(ref, blocks, mask, count):
    center = sum(column_sum(b[...] * mask) for b in blocks) / count
    square = sum(column_sum(jnp.square((b[...] - center) * mask)) for b in blocks)
    ref[0:1, :] = center
    ref[1:2, :] = square


def lanes(width):
    return [slice(at, at + 128) for at in range(0, width, 128)]


def parity_pieces(f):
    for large, number, out, pitch, base in (
        (True, f.large, f.lo, f.lp, 0),
        (False, f.small, f.so, f.sp, f.lrows),
    ):
        for n in range(number):
            for i in range(out):
                for ph in range(2):
                    for pw in range(2):
                        at = (2 * ph + pw) * f.rows + base + n * pitch**2 + i * pitch
                        yield large, n, 2 * i + ph, pw, at, pitch


def split_kernel(f, large_ref, small_ref, out_ref, lt, st, acc):
    acc[...] = jnp.zeros_like(acc)
    for k, lane in enumerate(lanes(out_ref.shape[1])):
        for t, ref, side in ((lt, large_ref, f.large_in), (st, small_ref, f.small_in)):
            t[k] = jnp.zeros_like(t[k])
            t[k, :, :, 0:side, :] = ref[:, :, :, lane].astype(F32)
        for large, n, row, pw, at, pitch in parity_pieces(f):
            t = lt if large else st
            acc[at : at + pitch, lane] = t[k, n, row, pl.ds(pw, pitch, stride=2), :]
    out_ref[...] = acc[...].astype(BF16)


def parity_scratch(f, width):
    return [
        pltpu.VMEM((width // 128, f.large, f.large_in, 2 * f.lp, 128), F32),
        pltpu.VMEM((width // 128, f.small, f.small_in, 2 * f.sp, 128), F32),
        pltpu.VMEM((4 * f.rows, width), F32),
    ]


def split_cells(f, large, small, width=256, after=()):
    c = large.shape[3]
    return call(
        functools.partial(split_kernel, f),
        (c // width,),
        [cols(large, width), cols(small, width)],
        [out_cols((4 * f.rows, c), BF16, width)],
        parity_scratch(f, width),
        us=5,
        after=after,
    )[0]


def linear_kernel(f, count, x_ref, w_ref, mask_ref, out_ref, stats_ref):
    width = out_ref.shape[1]
    mask = spread(mask_ref[...], width)
    blocks = []
    for at in range(0, out_ref.shape[0], f.rows):
        block = out_ref.at[at : at + f.rows, :]
        block[...] = dot(x_ref[at : at + f.rows, :], w_ref[...])
        blocks.append(block)
    store_stats(stats_ref, blocks, mask, count)


def linear(f, x, w, mask, phases, width, after=()):
    n = w.shape[1]
    x_in = (x, (phases * f.rows, x.shape[1]), lambda i: (0, 0))
    return call(
        functools.partial(linear_kernel, f, phases * f.valid),
        (n // width,),
        [x_in, cols(w, width), whole(mask)],
        [out_cols((phases * f.rows, n), F32, width), out_cols((2, n), F32, width)],
        us=6,
        after=after,
    )


TAPS = [(p, q) for p in range(3) for q in range(3)]


def conv_kernel(
    f, stride, count, pre_ref, stats_ref, affine_ref, w_ref, mask_ref,
    patch_ref, out_ref, new_ref, act,
):
    width = pre_ref.shape[1]

    @pl.when(pl.program_id(0) == 0)
    def _():
        norm = Norm(stats_ref, affine_ref, count)
        mask = spread(mask_ref[...], width)
        for phase in range(act.shape[0]):
            act[phase, 0:GUARD, :] = jnp.zeros((GUARD, width), F32)
            act[phase, GUARD + f.rows :, :] = jnp.zeros((GUARD, width), F32)
            v = norm.scaled(norm.hat(pre_ref[phase * f.rows : (phase + 1) * f.rows, :]))
            act[phase, GUARD : GUARD + f.rows, :] = v * sigmoid(v) * mask
        for tap, (p, q) in enumerate(TAPS):
            if stride == 2:
                phase = 2 * (p != 1) + (q != 1)
                step = (-(p == 0), -(q == 0))
            else:
                phase, step = 0, (p - 1, q - 1)
            patch_ref[:, tap * width : (tap + 1) * width] = f.shifted(
                act.at[phase], *step
            ).astype(BF16)

    out_ref[...] = dot(patch_ref[...], w_ref[...])
    store_stats(new_ref, [out_ref], spread(mask_ref[...], out_ref.shape[1]), f.valid)


def conv(f, stride, count, pre, stats, affine, w, mask, tile=256, after=()):
    c, n = pre.shape[1], w.shape[1]
    phases = stride * stride
    return call(
        functools.partial(conv_kernel, f, stride, count),
        (n // tile,),
        [whole(pre), whole(stats), whole(affine), cols(w, tile), whole(mask)],
        [
            out_whole((f.rows, 9 * c), BF16),
            out_cols((f.rows, n), F32, tile),
            out_cols((2, n), F32, tile),
        ],
        [pltpu.VMEM((phases, f.rows + 2 * GUARD, c), F32)],
        us=8,
        after=after,
    )


def expand_kernel(f, count, pre_ref, stats_ref, affine_ref, w_ref, mask_ref, low_ref, out_ref, new_ref):
    @pl.when(pl.program_id(0) == 0)
    def _():
        norm = Norm(stats_ref, affine_ref, count)
        v = norm.scaled(norm.hat(pre_ref[...]))
        low_ref[...] = (v * sigmoid(v) * spread(mask_ref[...], v.shape[1])).astype(BF16)

    out_ref[...] = dot(low_ref[...], w_ref[...])
    store_stats(new_ref, [out_ref], spread(mask_ref[...], out_ref.shape[1]), f.valid)


def expand(f, count, pre, stats, affine, w, mask, tile=512, after=()):
    c, n = w.shape
    return call(
        functools.partial(expand_kernel, f, count),
        (n // tile,),
        [whole(pre), whole(stats), whole(affine), cols(w, tile), whole(mask)],
        [
            out_whole((f.rows, c), BF16),
            out_cols((f.rows, n), F32, tile),
            out_cols((2, n), F32, tile),
        ],
        us=5.3,
        after=after,
    )


def mix_kernel(
    f, count, exp_ref, skip_ref, stats_a, affine_a, stats_b, affine_b, w_ref, mask_ref,
    low_ref, pre_ref, out_ref, new_ref,
):
    step = pl.program_id(0)
    mask = spread(mask_ref[...], exp_ref.shape[1])
    first = Norm(stats_a, affine_a, count)
    second = Norm(stats_b, affine_b, count)
    v = first.scaled(first.hat(exp_ref[...])) + second.scaled(second.hat(skip_ref[...]))
    pre_ref[...] = v
    low = (v * sigmoid(v) * mask).astype(BF16)
    low_ref[...] = low
    part = dot(low, w_ref[...])

    @pl.when(step == 0)
    def _():
        out_ref[...] = part

    @pl.when(step > 0)
    def _():
        out_ref[...] += part

    @pl.when(step == pl.num_programs(0) - 1)
    def _():
        store_stats(new_ref, [out_ref], spread(mask_ref[...], out_ref.shape[1]), f.valid)


def mix(f, count, expanded, skipped, stats_a, affine_a, stats_b, affine_b, w, mask, tile=512, after=()):
    k, n = w.shape
    return call(
        functools.partial(mix_kernel, f, count),
        (k // tile,),
        [cols(a, tile) for a in (expanded, skipped, stats_a, affine_a, stats_b, affine_b)]
        + [rows(w, tile), whole(mask)],
        [
            out_cols((f.rows, k), BF16, tile),
            out_cols((f.rows, k), F32, tile),
            out_whole((f.rows, n), F32),
            out_whole((2, n), F32),
        ],
        us=8,
        after=after,
    )


def pool_kernel(
    f, count, wide_ref, pre_ref, stats_ref, affine_ref, mask_ref,
    pooled_ref, slope_ref, view_ref,
):
    mask = spread(mask_ref[...], wide_ref.shape[1])
    norm = Norm(stats_ref, affine_ref, count)
    hat = norm.hat(wide_ref[...])
    before = pre_ref[...]
    v = norm.scaled(hat) + before * sigmoid(before)
    s = sigmoid(v)
    d = s * (1.0 + v * (1.0 - s)) * mask
    slope_ref[...] = d

    def put(ref, at, pair, scale=(1.0, 1.0)):
        ref[at : at + f.large, :] = pair[0] * scale[0]
        ref[at + f.large : at + f.views, :] = pair[1] * scale[1]
        if f.views < SLOT:
            ref[at + f.views : at + SLOT, :] = jnp.zeros((SLOT - f.views, ref.shape[1]), F32)

    put(pooled_ref, 0, f.per_view(v * s * mask), (1.0 / f.lo**2, 1.0 / f.so**2))
    put(view_ref, 0, f.per_view(d))
    put(view_ref, SLOT, f.per_view(d * hat))


def pool(f, count, wide, pre, stats, affine, mask, tile=512, after=()):
    n = wide.shape[1]
    return call(
        functools.partial(pool_kernel, f, count),
        (n // tile,),
        [cols(a, tile) for a in (wide, pre, stats, affine)] + [whole(mask)],
        [
            out_cols((SLOT, n), F32, tile),
            out_cols((f.rows, n), F32, tile),
            out_cols((2 * SLOT, n), F32, tile),
        ],
        us=6.7,
        after=after,
    )


def head_kernel(
    f, devices, shard, place_ref, p_ref, digit_ref, h_ref, e_ref, affine_ref, view_ref, cells_ref,
    loss_ref, hidden_ref, embed_ref, gain_ref, back_ref, sums_ref,
    hat, low, emb, grad, own, factors, pooled_grad,
):
    step = pl.program_id(0)
    tiles = pl.num_programs(0) // 2
    v = p_ref.shape[0]
    tile = h_ref.shape[1]
    number = devices * f.views
    row_id = lax.broadcasted_iota(jnp.int32, (v, 128), 0)
    row_ok = (row_id % SLOT < f.views).astype(F32)
    mask = spread(row_ok, tile)
    gain, offset = affine_ref[0:1, :], affine_ref[1:2, :]

    @pl.when(step < tiles)
    def _():
        t = dot(p_ref[...], h_ref[...])
        center = column_sum(t * mask) / number
        t = (t - center) * mask
        factor = lax.rsqrt(column_sum(t * t) / number + EPSILON)
        t = t * factor
        hat[step] = t
        factors[step, 0:1, :] = factor
        t = t * gain + offset
        lowered = (t * sigmoid(t) * mask).astype(BF16)
        low[step] = lowered
        part = dot(lowered, e_ref[...])

        @pl.when(step == 0)
        def _():
            emb[...] = part

        @pl.when(step > 0)
        def _():
            emb[...] += part

    @pl.when(step == tiles - 1)
    def _():
        e = emb[...]
        inverse = lax.rsqrt(jnp.sum(e * e, 1, keepdims=True) + NORM_EPSILON)
        unit = e * inverse
        lowered = unit.astype(BF16)
        scores = dot(lowered, lowered, NT) / SOFTMAX_TEMP
        i = lax.broadcasted_iota(jnp.int32, (v, v), 0)
        j = lax.broadcasted_iota(jnp.int32, (v, v), 1)
        i_ok = i % SLOT < f.views
        j_ok = j % SLOT < f.views
        use = (i != j) & i_ok & j_ok
        digits = digit_ref[...].astype(F32)
        across = digits.T
        paired = use & (digits[:, 0:1] * 256.0 + digits[:, 1:2] == across[0:1, :] * 256.0 + across[1:2, :])
        weight = paired.astype(F32) / POSITIVES
        masked = jnp.where(use, scores, MASKED)

        def log_total(axis):
            top = jnp.max(masked, axis, keepdims=True)
            terms = jnp.where(use, jnp.exp(masked - top), 0.0)
            total = jnp.sum(terms, axis, keepdims=True)
            return top + jnp.log(jnp.where(total > 0.0, total, 1.0))

        by_row = log_total(1)
        by_col = log_total(0)
        positive = jnp.sum(jnp.where(paired, scores, 0.0), 1, keepdims=True)
        fine = lax.broadcasted_iota(jnp.int32, (v, 1), 0) % SLOT < f.views
        per_row = jnp.where(fine, by_row - positive / POSITIVES, 0.0)
        loss_ref[...] = jnp.broadcast_to(
            jnp.sum(per_row, 0, keepdims=True) / number, loss_ref.shape
        )

        def pair_grad(logs):
            chance = jnp.where(use, jnp.exp(masked - logs), 0.0)
            return ((chance - weight) / number).astype(BF16)

        unit_grad = (dot(pair_grad(by_row), lowered) + dot(pair_grad(by_col), lowered)) / SOFTMAX_TEMP
        along = jnp.sum(unit * unit_grad, 1, keepdims=True)
        g = inverse * (unit_grad - unit * along)
        grad[...] = jnp.where(fine, g, 0.0).astype(BF16)

    @pl.when(step >= tiles)
    def _():
        now = step - tiles
        t = hat[now]
        d = dot(grad[...], e_ref[...], NT) * slope(t * gain + offset)
        shift_grad = column_sum(d)
        gain_grad = column_sum(d * t)
        gain_ref[0:1, :] = gain_grad
        gain_ref[1:2, :] = shift_grad
        d = (factors[now, 0:1, :] * gain) * (d - shift_grad / number - t * (gain_grad / number))
        lowered = (d * mask).astype(BF16)
        own[...] = lowered
        mine = pl.multiple_of(place_ref[0] * shard, 128)
        hidden_ref[...] = dot(p_ref[:, pl.ds(mine, shard)], lowered, TN)
        here = pl.multiple_of(place_ref[2] * SLOT, SLOT)
        part = dot(own[pl.ds(here, SLOT), :], h_ref[...], NT)

        @pl.when(now == 0)
        def _():
            pooled_grad[...] = part

        @pl.when(now > 0)
        def _():
            pooled_grad[...] += part

    @pl.when(step == 2 * tiles - 1)
    def _():
        per = tile // shard if tile > shard else 1
        at = place_ref[0] // per
        inner = pl.multiple_of((place_ref[0] % per) * shard, 128)
        embed_ref[...] = dot(low[at, :, pl.ds(inner, shard)], grad[...], TN)
        b = pooled_grad[...] * cells_ref[...]
        back_ref[...] = b
        sums_ref[0:1, :] = column_sum(b * view_ref[0:SLOT, :])
        sums_ref[1:2, :] = column_sum(b * view_ref[SLOT:, :])


def head(f, devices, shard, place, pooled, weight, affine, view_sums, tile=512):
    v, c = pooled.shape[0], weight.shape[0]
    n, w = affine.shape[1], weight.shape[1] - affine.shape[1]
    tiles = n // tile
    cells = jnp.asarray(np.repeat(f.cells(), c, 1))
    late = lambda i: (0, jnp.maximum(i - tiles, 0))
    inputs = [
        (pooled, (v, c), lambda i: (0, 0)),
        (pooled, (v, 128), lambda i: (0, c // 128)),
        (weight, (c, tile), lambda i: (0, i % tiles)),
        (weight, (tile, w), lambda i: (i % tiles, n // w)),
        (affine, (2, tile), lambda i: (0, i % tiles)),
        whole(view_sums),
        whole(cells),
    ]
    outputs = [
        out_whole((8, 128), F32),
        ((shard, n), F32, (shard, tile), late),
        out_whole((shard, w), F32),
        ((2, n), F32, (2, tile), late),
        out_whole((SLOT, c), F32),
        out_whole((2, c), F32),
    ]
    return pl.pallas_call(
        functools.partial(head_kernel, f, devices, shard),
        name="head",
        grid=(2 * tiles,),
        in_specs=[pl.BlockSpec(memory_space=pltpu.SMEM)] + [pl.BlockSpec(b, m) for _, b, m in inputs],
        out_specs=[pl.BlockSpec(b, m) for _, _, b, m in outputs],
        out_shape=[jax.ShapeDtypeStruct(s, d) for s, d, _, _ in outputs],
        scratch_shapes=[
            pltpu.VMEM((tiles, v, tile), F32),
            pltpu.VMEM((tiles, v, tile), BF16),
            pltpu.VMEM((v, w), F32),
            pltpu.VMEM((v, w), BF16),
            pltpu.VMEM((v, tile), BF16),
            pltpu.VMEM((tiles, 8, tile), F32),
            pltpu.VMEM((SLOT, c), F32),
        ],
        compiler_params=pltpu.CompilerParams(vmem_limit_bytes=VMEM_LIMIT),
        cost_estimate=cost(22),
    )(place, *[a for a, _, _ in inputs])


def widen_back_kernel(
    f, count, wide_ref, slope_ref, back_ref, stats_ref, affine_ref, sums_ref, w_ref,
    turn_ref, turn_stats, turn_affine, mask_ref,
    low_ref, out_ref, new_ref,
):
    step = pl.program_id(0)
    norm = Norm(stats_ref, affine_ref, count)
    hat = norm.hat(wide_ref[...])
    d = f.to_rows(back_ref[...]) * slope_ref[...]
    low = (norm.backward(d, hat, sums_ref) * spread(mask_ref[...], hat.shape[1])).astype(BF16)
    low_ref[...] = low
    finish_back(step, dot(low, w_ref[...], NT), turn_ref, turn_stats, turn_affine, count, mask_ref, out_ref, new_ref)


def finish_back(step, part, pre_ref, stats, affine, count, mask_ref, out_ref, new_ref):
    @pl.when(step == 0)
    def _():
        out_ref[...] = part

    @pl.when(step > 0)
    def _():
        out_ref[...] += part

    @pl.when(step == pl.num_programs(0) - 1)
    def _():
        norm = Norm(stats, affine, count)
        hat = norm.hat(pre_ref[...])
        d = out_ref[...] * slope(norm.scaled(hat)) * spread(mask_ref[...], hat.shape[1])
        out_ref[...] = d
        new_ref[0:1, :] = column_sum(d)
        new_ref[1:2, :] = column_sum(d * hat)


def widen_back(f, count, wide, slopes, back, stats, affine, sums, w, turn, tstats, taffine, mask, tile=512, after=()):
    c, n = w.shape
    return call(
        functools.partial(widen_back_kernel, f, count),
        (n // tile,),
        [cols(a, tile) for a in (wide, slopes, back, stats, affine, sums, w)]
        + [whole(a) for a in (turn, tstats, taffine, mask)],
        [
            out_cols((f.rows, n), BF16, tile),
            out_whole((f.rows, c), F32),
            out_whole((2, c), F32),
        ],
        us=7.4,
        after=after,
    )


def conv_back_kernel(
    f, stride, count, in_count, d_ref, pre_ref, stats_ref, affine_ref, sums_ref, w_ref,
    in_ref, in_stats, in_affine, mask_ref,
    low_ref, out_ref, new_ref, act, moved,
):
    width = d_ref.shape[1]
    steps = [(a, b) for a in (0, 1) for b in (0, 1)] if stride == 2 else [(1 - p, 1 - q) for p, q in TAPS]

    @pl.when(pl.program_id(0) == 0)
    def _():
        norm = Norm(stats_ref, affine_ref, count)
        hat = norm.hat(pre_ref[...])
        low = (norm.backward(d_ref[...], hat, sums_ref) * spread(mask_ref[...], width)).astype(BF16)
        low_ref[...] = low
        act[0:GUARD, :] = jnp.zeros((GUARD, width), F32)
        act[GUARD + f.rows :, :] = jnp.zeros((GUARD, width), F32)
        act[GUARD : GUARD + f.rows, :] = low.astype(F32)
        for k, step in enumerate(steps):
            moved[k] = f.shifted(act, *step).astype(BF16)

    tile = out_ref.shape[1]
    mask = spread(mask_ref[...], tile)
    norm = Norm(in_stats, in_affine, in_count)
    total = jnp.zeros((1, tile), F32)
    total_hat = jnp.zeros((1, tile), F32)
    for phase in range(stride * stride):
        acc = None
        for tap, (p, q) in enumerate(TAPS):
            if stride == 2:
                if phase != 2 * (p != 1) + (q != 1):
                    continue
                step = (int(p == 0), int(q == 0))
            else:
                step = (1 - p, 1 - q)
            part = dot(moved[steps.index(step)], w_ref[tap], NT)
            acc = part if acc is None else acc + part
        at = phase * f.rows
        hat = norm.hat(in_ref[at : at + f.rows, :])
        d = acc * slope(norm.scaled(hat)) * mask
        out_ref[at : at + f.rows, :] = d
        total += column_sum(d)
        total_hat += column_sum(d * hat)
    new_ref[0:1, :] = total
    new_ref[1:2, :] = total_hat


def conv_back(f, stride, count, in_count, d, pre, stats, affine, sums, w, inside, istats, iaffine, mask, tile=256, after=()):
    n = d.shape[1]
    c = w.shape[1]
    phases = stride * stride
    return call(
        functools.partial(conv_back_kernel, f, stride, count, in_count),
        (c // tile,),
        [whole(a) for a in (d, pre, stats, affine, sums)]
        + [(w, (9, tile, n), lambda i: (0, i, 0))]
        + [cols(a, tile) for a in (inside, istats, iaffine)]
        + [whole(mask)],
        [
            out_whole((f.rows, n), BF16),
            out_cols((phases * f.rows, c), F32, tile),
            out_cols((2, c), F32, tile),
        ],
        [
            pltpu.VMEM((f.rows + 2 * GUARD, n), F32),
            pltpu.VMEM((4 if stride == 2 else 9, f.rows, n), BF16),
        ],
        us=7.2,
        after=after,
    )


def mix_back_kernel(
    f, count, d_ref, mix_ref, stats_ref, affine_ref, sums_ref, w_ref, back_ref, slope_ref,
    pre_ref, exp_ref, exp_stats, exp_affine, skip_ref, skip_stats, skip_affine, mask_ref,
    low_ref, out_ref, new_ref,
):
    @pl.when(pl.program_id(0) == 0)
    def _():
        norm = Norm(stats_ref, affine_ref, count)
        hat = norm.hat(mix_ref[...])
        d = norm.backward(d_ref[...], hat, sums_ref)
        low_ref[...] = (d * spread(mask_ref[...], hat.shape[1])).astype(BF16)

    g = f.to_rows(back_ref[...]) * slope_ref[...] + dot(low_ref[...], w_ref[...], NT)
    g = g * slope(pre_ref[...]) * spread(mask_ref[...], g.shape[1])
    out_ref[...] = g
    first = Norm(exp_stats, exp_affine, count)
    second = Norm(skip_stats, skip_affine, count)
    new_ref[0:1, :] = column_sum(g)
    new_ref[1:2, :] = column_sum(g * first.hat(exp_ref[...]))
    new_ref[2:3, :] = column_sum(g * second.hat(skip_ref[...]))


def mix_back(
    f, count, d, mixing, stats, affine, sums, w, back, slopes, pre,
    expanded, estats, eaffine, skipped, sstats, saffine, mask, tile=512, after=()):
    n, c = w.shape
    return call(
        functools.partial(mix_back_kernel, f, count),
        (n // tile,),
        [whole(a) for a in (d, mixing, stats, affine, sums)]
        + [rows(w, tile)]
        + [cols(a, tile) for a in (back, slopes, pre, expanded, estats, eaffine, skipped, sstats, saffine)]
        + [whole(mask)],
        [
            out_whole((f.rows, c), BF16),
            out_cols((f.rows, n), F32, tile),
            out_cols((3, n), F32, tile),
        ],
        us=9.8,
        after=after,
    )


def block_back_kernel(
    f, count, g_ref, exp_ref, exp_stats, exp_affine, skip_ref, skip_stats, skip_affine,
    sums_ref, w_ref, turn_ref, turn_stats, turn_affine, mask_ref,
    exp_low, skip_low, out_ref, new_ref,
):
    g = g_ref[...]
    mask = spread(mask_ref[...], g.shape[1])
    sums = sums_ref[...]
    first = Norm(exp_stats, exp_affine, count)
    low = (first.backward(g, first.hat(exp_ref[...]), sums[0:2]) * mask).astype(BF16)
    exp_low[...] = low
    second = Norm(skip_stats, skip_affine, count)
    other = jnp.concatenate([sums[0:1], sums[2:3]], 0)
    skip_low[...] = (second.backward(g, second.hat(skip_ref[...]), other) * mask).astype(BF16)
    finish_back(
        pl.program_id(0), dot(low, w_ref[...], NT), turn_ref, turn_stats, turn_affine,
        count, mask_ref, out_ref, new_ref,
    )


def block_back(
    f, count, g, expanded, estats, eaffine, skipped, sstats, saffine, sums, w,
    turned, tstats, taffine, mask, tile=512, after=()):
    c, n = w.shape
    return call(
        functools.partial(block_back_kernel, f, count),
        (n // tile,),
        [cols(a, tile) for a in (g, expanded, estats, eaffine, skipped, sstats, saffine, sums, w)]
        + [whole(a) for a in (turned, tstats, taffine, mask)],
        [
            out_cols((f.rows, n), BF16, tile),
            out_cols((f.rows, n), BF16, tile),
            out_whole((f.rows, c), F32),
            out_whole((2, c), F32),
        ],
        us=8.8,
        after=after,
    )


def input_back_kernel(
    f, count, d_ref, pre_ref, stats_ref, affine_ref, sums_ref, w_ref, sub_ref, mask_ref,
    low_ref, large_ref, small_ref, lt, st, acc,
):
    @pl.when(pl.program_id(0) == 0)
    def _():
        norm = Norm(stats_ref, affine_ref, count)
        mask = spread(mask_ref[...], d_ref.shape[1])
        for phase in range(4):
            at = phase * f.rows
            hat = norm.hat(pre_ref[at : at + f.rows, :])
            d = norm.backward(d_ref[at : at + f.rows, :], hat, sums_ref)
            low_ref[at : at + f.rows, :] = (d * mask).astype(BF16)

    for phase in range(4):
        at = phase * f.rows
        part = dot(low_ref[at : at + f.rows, :], w_ref[...], NT)
        if phase == 0:
            part = part + sub_ref[...]
        acc[at : at + f.rows, :] = part
    for k, lane in enumerate(lanes(acc.shape[1])):
        for large, n, row, pw, at, pitch in parity_pieces(f):
            t = lt if large else st
            t[k, n, row, pl.ds(pw, pitch, stride=2), :] = acc[at : at + pitch, lane]
        large_ref[:, :, :, lane] = lt[k, :, :, 0 : f.large_in, :].astype(BF16)
        small_ref[:, :, :, lane] = st[k, :, :, 0 : f.small_in, :].astype(BF16)


def input_back(f, count, d, pre, stats, affine, sums, w, sub, mask, tile=256, after=()):
    n, c = w.shape
    return call(
        functools.partial(input_back_kernel, f, count),
        (n // tile,),
        [whole(a) for a in (d, pre, stats, affine, sums)]
        + [rows(w, tile), cols(sub, tile), whole(mask)],
        [
            out_whole((4 * f.rows, c), BF16),
            out_cols((f.large, f.large_in, f.large_in, n), BF16, tile),
            out_cols((f.small, f.small_in, f.small_in, n), BF16, tile),
        ],
        parity_scratch(f, tile),
        us=8.4,
        after=after,
    )


def assemble_kernel(axis, rows, place_ref, own_ref, other_ref, out_ref, sems):
    copies = []
    for m in range(32):
        c, j, k = m & 1, (m >> 1) & 3, m >> 3
        src = (other_ref if c else own_ref).at[j, k]
        at = pl.ds(pl.multiple_of((place_ref[2] ^ m) * rows, 16), rows)
        dst = out_ref.at[at, :] if axis == 0 else out_ref.at[:, at, :]
        copies.append(pltpu.make_async_copy(src, dst, sems.at[m]))
    for copy in copies:
        copy.start()
    for copy in copies:
        copy.wait()


def assemble(place, own, other, after=()):
    block = own.shape[2:]
    axis = len(block) - 2
    shape = block[:axis] + (32 * block[axis],) + block[axis + 1 :]
    return pl.pallas_call(
        skipping(functools.partial(assemble_kernel, axis, block[axis]), 3, len(after)),
        name="assemble",
        in_specs=[IN_SMEM] + [IN_PLACE] * (2 + len(after)),
        out_specs=IN_PLACE,
        out_shape=jax.ShapeDtypeStruct(shape, own.dtype),
        scratch_shapes=[pltpu.SemaphoreType.DMA((32,))],
        compiler_params=pltpu.CompilerParams(vmem_limit_bytes=4 * 1024 * 1024),
        cost_estimate=cost(3.5),
    )(place, own, other, *after)


def join_kernel(at, half, split, folds, place_ref, own_ref, other_ref, out_ref, sems):
    copies = []
    pieces = split * folds
    rows = half // pieces
    for m in range(16 * pieces):
        piece, c, k = m % pieces, m // pieces % 2, m // (2 * pieces)
        src = (other_ref if c else own_ref).at[k]
        row = (2 * k + ((place_ref[1] % 2) ^ c)) * half + piece * rows
        there = pl.ds(pl.multiple_of(row, 16), rows)
        fold, part = piece // split, piece % split
        here = pl.ds(at + part * rows, rows)
        if folds > 1:
            width = out_ref.shape[-1]
            src, dst = src.at[here, pl.ds(fold * width, width)], out_ref.at[there, :]
        elif len(src.shape) == 2:
            src, dst = src.at[here, :], out_ref.at[there, :]
        else:
            src, dst = src.at[:, here, :], out_ref.at[:, there, :]
        copies.append(pltpu.make_async_copy(src, dst, sems.at[m]))
    for copy in copies:
        copy.start()
    for copy in copies:
        copy.wait()


def join_halves(place, own, other, at, half, folds):
    block = own.shape[1:]
    split = 1 if folds > 1 else 2
    shape = block[:-2] + (16 * half, block[-1] // folds)
    return pl.pallas_call(
        functools.partial(join_kernel, at, half, split, folds),
        name="join_halves",
        in_specs=[IN_SMEM, IN_PLACE, IN_PLACE],
        out_specs=IN_PLACE,
        out_shape=jax.ShapeDtypeStruct(shape, own.dtype),
        scratch_shapes=[pltpu.SemaphoreType.DMA((16 * split * folds,))],
        compiler_params=pltpu.CompilerParams(vmem_limit_bytes=4 * 1024 * 1024),
        cost_estimate=cost(4),
    )(place, own, other)


def half_kernel(place_ref, *refs):
    shards, out_ref = refs[:-1], refs[-1]
    base = 0
    for shard in shards:
        half = shard.shape[-2] // 2
        at = pl.multiple_of(place_ref[1] % 2 * half, 16)
        if len(shard.shape) == 3:
            out_ref[...] = shard[:, pl.ds(at, half), :]
            continue
        width = shard.shape[1]
        folds = out_ref.shape[1] // width
        rows = half // folds
        for fold in range(folds):
            value = shard[pl.ds(pl.multiple_of(at + fold * rows, 16), rows), :]
            out_ref[base : base + rows, fold * width : (fold + 1) * width] = value
        base += rows


def half_of(place, shards, after=()):
    shape = shards[0].shape
    if len(shape) == 2:
        width = max(s.shape[1] for s in shards)
        shape = (sum(s.size for s in shards) // (2 * width), width)
    else:
        shape = (shape[0], shape[1] // 2, shape[2])
    in_vmem = pl.BlockSpec(memory_space=pltpu.VMEM)
    return pl.pallas_call(
        skipping(half_kernel, 1 + len(shards), len(after)),
        name="half",
        in_specs=[IN_SMEM] + [in_vmem] * len(shards) + [IN_PLACE] * len(after),
        out_specs=in_vmem,
        out_shape=jax.ShapeDtypeStruct(shape, BF16),
        compiler_params=pltpu.CompilerParams(vmem_limit_bytes=VMEM_LIMIT),
        cost_estimate=cost(1.5),
    )(place, *shards, *after)


def cut_kernel(number, place_ref, *refs):
    ins, outs, sems = refs[:number], refs[number : 2 * number], refs[2 * number]
    copies = []
    for k in range(number):
        rows = outs[k].shape[-2]
        at = pl.ds(pl.multiple_of(place_ref[1] * rows, 16), rows)
        src = ins[k].at[at, :] if len(ins[k].shape) == 2 else ins[k].at[:, at, :]
        copies.append(pltpu.make_async_copy(src, outs[k], sems.at[k]))
    for copy in copies:
        copy.start()
    for copy in copies:
        copy.wait()


def cut(place, shards, after=()):
    shapes = [s.shape[:-2] + (s.shape[-2] // 4, s.shape[-1]) for s in shards]
    number = len(shards)
    return pl.pallas_call(
        skipping(functools.partial(cut_kernel, number), 1 + number, len(after)),
        name="cut",
        in_specs=[IN_SMEM] + [IN_PLACE] * (number + len(after)),
        out_specs=[IN_PLACE] * number,
        out_shape=[jax.ShapeDtypeStruct(s, BF16) for s in shapes],
        scratch_shapes=[pltpu.SemaphoreType.DMA((number,))],
        compiler_params=pltpu.CompilerParams(vmem_limit_bytes=4 * 1024 * 1024),
        cost_estimate=cost(0.7),
    )(place, *shards, *after)


def local_kernel(function, number, *refs):
    ins, outs = refs[:number], refs[number:]
    for out, value in zip(outs, function(*[r[...] for r in ins])):
        out[...] = value


def local(function, arrays, after=(), name="local", us=2):
    shapes = jax.eval_shape(function, *arrays)
    in_vmem = pl.BlockSpec(memory_space=pltpu.VMEM)
    kernel = functools.partial(local_kernel, function, len(arrays))
    return pl.pallas_call(
        skipping(kernel, len(arrays), len(after)),
        name=name,
        in_specs=[in_vmem] * len(arrays) + [IN_PLACE] * len(after),
        out_specs=[in_vmem] * len(shapes),
        out_shape=list(shapes),
        compiler_params=pltpu.CompilerParams(vmem_limit_bytes=VMEM_LIMIT),
        cost_estimate=cost(us),
    )(*arrays, *after)


def nothing(*refs):
    del refs


def pin(v, after):
    if not after:
        return v
    return pl.pallas_call(
        nothing,
        name="pin",
        in_specs=[IN_PLACE] * (1 + len(after)),
        out_specs=IN_PLACE,
        out_shape=jax.ShapeDtypeStruct(v.shape, v.dtype),
        input_output_aliases={0: 0},
        compiler_params=pltpu.CompilerParams(vmem_limit_bytes=4 * 1024 * 1024),
        cost_estimate=cost(0.5),
    )(v, *after)


def weight_kernel(by_tap, rows, parts, place_ref, left_ref, right_ref, keep_ref, send_ref, acc):
    acc[...] = dot(left_ref[...], right_ref[...], TN)
    for m in range(parts):
        if parts == 32:
            at, c, place = place_ref[2] ^ m, m & 1, ((m >> 1) & 3, m >> 3)
            place = place + (0,) if by_tap else place
        else:
            at, c, place = (m & ~1) + ((place_ref[1] % 2) ^ (m & 1)), m & 1, (m >> 1,)
        block = acc[pl.ds(pl.multiple_of(at * rows, 16), rows), :].astype(BF16)
        (send_ref if c else keep_ref)[place] = block


def weight_grad(place, left, right, taps=1, halves=False, tile=512):
    k, n = left.shape[1] // taps, right.shape[1]
    parts = 16 if halves else 32
    rows = k // parts
    if taps == 1:
        steps = n // tile
        left_in = (right.shape[0], k), lambda i: (0, 0)
        right_in = (right.shape[0], tile), lambda i: (0, i)
        shape, block = (4, 4, rows, n), (4, 4, rows, tile)
        out_map = lambda i: (0, 0, 0, i)
    else:
        steps, tile = taps, n
        left_in = (right.shape[0], k), lambda i: (0, i)
        right_in = right.shape, lambda i: (0, 0)
        shape, block = (4, 4, taps, rows, n), (4, 4, 1, rows, n)
        out_map = lambda i: (0, 0, i, 0, 0)
    if halves:
        shape, block = (8, steps * rows, tile), (8, rows, tile)
        out_map = lambda i: (0, i, 0)
    return pl.pallas_call(
        functools.partial(weight_kernel, taps > 1, rows, parts),
        name="weight_grad",
        grid=(steps,),
        in_specs=[IN_SMEM, pl.BlockSpec(*left_in), pl.BlockSpec(*right_in)],
        out_specs=[pl.BlockSpec(block, out_map)] * 2,
        out_shape=[jax.ShapeDtypeStruct(shape, BF16)] * 2,
        scratch_shapes=[pltpu.VMEM((k, tile), F32)],
        compiler_params=pltpu.CompilerParams(vmem_limit_bytes=VMEM_LIMIT),
        cost_estimate=cost(10 if taps > 1 else 5),
    )(place, left, right)


class Links:
    def __init__(self):
        self.img, self.blk = lax.axis_size("img"), lax.axis_size("blk")
        self.size = self.img * self.blk
        self.me = lax.axis_index("img") * self.blk + lax.axis_index("blk")
        low, high = self.blk.bit_length() - 1, self.img.bit_length() - 1
        self.low, self.high = low, high

    def swap(self, v, bits):
        return lax.ppermute(v, AXES, [(i, i ^ bits) for i in range(self.size)])

    def stages(self):
        found = []

        def cut(start, number):
            if number % 2 and number > 1:
                found.append([1 << start])
                start, number = start + 1, number - 1
            while number > 0:
                take = min(2, number)
                found.append([1 << (start + k) for k in range(take)])
                start, number = start + take, number - take

        cut(0, self.low)
        cut(self.low, self.high)
        return found

    def partners(self, v, stage):
        if len(stage) == 1:
            return [self.swap(v, stage[0])]
        a, b = stage
        return [self.swap(v, a), self.swap(v, b), self.swap(v, a | b)]

    def total(self, v):
        for stage in self.stages():
            got = self.partners(v, stage)
            if len(got) == 1:
                v = v + got[0]
            else:
                v = (v + got[0]) + (got[1] + got[2])
        return v

    def moments(self, v, count):
        for stage in self.stages():
            got = [v] + self.partners(v, stage)
            if len(got) == 2:
                a, b = got
                center = (a[0] + b[0]) * 0.5
                square = (a[1] + b[1]) + count * (
                    jnp.square(a[0] - center) + jnp.square(b[0] - center)
                )
            else:
                a, b, c, d = got
                center = ((a[0] + b[0]) + (c[0] + d[0])) * 0.25
                square = ((a[1] + b[1]) + (c[1] + d[1])) + count * (
                    (jnp.square(a[0] - center) + jnp.square(b[0] - center))
                    + (jnp.square(c[0] - center) + jnp.square(d[0] - center))
                )
            count = count * len(got)
            v = jnp.stack([center, square])
        return v

    def from_each(self, v, bits):
        return [v] + [self.swap(v, b) for b in bits]

    def across(self, own):
        return self.swap(own, 1)

    def joined(self, parts):
        a, b, c, d = parts
        core, y = self.me & 1, (self.me >> 1) & 1
        pick = lambda bit, p, q: (jnp.where(bit == 0, p, q), jnp.where(bit == 0, q, p))
        a, b = pick(core, a, b)
        c, d = pick(core, c, d)
        a, c = pick(y, a, c)
        b, d = pick(y, b, d)
        return jnp.concatenate([a, b, c, d], a.ndim - 2).astype(F32)

    def scatter_plain(self, left, right, taps=1):
        g = dot(left[: right.shape[0]], right, TN).astype(BF16)
        if taps > 1:
            g = g.reshape(taps, left.shape[1] // taps, -1)
        g = lax.psum_scatter(g, "img", scatter_dimension=int(taps > 1), tiled=True)
        return lax.psum(g, "blk").astype(F32)

    def gather(self, v):
        depth = 0
        for bit in reversed(range(self.low + self.high)):
            got = self.swap(v, 1 << bit)
            upper = (self.me >> bit) & 1
            v = jnp.stack(
                [jnp.where(upper == 0, v, got), jnp.where(upper == 0, got, v)], depth
            )
            depth += 1
        return v.reshape((self.size,) + v.shape[depth:])


class Weights:
    def __init__(self, links, place, staged, shards):
        self.links, self.place, self.staged, self.shards = links, place, staged, shards
        self.now, self.halves = {}, {}

    def cut(self, names, after=()):
        if self.staged:
            self.now.update(zip(names, cut(self.place, [self.shards[n] for n in names], after)))

    def along_z(self, name):
        if self.staged:
            self.now[name] = self.links.from_each(self.now[name], (8, 16, 24))

    def in_plane(self, name, after=()):
        if self.staged:
            (z,) = local(lambda *v: [jnp.stack(v)], self.now[name], after, "stack")
            self.now[name] = self.links.from_each(z, (2, 4, 6))

    def swap(self, name, after=()):
        if self.staged:
            (own,) = local(lambda *v: [jnp.stack(v)], self.now[name], after, "stack")
            self.now[name] = own, self.links.across(own)

    def fetch(self, *names, after=()):
        if not self.staged:
            return ()
        at, widest = 0, max(self.shards[n].shape[-1] for n in names)
        for n in names:
            half, folds = self.shards[n].shape[-2] // 2, widest // self.shards[n].shape[-1]
            self.halves[n] = names, at, half, folds
            at += half // folds
        own = half_of(self.place, [self.shards[n] for n in names], after)
        self.now[names] = lax.all_gather(own, "img")
        return (own,)

    def hand_on(self, *names, after=()):
        if self.staged:
            own = pin(self.now[names], after)
            self.now[names] = own, self.links.across(own)

    def get(self, name):
        if not self.staged:
            shard = self.shards[name]
            return lax.all_gather(shard, "img", axis=shard.ndim - 2, tiled=True)
        if name in self.halves:
            names, *where = self.halves[name]
            return join_halves(self.place, *self.now[names], *where)
        return assemble(self.place, *self.now[name])

    def state(self, *names):
        return tuple(jax.tree.leaves([self.now[n] for n in names])) if self.staged else ()


class Sums:
    def __init__(self, links, place, staged):
        self.links, self.place, self.staged = links, place, staged
        self.now = {}

    def start(self, name, left, right, taps=1, halves=False):
        if self.staged:
            self.now[name] = weight_grad(self.place, left, right, taps, halves)
        else:
            self.now[name] = self.links.scatter_plain(left, right, taps)

    def swap(self, name):
        if self.staged:
            keep, send = self.now[name]
            self.now[name] = keep, self.links.across(send)

    def in_plane(self, name, after=()):
        if self.staged:
            fold = lambda keep, got: [add2(keep[j], got[j]) for j in range(4)]
            part = local(fold, self.now[name], after, "fold")
            self.now[name] = [part[0]] + [self.links.swap(part[j], 2 * j) for j in (1, 2, 3)]

    def along_z(self, name, after=()):
        if self.staged:
            fold = lambda *got: [sum4([g[k] for g in got]) for k in range(4)]
            part = local(fold, self.now[name], after, "fold")
            self.now[name] = [part[0]] + [self.links.swap(part[k], 8 * k) for k in (1, 2, 3)]

    def join(self, name, after=()):
        if self.staged:
            (part,) = local(lambda *got: [sum4(got)], self.now[name], after, "fold")
            self.now[name] = self.links.from_each(part, (1, 2, 3))

    def scatter(self, *names, after=()):
        if self.staged:
            parts = [p for n in names for p in self.now[n]]
            join = lambda *v: [jnp.concatenate([add2(a, b) for a, b in zip(v[::2], v[1::2])], 1)]
            (part,) = local(join, parts, after, "fold", 4)
            self.now[names] = lax.psum_scatter(part, "img", scatter_dimension=0, tiled=False)

    def across_y(self, *names):
        if self.staged:
            own = self.now[names]
            (own,) = local(lambda a, b: [add2(a, b)], [own, self.links.swap(own, 2)], (), "fold")
            self.now[names] = own, self.links.across(own)

    def split(self, names, rows):
        if not self.staged:
            return [self.now[n] for n in names]
        own, other = self.now[names]
        core = self.links.me & 1
        both = jnp.where(core == 0, own, other), jnp.where(core == 0, other, own)
        found, at = [], 0
        for steps, half, by_tap in rows:
            pieces = [b[at : at + steps * half].reshape(steps, half, -1) for b in both]
            piece = jnp.concatenate(pieces, 1).astype(F32)
            if not by_tap:
                piece = jnp.concatenate([piece[k] for k in range(steps)], 1)
            found.append(piece)
            at += steps * half
        return found

    def state(self, *names):
        return tuple(jax.tree.leaves([self.now[n] for n in names])) if self.staged else ()

    def get(self, name):
        if not self.staged:
            return self.now[name]
        return self.links.joined(self.now[name])


def add2(a, b):
    return (a.astype(F32) + b.astype(F32)).astype(BF16)


def sum4(v):
    a, b, c, d = [x.astype(F32) for x in v]
    return ((a + b) + (c + d)).astype(BF16)


def head_plain(f, links, pooled, hidden, embed, affine, labels):
    number = links.size * f.views
    line = dot(pooled, hidden)
    center = lax.psum(jnp.sum(line, 0), AXES) / number
    line = line - center
    factor = lax.rsqrt(lax.psum(jnp.sum(line * line, 0), AXES) / number + EPSILON)
    hat = line * factor
    v = hat * affine[0] + affine[1]
    low = (v * sigmoid(v)).astype(BF16)
    e = dot(low, embed)
    inverse = lax.rsqrt(jnp.sum(e * e, 1, keepdims=True) + NORM_EPSILON)
    unit = e * inverse
    lowered = unit.astype(BF16)
    every = lax.all_gather(lowered, AXES, axis=0, tiled=True)
    every_label = lax.all_gather(labels, AXES, axis=0, tiled=True)
    scores = dot(lowered, every, NT) / SOFTMAX_TEMP
    anchor = links.me * f.views + jnp.arange(f.views, dtype=jnp.int32)
    itself = anchor[:, None] == jnp.arange(number, dtype=jnp.int32)[None, :]
    paired = (labels[:, None] == every_label[None, :]) & jnp.logical_not(itself)
    masked = jnp.where(itself, MASKED, scores)
    top = jnp.max(masked, 1)
    log_total = top + jnp.log(jnp.sum(jnp.where(itself, 0.0, jnp.exp(masked - top[:, None])), 1))
    positive = jnp.sum(jnp.where(paired, scores, 0.0), 1)
    loss = lax.psum(jnp.sum(log_total - positive / POSITIVES), AXES) / number
    every_log = lax.all_gather(log_total, AXES, axis=0, tiled=True)

    def pair_grad(logs):
        chance = jnp.where(itself, 0.0, jnp.exp(scores - logs))
        return ((chance - paired.astype(F32) / POSITIVES) / number).astype(BF16)

    unit_grad = (
        dot(pair_grad(log_total[:, None]), every) + dot(pair_grad(every_log[None, :]), every)
    ) / SOFTMAX_TEMP
    along = jnp.sum(unit * unit_grad, 1, keepdims=True)
    grad = (inverse * (unit_grad - unit * along)).astype(BF16)
    d = dot(grad, embed, NT) * slope(v)
    shift_grad = lax.psum(jnp.sum(d, 0), AXES)
    gain_grad = lax.psum(jnp.sum(d * hat, 0), AXES)
    back = (affine[0] * factor * (d - shift_grad / number - hat * (gain_grad / number))).astype(BF16)
    return loss, back, low, grad, gain_grad, shift_grad, dot(back, hidden, NT)


def per_device(
    x_large, x_small, large_image, small_image,
    first_reduce, first_spatial, first_expand, first_short,
    second_reduce, second_spatial, second_expand, head_hidden, head_embed,
    norm_gain, norm_shift,
):
    f = Frames(x_large, x_small)
    links = Links()
    mid, wide, proj = first_reduce.shape[1], first_short.shape[1], head_hidden.shape[1]
    widths = [mid, mid, wide, wide, mid, mid, wide, proj]
    starts = np.cumsum([0] + widths)
    both = jnp.stack([norm_gain, norm_shift])
    affine = [both[:, starts[k] : starts[k + 1]] for k in range(8)]
    mask = f.mask()

    place = jnp.stack([lax.axis_index("img"), lax.axis_index("blk"), links.me]).astype(jnp.int32)
    kernel_shape = (9,) + first_spatial.shape[2:]
    shards = {
        "reduce": first_reduce,
        "spatial": first_spatial.reshape(kernel_shape),
        "expand": first_expand,
        "short": first_short,
        "reduce2": second_reduce,
        "spatial2": second_spatial.reshape(kernel_shape),
        "expand2": second_expand,
        "head": jnp.concatenate([head_hidden, head_embed], 1),
    }
    staged = links.img == 8 and links.blk == 4
    staged = staged and all(w.shape[-2] % 64 == 0 for w in shards.values())
    weights = Weights(links, place, staged, shards)
    sums = Sums(links, place, staged)
    n_in, n_out = 4 * f.valid, f.valid
    all_in, all_out = n_in * links.size, n_out * links.size

    weights.cut(["reduce"])
    reduce_cut = weights.state("reduce")
    weights.along_z("reduce")
    weights.fetch("spatial")
    x = split_cells(f, x_large, x_small, after=reduce_cut)
    weights.in_plane("reduce", after=(x,))
    first = ("expand", "short", "reduce2", "expand2")
    first_half = weights.fetch(*first, after=(x,))
    weights.swap("reduce")
    w_reduce = weights.get("reduce")
    reduced, part0 = linear(f, x, w_reduce, mask, 4, 256, after=first_half)
    st0 = links.moments(part0, n_in)
    weights.hand_on("spatial", after=(st0,))
    spatial2_half = weights.fetch("spatial2", after=(st0,))
    w_spatial = weights.get("spatial")
    patch1, turned, part1 = conv(
        f, 2, all_in, reduced, st0, affine[0], w_spatial.reshape(9 * mid, mid), mask, after=spatial2_half
    )
    st1 = links.moments(part1, n_out)
    weights.hand_on(*first, after=(st1,))
    w_expand, w_short, w_reduce2, w_expand2 = [weights.get(n) for n in first]
    head_half = weights.fetch("head", after=(st1,))
    turned_low, expanded, part2 = expand(f, all_out, turned, st1, affine[1], w_expand, mask)
    skipped, part3 = linear(f, x, w_short, mask, 1, 512, after=(part2,) + head_half)
    joint = links.moments(jnp.concatenate([part2, part3], 1), n_out)
    st2, st3 = joint[:, :wide], joint[:, wide:]
    block_low, block_pre, mixing, part4 = mix(
        f, all_out, expanded, skipped, st2, affine[2], st3, affine[3], w_reduce2, mask
    )
    weights.hand_on("spatial2", after=(part4,))
    st4 = links.moments(part4, n_out)
    w_spatial2 = weights.get("spatial2")
    patch2, rotated, part5 = conv(
        f, 1, all_out, mixing, st4, affine[4], w_spatial2.reshape(9 * mid, mid), mask, after=(w_expand2,)
    )
    st5 = links.moments(part5, n_out)
    rotated_low, widened, part6 = expand(f, all_out, rotated, st5, affine[5], w_expand2, mask)
    st6 = links.moments(part6, n_out)
    weights.hand_on("head", after=(st6,))
    pooled, slopes, view_sums = pool(f, all_out, widened, block_pre, st6, affine[6], mask)
    pooled = pooled.astype(BF16)
    labels = jnp.concatenate([large_image, small_image], 0)
    w_head = weights.get("head")

    shard = head_hidden.shape[0]
    if staged:
        digits = jnp.concatenate([labels, jnp.full((SLOT - f.views,), -1, jnp.int32)])
        digits = jnp.stack([digits // 256, digits % 256], 1).astype(BF16)
        pooled = jnp.concatenate([pooled, jnp.pad(digits, ((0, 0), (0, 126)))], 1)
        every = jnp.stack(links.from_each(pooled, (8, 16, 24)))
        every = jnp.stack(links.from_each(every, (2, 4, 6)))
        every = assemble(place, every, links.across(every))
        loss, hidden_grad, embed_grad, gains7, back, sums6 = head(
            f, links.size, shard, place, every, w_head, affine[7], view_sums
        )
        loss = loss[0, 0]
        gain7, shift7 = gains7[0], gains7[1]
    else:
        pooled = pooled[: f.views]
        loss, hidden_back, head_low, embed_back, gain7, shift7, back = head_plain(
            f, links, pooled, w_head[:, :proj], w_head[:, proj:], affine[7], labels
        )
        back = jnp.pad(back, ((0, SLOT - f.views), (0, 0))) * f.cells()
        sums6 = jnp.stack([jnp.sum(back * view_sums[:SLOT], 0), jnp.sum(back * view_sums[SLOT:], 0)])
        hidden_grad = links.scatter_plain(pooled, hidden_back)
        embed_grad = links.scatter_plain(head_low, embed_back)
    sums6 = links.total(sums6)

    widened_back, d5, part5 = widen_back(
        f, all_out, widened, slopes, back, st6, affine[6], sums6, w_expand2, rotated, st5, affine[5], mask
    )
    sums.start("expand2", rotated_low, widened_back, halves=True)
    sums.swap("expand2")
    sums5 = links.total(part5)
    rotated_back, d4, part4 = conv_back(
        f, 1, all_out, all_out, d5, rotated, st5, affine[5], sums5, w_spatial2, mixing, st4, affine[4],
        mask, after=sums.state("expand2"),
    )
    sums.start("spatial2", patch2, rotated_back, 9, halves=True)
    sums.swap("spatial2")
    sums4 = links.total(part4)
    first = ("expand2", "spatial2")
    sums.scatter(*first, after=(sums4,))
    mixing_back, block_grad, part23 = mix_back(
        f, all_out, d4, mixing, st4, affine[4], sums4, w_reduce2, back, slopes, block_pre,
        expanded, st2, affine[2], skipped, st3, affine[3], mask, after=sums.state("spatial2"),
    )
    sums.start("reduce2", block_low, mixing_back, halves=True)
    sums.swap("reduce2")
    sums23 = links.total(part23)
    expanded_back, skipped_back, d1, part1 = block_back(
        f, all_out, block_grad, expanded, st2, affine[2], skipped, st3, affine[3], sums23, w_expand,
        turned, st1, affine[1], mask, after=sums.state("reduce2"),
    )
    sums.start("expand", turned_low, expanded_back, halves=True)
    sums.swap("expand")
    sums.start("short", x, skipped_back, halves=True)
    sums.swap("short")
    sub = dot(skipped_back, w_short, NT)
    sums1 = links.total(part1)
    second = ("reduce2", "expand", "short")
    sums.scatter(*second, after=(sums1,))
    turned_back, d0, part0 = conv_back(
        f, 2, all_out, all_in, d1, turned, st1, affine[1], sums1, w_spatial, reduced, st0, affine[0], mask,
        after=sums.state("expand", "short"),
    )
    sums.start("spatial", patch1, turned_back, 9)
    sums.swap("spatial")
    sums0 = links.total(pin(part0, sums.state(first)))
    sums.across_y(*first)
    sums.in_plane("spatial", after=(sums0,))
    reduced_back, grad_large, grad_small = input_back(
        f, all_in, d0, reduced, st0, affine[0], sums0, w_reduce, sub, mask, after=sums.state("spatial")[:1]
    )
    sums.start("reduce", x, reduced_back)
    sums.swap("reduce")
    sums.in_plane("reduce", after=sums.state("spatial"))
    sums.along_z("spatial")
    sums.along_z("reduce")
    sums.join("spatial")
    sums.join("reduce")
    sums.across_y(*second)
    eighth = lambda n: n // (2 * links.img)
    expand2_grad, spatial2_grad = sums.split(
        first, [(wide // 512, eighth(mid), False), (9, eighth(mid), True)]
    )
    reduce2_grad, expand_grad, short_grad = sums.split(
        second,
        [(1, eighth(wide), False), (wide // 512, eighth(mid), False), (wide // 512, eighth(2 * mid), False)],
    )
    spatial_grad, reduce_grad = sums.get("spatial"), sums.get("reduce")

    gain_grads = jnp.concatenate(
        [sums0[1], sums1[1], sums23[1], sums23[2], sums4[1], sums5[1], sums6[1], gain7]
    )
    shift_grads = jnp.concatenate(
        [sums0[0], sums1[0], sums23[0], sums23[0], sums4[0], sums5[0], sums6[0], shift7]
    )
    return (
        loss, grad_large, grad_small, reduce_grad, spatial_grad.reshape(first_spatial.shape), expand_grad, short_grad,
        reduce2_grad, spatial2_grad.reshape(first_spatial.shape), expand2_grad, hidden_grad, embed_grad, gain_grads, shift_grads,
    )


def solution(mesh):
    image = P(("img", "blk"), None, None, None)
    label = P(("img", "blk"))
    matrix = P("img", None)
    kernel = P(None, None, "img", None)
    weights = (matrix, kernel, matrix, matrix, matrix, kernel, matrix, matrix, matrix)
    return jax.shard_map(
        per_device,
        mesh=mesh,
        in_specs=(image, image, label, label) + weights + (P(), P()),
        out_specs=(P(), image, image) + weights + (P(), P()),
        check_vma=False,
    )
```

```python
import functools

import jax
import jax.numpy as jnp
import numpy as np
from jax import lax
from jax.experimental import pallas as pl
from jax.experimental.pallas import tpu as pltpu
from jax.sharding import PartitionSpec as P

POSITIVES = 5
EPSILON = 1e-05
NORM_EPSILON = 1e-06
SOFTMAX_TEMP = 0.1
MASKED = -1e30
GUARD = 16
SLOT = 16
VMEM_LIMIT = 56 * 1024 * 1024
AXES = ("img", "blk")
F32 = jnp.float32
BF16 = jnp.bfloat16

NN = (((1,), (0,)), ((), ()))
NT = (((1,), (1,)), ((), ()))
TN = (((0,), (0,)), ((), ()))


def dot(left, right, dims=NN):
    return lax.dot_general(left, right, dims, preferred_element_type=F32)


def call(kernel, grid, inputs, outputs, scratch=(), us=6, after=()):
    return pl.pallas_call(
        skipping(kernel, len(inputs), len(after)),
        name=kernel.func.__name__,
        grid=grid,
        in_specs=[pl.BlockSpec(b, m) for _, b, m in inputs] + [IN_PLACE] * len(after),
        out_specs=[pl.BlockSpec(b, m) for _, _, b, m in outputs],
        out_shape=[jax.ShapeDtypeStruct(s, d) for s, d, _, _ in outputs],
        scratch_shapes=list(scratch),
        compiler_params=pltpu.CompilerParams(vmem_limit_bytes=VMEM_LIMIT),
        cost_estimate=cost(us),
    )(*[a for a, _, _ in inputs], *after)


def cost(us):
    return pl.CostEstimate(flops=0, bytes_accessed=int(us * 3.5e6), transcendentals=0)


IN_PLACE = pl.BlockSpec(memory_space=pl.ANY)
IN_SMEM = pl.BlockSpec(memory_space=pltpu.SMEM)


def skipping(kernel, used, unused):
    if not unused:
        return kernel
    return lambda *refs: kernel(*refs[:used], *refs[used + unused :])


def whole(a):
    return (a, a.shape, lambda *_: (0,) * a.ndim)


def cols(a, width):
    return (a, a.shape[:-1] + (width,), lambda i: (0,) * (a.ndim - 1) + (i,))


def rows(a, height):
    return (a, (height,) + a.shape[1:], lambda i: (i,) + (0,) * (a.ndim - 1))


def out_whole(shape, dtype):
    return (shape, dtype, shape, lambda *_: (0,) * len(shape))


def out_cols(shape, dtype, width):
    return (shape, dtype, shape[:-1] + (width,), lambda i: (0,) * (len(shape) - 1) + (i,))


class Packed:
    PARTS = 32

    def __init__(self, buffer, base, rows, steps):
        self.buffer, self.base, self.rows, self.steps = buffer, base, rows, steps

    def column_tile(self):
        rows, first = self.rows, self.base // self.rows
        return self.buffer, (self.PARTS, rows, 512), lambda i: (0, first + i, 0)

    def row_tile(self):
        rows, first = self.rows, self.base // self.rows
        return self.buffer, (512 // rows, rows, 512), lambda i: (i, first, 0)

    def taps_by_column(self, tile):
        rows = self.rows * self.steps
        first = self.base // rows
        return self.buffer, (self.PARTS, rows, tile), lambda i: (0, first, i)

    def taps_by_row(self, tile):
        rows = self.rows * self.steps
        first = self.base // rows
        return self.buffer, (tile // self.rows, rows, 512), lambda i: (i, first, 0)


def flat(ref):
    return ref[...].reshape(-1, ref.shape[-1])


def tap_of(ref, tap):
    rows = ref.shape[1] // 9
    return ref[:, tap * rows : (tap + 1) * rows, :].reshape(-1, ref.shape[2])


def sigmoid(v):
    return 1.0 / (1.0 + jnp.exp(-v))


def spread(mask, width):
    return jnp.concatenate([mask] * (width // mask.shape[1]), 1)


def column_sum(v):
    return jnp.sum(v, 0, keepdims=True)


class Frames:
    def __init__(self, large, small):
        self.large, self.small = large.shape[0], small.shape[0]
        self.large_in, self.small_in = large.shape[1], small.shape[1]
        self.lo, self.so = self.large_in // 2, self.small_in // 2
        self.lp, self.sp = self.lo + 1, self.so + 1
        self.lrows, self.srows = self.large * self.lp**2, self.small * self.sp**2
        self.rows = self.lrows + self.srows
        self.valid = self.large * self.lo**2 + self.small * self.so**2
        self.views = self.large + self.small

    def mask(self):
        def grid(number, out):
            g = np.zeros((number, out + 1, out + 1), np.float32)
            g[:, :out, :out] = 1
            return g.reshape(-1)

        m = np.concatenate([grid(self.large, self.lo), grid(self.small, self.so)])
        return jnp.asarray(np.repeat(m[:, None], 128, 1))

    def cells(self):
        c = np.zeros((SLOT, 1), np.float32)
        c[: self.large] = 1.0 / self.lo**2
        c[self.large : self.views] = 1.0 / self.so**2
        return c

    def shifted(self, ref, row, col):
        a = GUARD + row * self.lp + col
        b = GUARD + self.lrows + row * self.sp + col
        return jnp.concatenate([ref[a : a + self.lrows, :], ref[b : b + self.srows, :]], 0)

    def per_view(self, v):
        w = v.shape[1]
        large = jnp.sum(v[: self.lrows].reshape(self.large, -1, w), 1)
        small = jnp.sum(v[self.lrows :].reshape(self.small, -1, w), 1)
        return large, small

    def to_rows(self, v):
        w = v.shape[1]
        large = jnp.broadcast_to(
            v[: self.large][:, None, :], (self.large, self.lp**2, w)
        ).reshape(self.lrows, w)
        small = jnp.broadcast_to(
            v[self.large : self.views][:, None, :], (self.small, self.sp**2, w)
        ).reshape(self.srows, w)
        return jnp.concatenate([large, small], 0)


class Norm:
    def __init__(self, stats, affine, count):
        self.center = stats[0:1, :]
        self.factor = lax.rsqrt(stats[1:2, :] / count + EPSILON)
        self.gain = affine[0:1, :]
        self.offset = affine[1:2, :]
        self.count = count

    def hat(self, v):
        return (v - self.center) * self.factor

    def scaled(self, hat):
        return hat * self.gain + self.offset

    def backward(self, d, hat, sums):
        return (self.gain * self.factor) * (
            d - sums[0:1, :] / self.count - hat * (sums[1:2, :] / self.count)
        )


def slope(v):
    s = sigmoid(v)
    return s * (1.0 + v * (1.0 - s))


def store_stats(ref, blocks, mask, count):
    center = sum(column_sum(b[...] * mask) for b in blocks) / count
    square = sum(column_sum(jnp.square((b[...] - center) * mask)) for b in blocks)
    ref[0:1, :] = center
    ref[1:2, :] = square


def lanes(width):
    return [slice(at, at + 128) for at in range(0, width, 128)]


def parity_pieces(f):
    for large, number, out, pitch, base in (
        (True, f.large, f.lo, f.lp, 0),
        (False, f.small, f.so, f.sp, f.lrows),
    ):
        for n in range(number):
            for i in range(out):
                for ph in range(2):
                    for pw in range(2):
                        at = (2 * ph + pw) * f.rows + base + n * pitch**2 + i * pitch
                        yield large, n, 2 * i + ph, pw, at, pitch


def split_kernel(f, large_ref, small_ref, out_ref, lt, st, acc):
    acc[...] = jnp.zeros_like(acc)
    for k, lane in enumerate(lanes(out_ref.shape[1])):
        for t, ref, side in ((lt, large_ref, f.large_in), (st, small_ref, f.small_in)):
            t[k] = jnp.zeros_like(t[k])
            t[k, :, :, 0:side, :] = ref[:, :, :, lane].astype(F32)
        for large, n, row, pw, at, pitch in parity_pieces(f):
            t = lt if large else st
            acc[at : at + pitch, lane] = t[k, n, row, pl.ds(pw, pitch, stride=2), :]
    out_ref[...] = acc[...].astype(BF16)


def parity_scratch(f, width):
    return [
        pltpu.VMEM((width // 128, f.large, f.large_in, 2 * f.lp, 128), F32),
        pltpu.VMEM((width // 128, f.small, f.small_in, 2 * f.sp, 128), F32),
        pltpu.VMEM((4 * f.rows, width), F32),
    ]


def split_cells(f, large, small, width=256, after=()):
    c = large.shape[3]
    return call(
        functools.partial(split_kernel, f),
        (c // width,),
        [cols(large, width), cols(small, width)],
        [out_cols((4 * f.rows, c), BF16, width)],
        parity_scratch(f, width),
        us=5,
        after=after,
    )[0]


def linear_kernel(f, count, x_ref, w_ref, mask_ref, out_ref, stats_ref):
    width = out_ref.shape[1]
    mask = spread(mask_ref[...], width)
    blocks = []
    for at in range(0, out_ref.shape[0], f.rows):
        block = out_ref.at[at : at + f.rows, :]
        block[...] = dot(x_ref[at : at + f.rows, :], flat(w_ref))
        blocks.append(block)
    store_stats(stats_ref, blocks, mask, count)


def linear(f, x, w_in, n, mask, phases, width, after=()):
    x_in = (x, (phases * f.rows, x.shape[1]), lambda i: (0, 0))
    return call(
        functools.partial(linear_kernel, f, phases * f.valid),
        (n // width,),
        [x_in, w_in, whole(mask)],
        [out_cols((phases * f.rows, n), F32, width), out_cols((2, n), F32, width)],
        us=6,
        after=after,
    )


TAPS = [(p, q) for p in range(3) for q in range(3)]


def conv_kernel(
    f, stride, count, pre_ref, stats_ref, affine_ref, w_ref, mask_ref,
    patch_ref, out_ref, new_ref, act,
):
    width = pre_ref.shape[1]

    @pl.when(pl.program_id(0) == 0)
    def _():
        norm = Norm(stats_ref, affine_ref, count)
        mask = spread(mask_ref[...], width)
        for phase in range(act.shape[0]):
            act[phase, 0:GUARD, :] = jnp.zeros((GUARD, width), F32)
            act[phase, GUARD + f.rows :, :] = jnp.zeros((GUARD, width), F32)
            v = norm.scaled(norm.hat(pre_ref[phase * f.rows : (phase + 1) * f.rows, :]))
            act[phase, GUARD : GUARD + f.rows, :] = v * sigmoid(v) * mask
        for tap, (p, q) in enumerate(TAPS):
            if stride == 2:
                phase = 2 * (p != 1) + (q != 1)
                step = (-(p == 0), -(q == 0))
            else:
                phase, step = 0, (p - 1, q - 1)
            patch_ref[:, tap * width : (tap + 1) * width] = f.shifted(
                act.at[phase], *step
            ).astype(BF16)

    total = None
    for tap in range(9):
        part = dot(patch_ref[:, tap * width : (tap + 1) * width], tap_of(w_ref, tap))
        total = part if total is None else total + part
    out_ref[...] = total
    store_stats(new_ref, [out_ref], spread(mask_ref[...], out_ref.shape[1]), f.valid)


def conv(f, stride, count, pre, stats, affine, w, mask, tile=256, after=()):
    c = n = pre.shape[1]
    phases = stride * stride
    return call(
        functools.partial(conv_kernel, f, stride, count),
        (n // tile,),
        [whole(pre), whole(stats), whole(affine), w.taps_by_column(tile), whole(mask)],
        [
            out_whole((f.rows, 9 * c), BF16),
            out_cols((f.rows, n), F32, tile),
            out_cols((2, n), F32, tile),
        ],
        [pltpu.VMEM((phases, f.rows + 2 * GUARD, c), F32)],
        us=8,
        after=after,
    )


def expand_kernel(f, count, pre_ref, stats_ref, affine_ref, w_ref, mask_ref, low_ref, out_ref, new_ref):
    @pl.when(pl.program_id(0) == 0)
    def _():
        norm = Norm(stats_ref, affine_ref, count)
        v = norm.scaled(norm.hat(pre_ref[...]))
        low_ref[...] = (v * sigmoid(v) * spread(mask_ref[...], v.shape[1])).astype(BF16)

    out_ref[...] = dot(low_ref[...], flat(w_ref))
    store_stats(new_ref, [out_ref], spread(mask_ref[...], out_ref.shape[1]), f.valid)


def expand(f, count, pre, stats, affine, w, mask, tile=512, after=()):
    c, n = pre.shape[1], w.steps * tile
    return call(
        functools.partial(expand_kernel, f, count),
        (n // tile,),
        [whole(pre), whole(stats), whole(affine), w.column_tile(), whole(mask)],
        [
            out_whole((f.rows, c), BF16),
            out_cols((f.rows, n), F32, tile),
            out_cols((2, n), F32, tile),
        ],
        us=5.3,
        after=after,
    )


def mix_kernel(
    f, count, exp_ref, skip_ref, stats_a, affine_a, stats_b, affine_b, w_ref, mask_ref,
    low_ref, pre_ref, out_ref, new_ref,
):
    step = pl.program_id(0)
    mask = spread(mask_ref[...], exp_ref.shape[1])
    first = Norm(stats_a, affine_a, count)
    second = Norm(stats_b, affine_b, count)
    v = first.scaled(first.hat(exp_ref[...])) + second.scaled(second.hat(skip_ref[...]))
    pre_ref[...] = v
    low = (v * sigmoid(v) * mask).astype(BF16)
    low_ref[...] = low
    part = dot(low, flat(w_ref))

    @pl.when(step == 0)
    def _():
        out_ref[...] = part

    @pl.when(step > 0)
    def _():
        out_ref[...] += part

    @pl.when(step == pl.num_programs(0) - 1)
    def _():
        store_stats(new_ref, [out_ref], spread(mask_ref[...], out_ref.shape[1]), f.valid)


def mix(f, count, expanded, skipped, stats_a, affine_a, stats_b, affine_b, w, mask, tile=512, after=()):
    k, n = expanded.shape[1], 512
    return call(
        functools.partial(mix_kernel, f, count),
        (k // tile,),
        [cols(a, tile) for a in (expanded, skipped, stats_a, affine_a, stats_b, affine_b)]
        + [w.row_tile(), whole(mask)],
        [
            out_cols((f.rows, k), BF16, tile),
            out_cols((f.rows, k), F32, tile),
            out_whole((f.rows, n), F32),
            out_whole((2, n), F32),
        ],
        us=8,
        after=after,
    )


def pool_kernel(
    f, count, wide_ref, pre_ref, stats_ref, affine_ref, mask_ref,
    pooled_ref, slope_ref, view_ref,
):
    mask = spread(mask_ref[...], wide_ref.shape[1])
    norm = Norm(stats_ref, affine_ref, count)
    hat = norm.hat(wide_ref[...])
    before = pre_ref[...]
    v = norm.scaled(hat) + before * sigmoid(before)
    s = sigmoid(v)
    d = s * (1.0 + v * (1.0 - s)) * mask
    slope_ref[...] = d

    def put(ref, at, pair, scale=(1.0, 1.0)):
        ref[at : at + f.large, :] = pair[0] * scale[0]
        ref[at + f.large : at + f.views, :] = pair[1] * scale[1]
        if f.views < SLOT:
            ref[at + f.views : at + SLOT, :] = jnp.zeros((SLOT - f.views, ref.shape[1]), F32)

    put(pooled_ref, 0, f.per_view(v * s * mask), (1.0 / f.lo**2, 1.0 / f.so**2))
    put(view_ref, 0, f.per_view(d))
    put(view_ref, SLOT, f.per_view(d * hat))


def pool(f, count, wide, pre, stats, affine, mask, tile=512, after=()):
    n = wide.shape[1]
    return call(
        functools.partial(pool_kernel, f, count),
        (n // tile,),
        [cols(a, tile) for a in (wide, pre, stats, affine)] + [whole(mask)],
        [
            out_cols((SLOT, n), F32, tile),
            out_cols((f.rows, n), F32, tile),
            out_cols((2 * SLOT, n), F32, tile),
        ],
        us=6.7,
        after=after,
    )


def head_kernel(
    f, devices, shard, place_ref, p_ref, digit_ref, h_ref, e_ref, affine_ref, view_ref, cells_ref,
    loss_ref, hidden_ref, embed_ref, gain_ref, back_ref, sums_ref,
    hat, low, emb, grad, own, factors, pooled_grad,
):
    step = pl.program_id(0)
    tiles = pl.num_programs(0) // 2
    v = p_ref.shape[0]
    tile = h_ref.shape[1]
    number = devices * f.views
    row_id = lax.broadcasted_iota(jnp.int32, (v, 128), 0)
    row_ok = (row_id % SLOT < f.views).astype(F32)
    mask = spread(row_ok, tile)
    gain, offset = affine_ref[0:1, :], affine_ref[1:2, :]

    @pl.when(step < tiles)
    def _():
        t = dot(p_ref[...], h_ref[...])
        center = column_sum(t * mask) / number
        t = (t - center) * mask
        factor = lax.rsqrt(column_sum(t * t) / number + EPSILON)
        t = t * factor
        hat[step] = t
        factors[step, 0:1, :] = factor
        t = t * gain + offset
        lowered = (t * sigmoid(t) * mask).astype(BF16)
        low[step] = lowered
        part = dot(lowered, e_ref[...])

        @pl.when(step == 0)
        def _():
            emb[...] = part

        @pl.when(step > 0)
        def _():
            emb[...] += part

    @pl.when(step == tiles - 1)
    def _():
        e = emb[...]
        inverse = lax.rsqrt(jnp.sum(e * e, 1, keepdims=True) + NORM_EPSILON)
        unit = e * inverse
        lowered = unit.astype(BF16)
        scores = dot(lowered, lowered, NT) / SOFTMAX_TEMP
        i = lax.broadcasted_iota(jnp.int32, (v, v), 0)
        j = lax.broadcasted_iota(jnp.int32, (v, v), 1)
        i_ok = i % SLOT < f.views
        j_ok = j % SLOT < f.views
        use = (i != j) & i_ok & j_ok
        digits = digit_ref[...].astype(F32)
        across = digits.T
        paired = use & (digits[:, 0:1] * 256.0 + digits[:, 1:2] == across[0:1, :] * 256.0 + across[1:2, :])
        weight = paired.astype(F32) / POSITIVES
        masked = jnp.where(use, scores, MASKED)

        def log_total(axis):
            top = jnp.max(masked, axis, keepdims=True)
            terms = jnp.where(use, jnp.exp(masked - top), 0.0)
            total = jnp.sum(terms, axis, keepdims=True)
            return top + jnp.log(jnp.where(total > 0.0, total, 1.0))

        by_row = log_total(1)
        by_col = log_total(0)
        positive = jnp.sum(jnp.where(paired, scores, 0.0), 1, keepdims=True)
        fine = lax.broadcasted_iota(jnp.int32, (v, 1), 0) % SLOT < f.views
        per_row = jnp.where(fine, by_row - positive / POSITIVES, 0.0)
        loss_ref[...] = jnp.broadcast_to(
            jnp.sum(per_row, 0, keepdims=True) / number, loss_ref.shape
        )

        def pair_grad(logs):
            chance = jnp.where(use, jnp.exp(masked - logs), 0.0)
            return ((chance - weight) / number).astype(BF16)

        unit_grad = (dot(pair_grad(by_row), lowered) + dot(pair_grad(by_col), lowered)) / SOFTMAX_TEMP
        along = jnp.sum(unit * unit_grad, 1, keepdims=True)
        g = inverse * (unit_grad - unit * along)
        grad[...] = jnp.where(fine, g, 0.0).astype(BF16)

    @pl.when(step >= tiles)
    def _():
        now = step - tiles
        t = hat[now]
        d = dot(grad[...], e_ref[...], NT) * slope(t * gain + offset)
        shift_grad = column_sum(d)
        gain_grad = column_sum(d * t)
        gain_ref[0:1, :] = gain_grad
        gain_ref[1:2, :] = shift_grad
        d = (factors[now, 0:1, :] * gain) * (d - shift_grad / number - t * (gain_grad / number))
        lowered = (d * mask).astype(BF16)
        own[...] = lowered
        mine = pl.multiple_of(place_ref[0] * shard, 128)
        hidden_ref[...] = dot(p_ref[:, pl.ds(mine, shard)], lowered, TN)
        here = pl.multiple_of(place_ref[2] * SLOT, SLOT)
        part = dot(own[pl.ds(here, SLOT), :], h_ref[...], NT)

        @pl.when(now == 0)
        def _():
            pooled_grad[...] = part

        @pl.when(now > 0)
        def _():
            pooled_grad[...] += part

    @pl.when(step == 2 * tiles - 1)
    def _():
        per = tile // shard if tile > shard else 1
        at = place_ref[0] // per
        inner = pl.multiple_of((place_ref[0] % per) * shard, 128)
        embed_ref[...] = dot(low[at, :, pl.ds(inner, shard)], grad[...], TN)
        b = pooled_grad[...] * cells_ref[...]
        back_ref[...] = b
        sums_ref[0:1, :] = column_sum(b * view_ref[0:SLOT, :])
        sums_ref[1:2, :] = column_sum(b * view_ref[SLOT:, :])


def head(f, devices, shard, place, pooled, weight, affine, view_sums, tile=512):
    v, c = pooled.shape[0], weight.shape[0]
    n, w = affine.shape[1], weight.shape[1] - affine.shape[1]
    tiles = n // tile
    cells = jnp.asarray(np.repeat(f.cells(), c, 1))
    late = lambda i: (0, jnp.maximum(i - tiles, 0))
    inputs = [
        (pooled, (v, c), lambda i: (0, 0)),
        (pooled, (v, 128), lambda i: (0, c // 128)),
        (weight, (c, tile), lambda i: (0, i % tiles)),
        (weight, (tile, w), lambda i: (i % tiles, n // w)),
        (affine, (2, tile), lambda i: (0, i % tiles)),
        whole(view_sums),
        whole(cells),
    ]
    outputs = [
        out_whole((8, 128), F32),
        ((shard, n), F32, (shard, tile), late),
        out_whole((shard, w), F32),
        ((2, n), F32, (2, tile), late),
        out_whole((SLOT, c), F32),
        out_whole((2, c), F32),
    ]
    return pl.pallas_call(
        functools.partial(head_kernel, f, devices, shard),
        name="head",
        grid=(2 * tiles,),
        in_specs=[pl.BlockSpec(memory_space=pltpu.SMEM)] + [pl.BlockSpec(b, m) for _, b, m in inputs],
        out_specs=[pl.BlockSpec(b, m) for _, _, b, m in outputs],
        out_shape=[jax.ShapeDtypeStruct(s, d) for s, d, _, _ in outputs],
        scratch_shapes=[
            pltpu.VMEM((tiles, v, tile), F32),
            pltpu.VMEM((tiles, v, tile), BF16),
            pltpu.VMEM((v, w), F32),
            pltpu.VMEM((v, w), BF16),
            pltpu.VMEM((v, tile), BF16),
            pltpu.VMEM((tiles, 8, tile), F32),
            pltpu.VMEM((SLOT, c), F32),
        ],
        compiler_params=pltpu.CompilerParams(vmem_limit_bytes=VMEM_LIMIT),
        cost_estimate=cost(22),
    )(place, *[a for a, _, _ in inputs])


def widen_back_kernel(
    f, count, wide_ref, slope_ref, back_ref, stats_ref, affine_ref, sums_ref, w_ref,
    turn_ref, turn_stats, turn_affine, mask_ref,
    low_ref, out_ref, new_ref,
):
    step = pl.program_id(0)
    norm = Norm(stats_ref, affine_ref, count)
    hat = norm.hat(wide_ref[...])
    d = f.to_rows(back_ref[...]) * slope_ref[...]
    low = (norm.backward(d, hat, sums_ref) * spread(mask_ref[...], hat.shape[1])).astype(BF16)
    low_ref[...] = low
    finish_back(step, dot(low, flat(w_ref), NT), turn_ref, turn_stats, turn_affine, count, mask_ref, out_ref, new_ref)


def finish_back(step, part, pre_ref, stats, affine, count, mask_ref, out_ref, new_ref):
    @pl.when(step == 0)
    def _():
        out_ref[...] = part

    @pl.when(step > 0)
    def _():
        out_ref[...] += part

    @pl.when(step == pl.num_programs(0) - 1)
    def _():
        norm = Norm(stats, affine, count)
        hat = norm.hat(pre_ref[...])
        d = out_ref[...] * slope(norm.scaled(hat)) * spread(mask_ref[...], hat.shape[1])
        out_ref[...] = d
        new_ref[0:1, :] = column_sum(d)
        new_ref[1:2, :] = column_sum(d * hat)


def widen_back(f, count, wide, slopes, back, stats, affine, sums, w, turn, tstats, taffine, mask, tile=512, after=()):
    c, n = turn.shape[1], w.steps * tile
    return call(
        functools.partial(widen_back_kernel, f, count),
        (n // tile,),
        [cols(a, tile) for a in (wide, slopes, back, stats, affine, sums)]
        + [w.column_tile()]
        + [whole(a) for a in (turn, tstats, taffine, mask)],
        [
            out_cols((f.rows, n), BF16, tile),
            out_whole((f.rows, c), F32),
            out_whole((2, c), F32),
        ],
        us=7.4,
        after=after,
    )


def conv_back_kernel(
    f, stride, count, in_count, d_ref, pre_ref, stats_ref, affine_ref, sums_ref, w_ref,
    in_ref, in_stats, in_affine, mask_ref,
    low_ref, out_ref, new_ref, act, moved,
):
    width = d_ref.shape[1]
    steps = [(a, b) for a in (0, 1) for b in (0, 1)] if stride == 2 else [(1 - p, 1 - q) for p, q in TAPS]

    @pl.when(pl.program_id(0) == 0)
    def _():
        norm = Norm(stats_ref, affine_ref, count)
        hat = norm.hat(pre_ref[...])
        low = (norm.backward(d_ref[...], hat, sums_ref) * spread(mask_ref[...], width)).astype(BF16)
        low_ref[...] = low
        act[0:GUARD, :] = jnp.zeros((GUARD, width), F32)
        act[GUARD + f.rows :, :] = jnp.zeros((GUARD, width), F32)
        act[GUARD : GUARD + f.rows, :] = low.astype(F32)
        for k, step in enumerate(steps):
            moved[k] = f.shifted(act, *step).astype(BF16)

    tile = out_ref.shape[1]
    mask = spread(mask_ref[...], tile)
    norm = Norm(in_stats, in_affine, in_count)
    total = jnp.zeros((1, tile), F32)
    total_hat = jnp.zeros((1, tile), F32)
    for phase in range(stride * stride):
        acc = None
        for tap, (p, q) in enumerate(TAPS):
            if stride == 2:
                if phase != 2 * (p != 1) + (q != 1):
                    continue
                step = (int(p == 0), int(q == 0))
            else:
                step = (1 - p, 1 - q)
            part = dot(moved[steps.index(step)], tap_of(w_ref, tap), NT)
            acc = part if acc is None else acc + part
        at = phase * f.rows
        hat = norm.hat(in_ref[at : at + f.rows, :])
        d = acc * slope(norm.scaled(hat)) * mask
        out_ref[at : at + f.rows, :] = d
        total += column_sum(d)
        total_hat += column_sum(d * hat)
    new_ref[0:1, :] = total
    new_ref[1:2, :] = total_hat


def conv_back(f, stride, count, in_count, d, pre, stats, affine, sums, w, inside, istats, iaffine, mask, tile=256, after=()):
    c = n = d.shape[1]
    phases = stride * stride
    return call(
        functools.partial(conv_back_kernel, f, stride, count, in_count),
        (c // tile,),
        [whole(a) for a in (d, pre, stats, affine, sums)]
        + [w.taps_by_row(tile)]
        + [cols(a, tile) for a in (inside, istats, iaffine)]
        + [whole(mask)],
        [
            out_whole((f.rows, n), BF16),
            out_cols((phases * f.rows, c), F32, tile),
            out_cols((2, c), F32, tile),
        ],
        [
            pltpu.VMEM((f.rows + 2 * GUARD, n), F32),
            pltpu.VMEM((4 if stride == 2 else 9, f.rows, n), BF16),
        ],
        us=7.2,
        after=after,
    )


def mix_back_kernel(
    f, count, d_ref, mix_ref, stats_ref, affine_ref, sums_ref, w_ref, back_ref, slope_ref,
    pre_ref, exp_ref, exp_stats, exp_affine, skip_ref, skip_stats, skip_affine, mask_ref,
    low_ref, out_ref, new_ref,
):
    @pl.when(pl.program_id(0) == 0)
    def _():
        norm = Norm(stats_ref, affine_ref, count)
        hat = norm.hat(mix_ref[...])
        d = norm.backward(d_ref[...], hat, sums_ref)
        low_ref[...] = (d * spread(mask_ref[...], hat.shape[1])).astype(BF16)

    g = f.to_rows(back_ref[...]) * slope_ref[...] + dot(low_ref[...], flat(w_ref), NT)
    g = g * slope(pre_ref[...]) * spread(mask_ref[...], g.shape[1])
    out_ref[...] = g
    first = Norm(exp_stats, exp_affine, count)
    second = Norm(skip_stats, skip_affine, count)
    new_ref[0:1, :] = column_sum(g)
    new_ref[1:2, :] = column_sum(g * first.hat(exp_ref[...]))
    new_ref[2:3, :] = column_sum(g * second.hat(skip_ref[...]))


def mix_back(
    f, count, d, mixing, stats, affine, sums, w, back, slopes, pre,
    expanded, estats, eaffine, skipped, sstats, saffine, mask, tile=512, after=()):
    n, c = expanded.shape[1], d.shape[1]
    return call(
        functools.partial(mix_back_kernel, f, count),
        (n // tile,),
        [whole(a) for a in (d, mixing, stats, affine, sums)]
        + [w.row_tile()]
        + [cols(a, tile) for a in (back, slopes, pre, expanded, estats, eaffine, skipped, sstats, saffine)]
        + [whole(mask)],
        [
            out_whole((f.rows, c), BF16),
            out_cols((f.rows, n), F32, tile),
            out_cols((3, n), F32, tile),
        ],
        us=9.8,
        after=after,
    )


def block_back_kernel(
    f, count, g_ref, exp_ref, exp_stats, exp_affine, skip_ref, skip_stats, skip_affine,
    sums_ref, w_ref, turn_ref, turn_stats, turn_affine, mask_ref,
    exp_low, skip_low, out_ref, new_ref,
):
    g = g_ref[...]
    mask = spread(mask_ref[...], g.shape[1])
    sums = sums_ref[...]
    first = Norm(exp_stats, exp_affine, count)
    low = (first.backward(g, first.hat(exp_ref[...]), sums[0:2]) * mask).astype(BF16)
    exp_low[...] = low
    second = Norm(skip_stats, skip_affine, count)
    other = jnp.concatenate([sums[0:1], sums[2:3]], 0)
    skip_low[...] = (second.backward(g, second.hat(skip_ref[...]), other) * mask).astype(BF16)
    finish_back(
        pl.program_id(0), dot(low, flat(w_ref), NT), turn_ref, turn_stats, turn_affine,
        count, mask_ref, out_ref, new_ref,
    )


def block_back(
    f, count, g, expanded, estats, eaffine, skipped, sstats, saffine, sums, w,
    turned, tstats, taffine, mask, tile=512, after=()):
    c, n = turned.shape[1], w.steps * tile
    return call(
        functools.partial(block_back_kernel, f, count),
        (n // tile,),
        [cols(a, tile) for a in (g, expanded, estats, eaffine, skipped, sstats, saffine, sums)]
        + [w.column_tile()]
        + [whole(a) for a in (turned, tstats, taffine, mask)],
        [
            out_cols((f.rows, n), BF16, tile),
            out_cols((f.rows, n), BF16, tile),
            out_whole((f.rows, c), F32),
            out_whole((2, c), F32),
        ],
        us=8.8,
        after=after,
    )


def sub_kernel(low_ref, w_ref, out_ref):
    part = dot(low_ref[...], flat(w_ref), NT)

    @pl.when(pl.program_id(0) == 0)
    def _():
        out_ref[...] = part

    @pl.when(pl.program_id(0) > 0)
    def _():
        out_ref[...] += part


def sub_back(low, w, c, tile=512, after=()):
    return call(
        functools.partial(sub_kernel),
        (w.steps,),
        [cols(low, tile), w.column_tile()],
        [out_whole((low.shape[0], c), F32)],
        us=0.1,
        after=after,
    )[0]


def input_low_kernel(f, count, d_ref, pre_ref, stats_ref, affine_ref, sums_ref, mask_ref, low_ref):
    norm = Norm(stats_ref, affine_ref, count)
    mask = spread(mask_ref[...], d_ref.shape[1])
    for phase in range(4):
        at = phase * f.rows
        hat = norm.hat(pre_ref[at : at + f.rows, :])
        d = norm.backward(d_ref[at : at + f.rows, :], hat, sums_ref)
        low_ref[at : at + f.rows, :] = (d * mask).astype(BF16)


def input_low(f, count, d, pre, stats, affine, sums, mask, tile=256, after=()):
    return call(
        functools.partial(input_low_kernel, f, count),
        (d.shape[1] // tile,),
        [cols(a, tile) for a in (d, pre, stats, affine, sums)] + [whole(mask)],
        [out_cols(d.shape, BF16, tile)],
        us=0.1,
        after=after,
    )[0]


def input_back_kernel(f, low_ref, w_ref, sub_ref, large_ref, small_ref, lt, st, acc):
    for phase in range(4):
        at = phase * f.rows
        part = dot(low_ref[at : at + f.rows, :], w_ref[...], NT)
        if phase == 0:
            part = part + sub_ref[...]
        acc[at : at + f.rows, :] = part
    for k, lane in enumerate(lanes(acc.shape[1])):
        for large, n, row, pw, at, pitch in parity_pieces(f):
            t = lt if large else st
            t[k, n, row, pl.ds(pw, pitch, stride=2), :] = acc[at : at + pitch, lane]
        large_ref[:, :, :, lane] = lt[k, :, :, 0 : f.large_in, :].astype(BF16)
        small_ref[:, :, :, lane] = st[k, :, :, 0 : f.small_in, :].astype(BF16)


def input_back(f, low, w, sub, tile=256, after=()):
    n, c = w.shape
    return call(
        functools.partial(input_back_kernel, f),
        (n // tile,),
        [whole(low), rows(w, tile), cols(sub, tile)],
        [
            out_cols((f.large, f.large_in, f.large_in, n), BF16, tile),
            out_cols((f.small, f.small_in, f.small_in, n), BF16, tile),
        ],
        parity_scratch(f, tile),
        us=0.1,
        after=after,
    )


def assemble_kernel(axis, rows, place_ref, own_ref, other_ref, out_ref, sems):
    copies = []
    for m in range(32):
        c, j, k = m & 1, (m >> 1) & 3, m >> 3
        src = (other_ref if c else own_ref).at[j, k]
        at = pl.ds(pl.multiple_of((place_ref[2] ^ m) * rows, 16), rows)
        dst = out_ref.at[at, :] if axis == 0 else out_ref.at[:, at, :]
        copies.append(pltpu.make_async_copy(src, dst, sems.at[m]))
    for copy in copies:
        copy.start()
    for copy in copies:
        copy.wait()


def assemble(place, own, other, after=()):
    block = own.shape[2:]
    axis = len(block) - 2
    shape = block[:axis] + (32 * block[axis],) + block[axis + 1 :]
    return pl.pallas_call(
        skipping(functools.partial(assemble_kernel, axis, block[axis]), 3, len(after)),
        name="assemble",
        in_specs=[IN_SMEM] + [IN_PLACE] * (2 + len(after)),
        out_specs=IN_PLACE,
        out_shape=jax.ShapeDtypeStruct(shape, own.dtype),
        scratch_shapes=[pltpu.SemaphoreType.DMA((32,))],
        compiler_params=pltpu.CompilerParams(vmem_limit_bytes=4 * 1024 * 1024),
        cost_estimate=cost(3.5),
    )(place, own, other, *after)


def pack_kernel(bases, place_ref, *refs):
    shards, out_ref = refs[:-1], refs[-1]
    out_ref[...] = jnp.zeros_like(out_ref)
    for base, shard in zip(bases, shards):
        rows = shard.shape[-2] // 4
        at = pl.ds(pl.multiple_of(place_ref[1] * rows, 16), rows)
        by_tap = len(shard.shape) == 3
        for k in range(shard.shape[0] if by_tap else shard.shape[1] // out_ref.shape[1]):
            width = out_ref.shape[1]
            value = shard[k, at, :] if by_tap else shard[at, k * width : (k + 1) * width]
            out_ref[base + k * rows : base + (k + 1) * rows, :] = value


def pack(place, shards, bases, shape, after=()):
    in_vmem = pl.BlockSpec(memory_space=pltpu.VMEM)
    return pl.pallas_call(
        skipping(functools.partial(pack_kernel, bases), 1 + len(shards), len(after)),
        name="pack",
        in_specs=[IN_SMEM] + [in_vmem] * len(shards) + [IN_PLACE] * len(after),
        out_specs=in_vmem,
        out_shape=jax.ShapeDtypeStruct(shape, BF16),
        compiler_params=pltpu.CompilerParams(vmem_limit_bytes=VMEM_LIMIT),
        cost_estimate=cost(2),
    )(place, *shards, *after)


def cut_kernel(number, place_ref, *refs):
    ins, outs, sems = refs[:number], refs[number : 2 * number], refs[2 * number]
    copies = []
    for k in range(number):
        rows = outs[k].shape[-2]
        at = pl.ds(pl.multiple_of(place_ref[1] * rows, 16), rows)
        src = ins[k].at[at, :] if len(ins[k].shape) == 2 else ins[k].at[:, at, :]
        copies.append(pltpu.make_async_copy(src, outs[k], sems.at[k]))
    for copy in copies:
        copy.start()
    for copy in copies:
        copy.wait()


def cut(place, shards, after=()):
    shapes = [s.shape[:-2] + (s.shape[-2] // 4, s.shape[-1]) for s in shards]
    number = len(shards)
    return pl.pallas_call(
        skipping(functools.partial(cut_kernel, number), 1 + number, len(after)),
        name="cut",
        in_specs=[IN_SMEM] + [IN_PLACE] * (number + len(after)),
        out_specs=[IN_PLACE] * number,
        out_shape=[jax.ShapeDtypeStruct(s, BF16) for s in shapes],
        scratch_shapes=[pltpu.SemaphoreType.DMA((number,))],
        compiler_params=pltpu.CompilerParams(vmem_limit_bytes=4 * 1024 * 1024),
        cost_estimate=cost(0.7),
    )(place, *shards, *after)


def unpack_kernel(kinds, place_ref, own_ref, other_ref, *outs):
    core = place_ref[1] % 2
    for ref, c in ((own_ref, core), (other_ref, 1 - core)):
        at = 0
        for (steps, rows, by_tap), out in zip(kinds, outs):
            there = pl.ds(pl.multiple_of(c * rows, 16), rows)
            for k in range(steps):
                value = ref[at : at + rows, :].astype(F32)
                if by_tap:
                    out[k, there, :] = value
                else:
                    out[there, k * 512 : (k + 1) * 512] = value
                at += rows


def unpack(place, own, other, kinds):
    in_vmem = pl.BlockSpec(memory_space=pltpu.VMEM)
    shapes = [(n, 2 * r, 512) if by_tap else (2 * r, n * 512) for n, r, by_tap in kinds]
    return pl.pallas_call(
        functools.partial(unpack_kernel, kinds),
        name="unpack",
        in_specs=[IN_SMEM, in_vmem, in_vmem],
        out_specs=[in_vmem] * len(kinds),
        out_shape=[jax.ShapeDtypeStruct(s, F32) for s in shapes],
        compiler_params=pltpu.CompilerParams(vmem_limit_bytes=VMEM_LIMIT),
        cost_estimate=cost(2),
    )(place, own, other)


def local_kernel(function, number, *refs):
    ins, outs = refs[:number], refs[number:]
    for out, value in zip(outs, function(*[r[...] for r in ins])):
        out[...] = value


def local(function, arrays, after=(), name="local", us=2):
    shapes = jax.eval_shape(function, *arrays)
    in_vmem = pl.BlockSpec(memory_space=pltpu.VMEM)
    kernel = functools.partial(local_kernel, function, len(arrays))
    return pl.pallas_call(
        skipping(kernel, len(arrays), len(after)),
        name=name,
        in_specs=[in_vmem] * len(arrays) + [IN_PLACE] * len(after),
        out_specs=[in_vmem] * len(shapes),
        out_shape=list(shapes),
        compiler_params=pltpu.CompilerParams(vmem_limit_bytes=VMEM_LIMIT),
        cost_estimate=cost(us),
    )(*arrays, *after)


def nothing(*refs):
    del refs


def pin(v, after):
    if not after:
        return v
    return pl.pallas_call(
        nothing,
        name="pin",
        in_specs=[IN_PLACE] * (1 + len(after)),
        out_specs=IN_PLACE,
        out_shape=jax.ShapeDtypeStruct(v.shape, v.dtype),
        input_output_aliases={0: 0},
        compiler_params=pltpu.CompilerParams(vmem_limit_bytes=4 * 1024 * 1024),
        cost_estimate=cost(0.5),
    )(v, *after)


def weight_kernel(by_tap, rows, halves, place_ref, left_ref, right_ref, keep_ref, send_ref, acc):
    acc[...] = dot(left_ref[...], right_ref[...], TN)
    for m in range(32):
        if halves:
            if m >= 16:
                break
            img, c = m >> 1, m & 1
            at, place = img * 2 + ((place_ref[1] % 2) ^ c), (img,)
        else:
            at, c, place = place_ref[2] ^ m, m & 1, ((m >> 1) & 3, m >> 3)
            place = place + (0,) if by_tap else place
        block = acc[pl.ds(pl.multiple_of(at * rows, 16), rows), :].astype(BF16)
        (send_ref if c else keep_ref)[place] = block


def weight_grad(place, left, right, taps=1, halves=False, us=None, tile=512):
    k, n = left.shape[1] // taps, right.shape[1]
    rows = k // (16 if halves else 32)
    if taps == 1:
        steps = n // tile
        left_in = (right.shape[0], k), lambda i: (0, 0)
        right_in = (right.shape[0], tile), lambda i: (0, i)
        shape, block = (4, 4, rows, n), (4, 4, rows, tile)
        out_map = lambda i: (0, 0, 0, i)
    else:
        steps, tile = taps, n
        left_in = (right.shape[0], k), lambda i: (0, i)
        right_in = right.shape, lambda i: (0, 0)
        shape, block = (4, 4, taps, rows, n), (4, 4, 1, rows, n)
        out_map = lambda i: (0, 0, i, 0, 0)
    if halves:
        shape, block = (8, steps * rows, tile), (8, rows, tile)
        out_map = lambda i: (0, i, 0)
    return pl.pallas_call(
        functools.partial(weight_kernel, taps > 1, rows, halves),
        name="weight_grad",
        grid=(steps,),
        in_specs=[IN_SMEM, pl.BlockSpec(*left_in), pl.BlockSpec(*right_in)],
        out_specs=[pl.BlockSpec(block, out_map)] * 2,
        out_shape=[jax.ShapeDtypeStruct(shape, BF16)] * 2,
        scratch_shapes=[pltpu.VMEM((k, tile), F32)],
        compiler_params=pltpu.CompilerParams(vmem_limit_bytes=VMEM_LIMIT),
        cost_estimate=cost(us or (10 if taps > 1 else 5)),
    )(place, left, right)


class Links:
    def __init__(self):
        self.img, self.blk = lax.axis_size("img"), lax.axis_size("blk")
        self.size = self.img * self.blk
        self.me = lax.axis_index("img") * self.blk + lax.axis_index("blk")
        low, high = self.blk.bit_length() - 1, self.img.bit_length() - 1
        self.low, self.high = low, high

    def swap(self, v, bits):
        return lax.ppermute(v, AXES, [(i, i ^ bits) for i in range(self.size)])

    def stages(self):
        found = []

        def cut(start, number):
            if number % 2 and number > 1:
                found.append([1 << start])
                start, number = start + 1, number - 1
            while number > 0:
                take = min(2, number)
                found.append([1 << (start + k) for k in range(take)])
                start, number = start + take, number - take

        cut(0, self.low)
        cut(self.low, self.high)
        return found

    def partners(self, v, stage):
        if len(stage) == 1:
            return [self.swap(v, stage[0])]
        a, b = stage
        return [self.swap(v, a), self.swap(v, b), self.swap(v, a | b)]

    def total(self, v):
        return self.end_total(self.begin_total(v))

    def begin_total(self, v):
        return self.add_stages(v, self.stages()[:1])

    def end_total(self, v):
        return self.add_stages(v, self.stages()[1:])

    def add_stages(self, v, stages):
        for stage in stages:
            got = self.partners(v, stage)
            if len(got) == 1:
                v = v + got[0]
            else:
                v = (v + got[0]) + (got[1] + got[2])
        return v

    def moments(self, v, count):
        for stage in self.stages():
            got = [v] + self.partners(v, stage)
            if len(got) == 2:
                a, b = got
                center = (a[0] + b[0]) * 0.5
                square = (a[1] + b[1]) + count * (
                    jnp.square(a[0] - center) + jnp.square(b[0] - center)
                )
            else:
                a, b, c, d = got
                center = ((a[0] + b[0]) + (c[0] + d[0])) * 0.25
                square = ((a[1] + b[1]) + (c[1] + d[1])) + count * (
                    (jnp.square(a[0] - center) + jnp.square(b[0] - center))
                    + (jnp.square(c[0] - center) + jnp.square(d[0] - center))
                )
            count = count * len(got)
            v = jnp.stack([center, square])
        return v

    def from_each(self, v, bits):
        return [v] + [self.swap(v, b) for b in bits]

    def across(self, own):
        return self.swap(own, 1)

    def joined(self, parts):
        a, b, c, d = parts
        core, y = self.me & 1, (self.me >> 1) & 1
        pick = lambda bit, p, q: (jnp.where(bit == 0, p, q), jnp.where(bit == 0, q, p))
        a, b = pick(core, a, b)
        c, d = pick(core, c, d)
        a, c = pick(y, a, c)
        b, d = pick(y, b, d)
        return jnp.concatenate([a, b, c, d], a.ndim - 2).astype(F32)

    def scatter_plain(self, left, right, taps=1):
        g = dot(left[: right.shape[0]], right, TN).astype(BF16)
        if taps > 1:
            g = g.reshape(taps, left.shape[1] // taps, -1)
        g = lax.psum_scatter(g, "img", scatter_dimension=int(taps > 1), tiled=True)
        return lax.psum(g, "blk").astype(F32)

    def gather(self, v):
        depth = 0
        for bit in reversed(range(self.low + self.high)):
            got = self.swap(v, 1 << bit)
            upper = (self.me >> bit) & 1
            v = jnp.stack(
                [jnp.where(upper == 0, v, got), jnp.where(upper == 0, got, v)], depth
            )
            depth += 1
        return v.reshape((self.size,) + v.shape[depth:])


class Weights:
    def __init__(self, links, place, staged, shards):
        self.links, self.place, self.staged, self.shards = links, place, staged, shards
        self.now = {}

    def whole(self, name):
        shard = self.shards[name]
        return lax.all_gather(shard, "img", axis=shard.ndim - 2, tiled=True)

    def first(self, name, during):
        if not self.staged:
            return self.whole(name), during(())
        (block,) = cut(self.place, [self.shards[name]])
        z = self.links.from_each(block, (8, 16, 24))
        x = during((block,))
        (z,) = local(lambda *v: [jnp.stack(v)], z, (x,), "stack")
        plane = self.links.from_each(z, (2, 4, 6))
        (own,) = local(lambda *v: [jnp.stack(v)], plane, (), "stack")
        return assemble(self.place, own, self.links.across(own)), x

    def fetch(self, bases, height, after=()):
        names = list(bases)
        if self.staged:
            shards = [self.shards[n] for n in names]
            own = pack(self.place, shards, list(bases.values()), (height, 512), after)
            buffer = lax.all_gather(own, AXES)
        else:
            own, at, blocks = None, 0, []
            for n in names:
                w = self.whole(n)
                if w.ndim == 2:
                    w = w.reshape(w.shape[0], -1, 512).transpose(1, 0, 2)
                w = w.reshape(w.shape[0], 32, -1, 512).transpose(1, 0, 2, 3).reshape(32, -1, 512)
                blocks += [jnp.zeros((32, bases[n] - at, 512), BF16), w]
                at = bases[n] + w.shape[1]
            blocks.append(jnp.zeros((32, height - at, 512), BF16))
            buffer = jnp.concatenate(blocks, 1)
        for n in names:
            shard = self.shards[n]
            rows = shard.shape[-2] * self.links.img // 32
            steps = shard.shape[0] if shard.ndim == 3 else shard.shape[1] // 512
            self.now[n] = Packed(buffer, bases[n], rows, steps)
        return () if own is None else (own,)

    def fetch_rows(self, name, after=()):
        if not self.staged:
            self.now[name] = self.whole(name)
            return ()
        (own,) = cut(self.place, [self.shards[name]], after)
        self.now[name] = lax.all_gather(own, AXES, axis=0, tiled=True)
        return (own,)


class Sums:
    def __init__(self, links, place, staged):
        self.links, self.place, self.staged = links, place, staged
        self.now = {}

    def start(self, name, left, right, taps=1, halves=False, us=None):
        if self.staged:
            self.now[name] = weight_grad(self.place, left, right, taps, halves, us)
        else:
            self.now[name] = self.links.scatter_plain(left, right, taps)

    def swap(self, name):
        if self.staged:
            keep, send = self.now[name]
            self.now[name] = keep, self.links.across(send)

    def in_plane(self, name, after=()):
        if self.staged:
            fold = lambda keep, got: [add2(keep[j], got[j]) for j in range(4)]
            part = local(fold, self.now[name], after, "fold")
            self.now[name] = [part[0]] + [self.links.swap(part[j], 2 * j) for j in (1, 2, 3)]

    def along_z(self, name, after=()):
        if self.staged:
            fold = lambda *got: [sum4([g[k] for g in got]) for k in range(4)]
            part = local(fold, self.now[name], after, "fold")
            self.now[name] = [part[0]] + [self.links.swap(part[k], 8 * k) for k in (1, 2, 3)]

    def join(self, name, after=()):
        if self.staged:
            (part,) = local(lambda *got: [sum4(got)], self.now[name], after, "fold")
            self.now[name] = self.links.from_each(part, (1, 2, 3))

    def scatter(self, *names, after=()):
        if self.staged:
            parts = [p for n in names for p in self.now[n]]
            join = lambda *v: [jnp.concatenate([add2(a, b) for a, b in zip(v[::2], v[1::2])], 1)]
            (part,) = local(join, parts, after, "fold", 4)
            self.now[names] = lax.psum_scatter(part, "img", scatter_dimension=0, tiled=False)
            return (part,)
        return ()

    def across_y(self, *names):
        if self.staged:
            own = self.now[names]
            self.now[names] = own, self.links.swap(own, 2)

    def across_cores(self, *names, after=()):
        if self.staged:
            (own,) = local(lambda a, b: [add2(a, b)], self.now[names], after, "fold")
            self.now[names] = own, self.links.across(own)

    def split(self, names, kinds):
        if not self.staged:
            return [self.now[n] for n in names]
        return unpack(self.place, *self.now[names], kinds)

    def state(self, *names):
        return tuple(jax.tree.leaves([self.now[n] for n in names])) if self.staged else ()

    def get(self, name):
        if not self.staged:
            return self.now[name]
        return self.links.joined(self.now[name])


def add2(a, b):
    return (a.astype(F32) + b.astype(F32)).astype(BF16)


def sum4(v):
    a, b, c, d = [x.astype(F32) for x in v]
    return ((a + b) + (c + d)).astype(BF16)


def head_plain(f, links, pooled, hidden, embed, affine, labels):
    number = links.size * f.views
    line = dot(pooled, hidden)
    center = lax.psum(jnp.sum(line, 0), AXES) / number
    line = line - center
    factor = lax.rsqrt(lax.psum(jnp.sum(line * line, 0), AXES) / number + EPSILON)
    hat = line * factor
    v = hat * affine[0] + affine[1]
    low = (v * sigmoid(v)).astype(BF16)
    e = dot(low, embed)
    inverse = lax.rsqrt(jnp.sum(e * e, 1, keepdims=True) + NORM_EPSILON)
    unit = e * inverse
    lowered = unit.astype(BF16)
    every = lax.all_gather(lowered, AXES, axis=0, tiled=True)
    every_label = lax.all_gather(labels, AXES, axis=0, tiled=True)
    scores = dot(lowered, every, NT) / SOFTMAX_TEMP
    anchor = links.me * f.views + jnp.arange(f.views, dtype=jnp.int32)
    itself = anchor[:, None] == jnp.arange(number, dtype=jnp.int32)[None, :]
    paired = (labels[:, None] == every_label[None, :]) & jnp.logical_not(itself)
    masked = jnp.where(itself, MASKED, scores)
    top = jnp.max(masked, 1)
    log_total = top + jnp.log(jnp.sum(jnp.where(itself, 0.0, jnp.exp(masked - top[:, None])), 1))
    positive = jnp.sum(jnp.where(paired, scores, 0.0), 1)
    loss = lax.psum(jnp.sum(log_total - positive / POSITIVES), AXES) / number
    every_log = lax.all_gather(log_total, AXES, axis=0, tiled=True)

    def pair_grad(logs):
        chance = jnp.where(itself, 0.0, jnp.exp(scores - logs))
        return ((chance - paired.astype(F32) / POSITIVES) / number).astype(BF16)

    unit_grad = (
        dot(pair_grad(log_total[:, None]), every) + dot(pair_grad(every_log[None, :]), every)
    ) / SOFTMAX_TEMP
    along = jnp.sum(unit * unit_grad, 1, keepdims=True)
    grad = (inverse * (unit_grad - unit * along)).astype(BF16)
    d = dot(grad, embed, NT) * slope(v)
    shift_grad = lax.psum(jnp.sum(d, 0), AXES)
    gain_grad = lax.psum(jnp.sum(d * hat, 0), AXES)
    back = (affine[0] * factor * (d - shift_grad / number - hat * (gain_grad / number))).astype(BF16)
    return loss, back, low, grad, gain_grad, shift_grad, dot(back, hidden, NT)


def per_device(
    x_large, x_small, large_image, small_image,
    first_reduce, first_spatial, first_expand, first_short,
    second_reduce, second_spatial, second_expand, head_hidden, head_embed,
    norm_gain, norm_shift,
):
    f = Frames(x_large, x_small)
    links = Links()
    mid, wide, proj = first_reduce.shape[1], first_short.shape[1], head_hidden.shape[1]
    widths = [mid, mid, wide, wide, mid, mid, wide, proj]
    starts = np.cumsum([0] + widths)
    both = jnp.stack([norm_gain, norm_shift])
    affine = [both[:, starts[k] : starts[k + 1]] for k in range(8)]
    mask = f.mask()

    place = jnp.stack([lax.axis_index("img"), lax.axis_index("blk"), links.me]).astype(jnp.int32)
    kernel_shape = (9,) + first_spatial.shape[2:]
    shards = {
        "reduce": first_reduce,
        "spatial": first_spatial.reshape(kernel_shape),
        "expand": first_expand,
        "short": first_short,
        "reduce2": second_reduce,
        "spatial2": second_spatial.reshape(kernel_shape),
        "expand2": second_expand,
        "head": jnp.concatenate([head_hidden, head_embed], 1),
    }
    staged = links.img == 8 and links.blk == 4
    staged = staged and all(w.shape[-2] % 64 == 0 for w in shards.values())
    weights = Weights(links, place, staged, shards)
    sums = Sums(links, place, staged)
    n_in, n_out = 4 * f.valid, f.valid
    all_in, all_out = n_in * links.size, n_out * links.size

    first = {"expand": 0, "reduce2": 64, "spatial": 144, "short": 288}
    second = {"spatial2": 0, "expand2": 144}
    weights.fetch(first, 416)
    w = weights.now
    w_reduce, x = weights.first(
        "reduce", lambda after: split_cells(f, x_large, x_small, after=after)
    )
    second_own = weights.fetch(second, 208, after=(x,))
    reduce_in = (w_reduce, (w_reduce.shape[0], 256), lambda i: (0, i))
    reduced, part0 = linear(f, x, reduce_in, mid, mask, 4, 256, after=second_own)
    st0 = links.moments(part0, n_in)
    head_own = weights.fetch_rows("head", after=(part0,))
    patch1, turned, part1 = conv(
        f, 2, all_in, reduced, st0, affine[0], w["spatial"], mask, after=head_own
    )
    st1 = links.moments(part1, n_out)
    turned_low, expanded, part2 = expand(f, all_out, turned, st1, affine[1], w["expand"], mask)
    skipped, part3 = linear(
        f, x, w["short"].column_tile(), wide, mask, 1, 512, after=(part2,)
    )
    joint = links.moments(jnp.concatenate([part2, part3], 1), n_out)
    st2, st3 = joint[:, :wide], joint[:, wide:]
    block_low, block_pre, mixing, part4 = mix(
        f, all_out, expanded, skipped, st2, affine[2], st3, affine[3], w["reduce2"], mask
    )
    st4 = links.moments(part4, n_out)
    patch2, rotated, part5 = conv(f, 1, all_out, mixing, st4, affine[4], w["spatial2"], mask)
    st5 = links.moments(part5, n_out)
    rotated_low, widened, part6 = expand(f, all_out, rotated, st5, affine[5], w["expand2"], mask)
    st6 = links.moments(part6, n_out)
    pooled, slopes, view_sums = pool(f, all_out, widened, block_pre, st6, affine[6], mask)
    pooled = pooled.astype(BF16)
    labels = jnp.concatenate([large_image, small_image], 0)
    w_head = w["head"]

    shard = head_hidden.shape[0]
    if staged:
        digits = jnp.concatenate([labels, jnp.full((SLOT - f.views,), -1, jnp.int32)])
        digits = jnp.stack([digits // 256, digits % 256], 1).astype(BF16)
        pooled = jnp.concatenate([pooled, jnp.pad(digits, ((0, 0), (0, 126)))], 1)
        every = jnp.stack(links.from_each(pooled, (8, 16, 24)))
        every = jnp.stack(links.from_each(every, (2, 4, 6)))
        every = assemble(place, every, links.across(every))
        loss, hidden_grad, embed_grad, gains7, back, sums6 = head(
            f, links.size, shard, place, every, w_head, affine[7], view_sums
        )
        loss = loss[0, 0]
        gain7, shift7 = gains7[0], gains7[1]
    else:
        pooled = pooled[: f.views]
        loss, hidden_back, head_low, embed_back, gain7, shift7, back = head_plain(
            f, links, pooled, w_head[:, :proj], w_head[:, proj:], affine[7], labels
        )
        back = jnp.pad(back, ((0, SLOT - f.views), (0, 0))) * f.cells()
        sums6 = jnp.stack([jnp.sum(back * view_sums[:SLOT], 0), jnp.sum(back * view_sums[SLOT:], 0)])
        hidden_grad = links.scatter_plain(pooled, hidden_back)
        embed_grad = links.scatter_plain(head_low, embed_back)
    sums6 = links.total(sums6)

    widened_back, d5, part5 = widen_back(
        f, all_out, widened, slopes, back, st6, affine[6], sums6, w["expand2"], rotated, st5, affine[5], mask
    )
    sums.start("expand2", rotated_low, widened_back, halves=True)
    started = sums.state("expand2")
    sums.swap("expand2")
    sums5 = links.total(part5)
    rotated_back, d4, part4 = conv_back(
        f, 1, all_out, all_out, d5, rotated, st5, affine[5], sums5, w["spatial2"], mixing, st4, affine[4],
        mask, after=started,
    )
    sums.start("spatial2", patch2, rotated_back, 9, halves=True)
    sums.swap("spatial2")
    sums4 = links.total(part4)
    first = ("expand2", "spatial2")
    first_own = sums.scatter(*first)
    mixing_back, block_grad, part23 = mix_back(
        f, all_out, d4, mixing, st4, affine[4], sums4, w["reduce2"], back, slopes, block_pre,
        expanded, st2, affine[2], skipped, st3, affine[3], mask, after=first_own,
    )
    sums.start("reduce2", block_low, mixing_back, halves=True)
    started = sums.state("reduce2")
    sums.swap("reduce2")
    sums23 = links.total(part23)
    expanded_back, skipped_back, d1, part1 = block_back(
        f, all_out, block_grad, expanded, st2, affine[2], skipped, st3, affine[3], sums23, w["expand"],
        turned, st1, affine[1], mask, after=started,
    )
    sums.start("expand", turned_low, expanded_back, halves=True)
    sums.swap("expand")
    sums.start("short", x, skipped_back, halves=True)
    sums.swap("short")
    sums1 = links.total(part1)
    second = ("reduce2", "expand", "short")
    second_own = sums.scatter(*second)
    turned_back, d0, part0 = conv_back(
        f, 2, all_out, all_in, d1, turned, st1, affine[1], sums1, w["spatial"], reduced, st0, affine[0], mask,
        after=second_own,
    )
    sums.start("spatial", patch1, turned_back, 9)
    sums.swap("spatial")
    sums0 = links.total(part0)
    sums.in_plane("spatial")
    reduced_back = input_low(
        f, all_in, d0, reduced, st0, affine[0], sums0, mask, after=sums.state("spatial")[:1]
    )
    sums.start("reduce", x, reduced_back, us=0.1)
    sums.swap("reduce")
    sub = sub_back(skipped_back, w["short"], x.shape[1], after=(reduced_back,))
    grad_large, grad_small = input_back(f, reduced_back, w_reduce, sub)
    sums.in_plane("reduce", after=sums.state("spatial") + (grad_small,))
    sums.along_z("spatial")
    sums.across_y(*first)
    sums.across_y(*second)
    sums.along_z("reduce")
    sums.across_cores(*first)
    sums.join("spatial", after=sums.state(first) + sums.state(second))
    sums.across_cores(*second)
    sums.join("reduce")
    part = lambda n: n // 16
    expand2_grad, spatial2_grad = sums.split(
        first, [(wide // 512, part(mid), False), (9, part(mid), True)]
    )
    reduce2_grad, expand_grad, short_grad = sums.split(
        second, [(1, part(wide), False), (wide // 512, part(mid), False), (wide // 512, part(2 * mid), False)]
    )
    reduce_grad, spatial_grad = sums.get("reduce"), sums.get("spatial")

    gain_grads = jnp.concatenate(
        [sums0[1], sums1[1], sums23[1], sums23[2], sums4[1], sums5[1], sums6[1], gain7]
    )
    shift_grads = jnp.concatenate(
        [sums0[0], sums1[0], sums23[0], sums23[0], sums4[0], sums5[0], sums6[0], shift7]
    )
    return (
        loss, grad_large, grad_small, reduce_grad, spatial_grad.reshape(first_spatial.shape), expand_grad, short_grad,
        reduce2_grad, spatial2_grad.reshape(first_spatial.shape), expand2_grad, hidden_grad, embed_grad, gain_grads, shift_grads,
    )


def solution(mesh):
    image = P(("img", "blk"), None, None, None)
    label = P(("img", "blk"))
    matrix = P("img", None)
    kernel = P(None, None, "img", None)
    weights = (matrix, kernel, matrix, matrix, matrix, kernel, matrix, matrix, matrix)
    return jax.shard_map(
        per_device,
        mesh=mesh,
        in_specs=(image, image, label, label) + weights + (P(), P()),
        out_specs=(P(), image, image) + weights + (P(), P()),
        check_vma=False,
    )
```

```python
import functools

import jax
import jax.numpy as jnp
import numpy as np
from jax import lax
from jax.experimental import pallas as pl
from jax.experimental.pallas import tpu as pltpu
from jax.sharding import PartitionSpec as P

POSITIVES = 5
EPSILON = 1e-05
NORM_EPSILON = 1e-06
SOFTMAX_TEMP = 0.1
MASKED = -1e30
GUARD = 16
SLOT = 16
VMEM_LIMIT = 56 * 1024 * 1024
AXES = ("img", "blk")
F32 = jnp.float32
BF16 = jnp.bfloat16

NN = (((1,), (0,)), ((), ()))
NT = (((1,), (1,)), ((), ()))
TN = (((0,), (0,)), ((), ()))


def dot(left, right, dims=NN):
    return lax.dot_general(left, right, dims, preferred_element_type=F32)


def call(kernel, grid, inputs, outputs, scratch=(), us=6, after=()):
    return pl.pallas_call(
        skipping(kernel, len(inputs), len(after)),
        name=kernel.func.__name__,
        grid=grid,
        in_specs=[pl.BlockSpec(b, m) for _, b, m in inputs] + [IN_PLACE] * len(after),
        out_specs=[pl.BlockSpec(b, m) for _, _, b, m in outputs],
        out_shape=[jax.ShapeDtypeStruct(s, d) for s, d, _, _ in outputs],
        scratch_shapes=list(scratch),
        compiler_params=pltpu.CompilerParams(vmem_limit_bytes=VMEM_LIMIT),
        cost_estimate=cost(us),
    )(*[a for a, _, _ in inputs], *after)


def cost(us):
    return pl.CostEstimate(flops=0, bytes_accessed=int(us * 3.5e6), transcendentals=0)


IN_PLACE = pl.BlockSpec(memory_space=pl.ANY)
IN_SMEM = pl.BlockSpec(memory_space=pltpu.SMEM)


def skipping(kernel, used, unused):
    if not unused:
        return kernel
    return lambda *refs: kernel(*refs[:used], *refs[used + unused :])


def whole(a):
    return (a, a.shape, lambda *_: (0,) * a.ndim)


def cols(a, width):
    return (a, a.shape[:-1] + (width,), lambda i: (0,) * (a.ndim - 1) + (i,))


def rows(a, height):
    return (a, (height,) + a.shape[1:], lambda i: (i,) + (0,) * (a.ndim - 1))


def out_whole(shape, dtype):
    return (shape, dtype, shape, lambda *_: (0,) * len(shape))


def out_cols(shape, dtype, width):
    return (shape, dtype, shape[:-1] + (width,), lambda i: (0,) * (len(shape) - 1) + (i,))


class Packed:
    PARTS = 32

    def __init__(self, buffer, base, rows, steps):
        self.buffer, self.base, self.rows, self.steps = buffer, base, rows, steps

    def column_tile(self):
        rows, first = self.rows, self.base // self.rows
        return self.buffer, (self.PARTS, rows, 512), lambda i: (0, first + i, 0)

    def row_tile(self):
        rows, first = self.rows, self.base // self.rows
        return self.buffer, (512 // rows, rows, 512), lambda i: (i, first, 0)

    def taps_by_column(self, tile):
        rows = self.rows * self.steps
        first = self.base // rows
        return self.buffer, (self.PARTS, rows, tile), lambda i: (0, first, i)

    def taps_by_row(self, tile):
        rows = self.rows * self.steps
        first = self.base // rows
        return self.buffer, (tile // self.rows, rows, 512), lambda i: (i, first, 0)


def flat(ref):
    return ref[...].reshape(-1, ref.shape[-1])


def tap_of(ref, tap):
    rows = ref.shape[1] // 9
    return ref[:, tap * rows : (tap + 1) * rows, :].reshape(-1, ref.shape[2])


def sigmoid(v):
    return 0.5 * jnp.tanh(0.5 * v) + 0.5


def spread(mask, width):
    return jnp.concatenate([mask] * (width // mask.shape[1]), 1)


def column_sum(v):
    return jnp.sum(v, 0, keepdims=True)


class Frames:
    def __init__(self, large, small):
        self.large, self.small = large.shape[0], small.shape[0]
        self.large_in, self.small_in = large.shape[1], small.shape[1]
        self.lo, self.so = self.large_in // 2, self.small_in // 2
        self.lp, self.sp = self.lo + 1, self.so + 1
        self.lrows, self.srows = self.large * self.lp**2, self.small * self.sp**2
        self.rows = self.lrows + self.srows
        self.valid = self.large * self.lo**2 + self.small * self.so**2
        self.views = self.large + self.small

    def mask(self):
        def grid(number, out):
            g = np.zeros((number, out + 1, out + 1), np.float32)
            g[:, :out, :out] = 1
            return g.reshape(-1)

        m = np.concatenate([grid(self.large, self.lo), grid(self.small, self.so)])
        return jnp.asarray(np.repeat(m[:, None], 128, 1))

    def cells(self):
        c = np.zeros((SLOT, 1), np.float32)
        c[: self.large] = 1.0 / self.lo**2
        c[self.large : self.views] = 1.0 / self.so**2
        return c

    def shifted(self, ref, row, col):
        a = GUARD + row * self.lp + col
        b = GUARD + self.lrows + row * self.sp + col
        return jnp.concatenate([ref[a : a + self.lrows, :], ref[b : b + self.srows, :]], 0)

    def per_view(self, v):
        w = v.shape[1]
        large = jnp.sum(v[: self.lrows].reshape(self.large, -1, w), 1)
        small = jnp.sum(v[self.lrows :].reshape(self.small, -1, w), 1)
        return large, small

    def to_rows(self, v):
        w = v.shape[1]
        large = jnp.broadcast_to(
            v[: self.large][:, None, :], (self.large, self.lp**2, w)
        ).reshape(self.lrows, w)
        small = jnp.broadcast_to(
            v[self.large : self.views][:, None, :], (self.small, self.sp**2, w)
        ).reshape(self.srows, w)
        return jnp.concatenate([large, small], 0)


class Norm:
    def __init__(self, stats, affine, count):
        self.center = stats[0:1, :]
        self.factor = lax.rsqrt(stats[1:2, :] / count + EPSILON)
        self.gain = affine[0:1, :]
        self.offset = affine[1:2, :]
        self.count = count

    def hat(self, v):
        return (v - self.center) * self.factor

    def scaled(self, hat):
        return hat * self.gain + self.offset

    def backward(self, d, hat, sums):
        return (self.gain * self.factor) * (
            d - sums[0:1, :] / self.count - hat * (sums[1:2, :] / self.count)
        )


def slope(v):
    s = sigmoid(v)
    return s * (1.0 + v * (1.0 - s))


def store_stats(ref, blocks, mask, count):
    center = sum(column_sum(b[...] * mask) for b in blocks) / count
    square = sum(column_sum(jnp.square((b[...] - center) * mask)) for b in blocks)
    ref[0:1, :] = center
    ref[1:2, :] = square


def lanes(width):
    return [slice(at, at + 128) for at in range(0, width, 128)]


def parity_pieces(f):
    for large, number, out, pitch, base in (
        (True, f.large, f.lo, f.lp, 0),
        (False, f.small, f.so, f.sp, f.lrows),
    ):
        for n in range(number):
            for i in range(out):
                for ph in range(2):
                    for pw in range(2):
                        at = (2 * ph + pw) * f.rows + base + n * pitch**2 + i * pitch
                        yield large, n, 2 * i + ph, pw, at, pitch


def split_kernel(f, large_ref, small_ref, out_ref, lt, st, acc):
    acc[...] = jnp.zeros_like(acc)
    for k, lane in enumerate(lanes(out_ref.shape[1])):
        for t, ref, side in ((lt, large_ref, f.large_in), (st, small_ref, f.small_in)):
            t[k] = jnp.zeros_like(t[k])
            t[k, :, :, 0:side, :] = ref[:, :, :, lane].astype(F32)
        for large, n, row, pw, at, pitch in parity_pieces(f):
            t = lt if large else st
            acc[at : at + pitch, lane] = t[k, n, row, pl.ds(pw, pitch, stride=2), :]
    out_ref[...] = acc[...].astype(BF16)


def parity_scratch(f, width):
    return [
        pltpu.VMEM((width // 128, f.large, f.large_in, 2 * f.lp, 128), F32),
        pltpu.VMEM((width // 128, f.small, f.small_in, 2 * f.sp, 128), F32),
        pltpu.VMEM((4 * f.rows, width), F32),
    ]


def split_cells(f, large, small, width=256, after=()):
    c = large.shape[3]
    return call(
        functools.partial(split_kernel, f),
        (c // width,),
        [cols(large, width), cols(small, width)],
        [out_cols((4 * f.rows, c), BF16, width)],
        parity_scratch(f, width),
        us=5,
        after=after,
    )[0]


def linear_kernel(f, count, x_ref, w_ref, mask_ref, out_ref, stats_ref):
    width = out_ref.shape[1]
    mask = spread(mask_ref[...], width)
    blocks = []
    for at in range(0, out_ref.shape[0], f.rows):
        block = out_ref.at[at : at + f.rows, :]
        block[...] = dot(x_ref[at : at + f.rows, :], flat(w_ref))
        blocks.append(block)
    store_stats(stats_ref, blocks, mask, count)


def linear(f, x, w_in, n, mask, phases, width, after=()):
    x_in = (x, (phases * f.rows, x.shape[1]), lambda i: (0, 0))
    return call(
        functools.partial(linear_kernel, f, phases * f.valid),
        (n // width,),
        [x_in, w_in, whole(mask)],
        [out_cols((phases * f.rows, n), F32, width), out_cols((2, n), F32, width)],
        us=6,
        after=after,
    )


TAPS = [(p, q) for p in range(3) for q in range(3)]


def conv_kernel(
    f, stride, count, pre_ref, stats_ref, affine_ref, w_ref, mask_ref,
    patch_ref, out_ref, new_ref, act,
):
    width = pre_ref.shape[1]

    @pl.when(pl.program_id(0) == 0)
    def _():
        norm = Norm(stats_ref, affine_ref, count)
        mask = spread(mask_ref[...], width)
        for phase in range(act.shape[0]):
            act[phase, 0:GUARD, :] = jnp.zeros((GUARD, width), F32)
            act[phase, GUARD + f.rows :, :] = jnp.zeros((GUARD, width), F32)
            v = norm.scaled(norm.hat(pre_ref[phase * f.rows : (phase + 1) * f.rows, :]))
            act[phase, GUARD : GUARD + f.rows, :] = v * sigmoid(v) * mask
        for tap, (p, q) in enumerate(TAPS):
            if stride == 2:
                phase = 2 * (p != 1) + (q != 1)
                step = (-(p == 0), -(q == 0))
            else:
                phase, step = 0, (p - 1, q - 1)
            patch_ref[:, tap * width : (tap + 1) * width] = f.shifted(
                act.at[phase], *step
            ).astype(BF16)

    total = None
    for tap in range(9):
        part = dot(patch_ref[:, tap * width : (tap + 1) * width], tap_of(w_ref, tap))
        total = part if total is None else total + part
    out_ref[...] = total
    store_stats(new_ref, [out_ref], spread(mask_ref[...], out_ref.shape[1]), f.valid)


def conv(f, stride, count, pre, stats, affine, w, mask, tile=256, after=()):
    c = n = pre.shape[1]
    phases = stride * stride
    return call(
        functools.partial(conv_kernel, f, stride, count),
        (n // tile,),
        [whole(pre), whole(stats), whole(affine), w.taps_by_column(tile), whole(mask)],
        [
            out_whole((f.rows, 9 * c), BF16),
            out_cols((f.rows, n), F32, tile),
            out_cols((2, n), F32, tile),
        ],
        [pltpu.VMEM((phases, f.rows + 2 * GUARD, c), F32)],
        us=8,
        after=after,
    )


def expand_kernel(f, count, pre_ref, stats_ref, affine_ref, w_ref, mask_ref, low_ref, out_ref, new_ref):
    @pl.when(pl.program_id(0) == 0)
    def _():
        norm = Norm(stats_ref, affine_ref, count)
        v = norm.scaled(norm.hat(pre_ref[...]))
        low_ref[...] = (v * sigmoid(v) * spread(mask_ref[...], v.shape[1])).astype(BF16)

    out_ref[...] = dot(low_ref[...], flat(w_ref))
    store_stats(new_ref, [out_ref], spread(mask_ref[...], out_ref.shape[1]), f.valid)


def expand(f, count, pre, stats, affine, w, mask, tile=512, after=()):
    c, n = pre.shape[1], w.steps * tile
    return call(
        functools.partial(expand_kernel, f, count),
        (n // tile,),
        [whole(pre), whole(stats), whole(affine), w.column_tile(), whole(mask)],
        [
            out_whole((f.rows, c), BF16),
            out_cols((f.rows, n), F32, tile),
            out_cols((2, n), F32, tile),
        ],
        us=5.3,
        after=after,
    )


def mix_kernel(
    f, count, exp_ref, skip_ref, stats_a, affine_a, stats_b, affine_b, w_ref, mask_ref,
    low_ref, pre_ref, out_ref, new_ref,
):
    step = pl.program_id(0)
    mask = spread(mask_ref[...], exp_ref.shape[1])
    first = Norm(stats_a, affine_a, count)
    second = Norm(stats_b, affine_b, count)
    v = first.scaled(first.hat(exp_ref[...])) + second.scaled(second.hat(skip_ref[...]))
    pre_ref[...] = v
    low = (v * sigmoid(v) * mask).astype(BF16)
    low_ref[...] = low
    part = dot(low, flat(w_ref))

    @pl.when(step == 0)
    def _():
        out_ref[...] = part

    @pl.when(step > 0)
    def _():
        out_ref[...] += part

    @pl.when(step == pl.num_programs(0) - 1)
    def _():
        store_stats(new_ref, [out_ref], spread(mask_ref[...], out_ref.shape[1]), f.valid)


def mix(f, count, expanded, skipped, stats_a, affine_a, stats_b, affine_b, w, mask, tile=512, after=()):
    k, n = expanded.shape[1], 512
    return call(
        functools.partial(mix_kernel, f, count),
        (k // tile,),
        [cols(a, tile) for a in (expanded, skipped, stats_a, affine_a, stats_b, affine_b)]
        + [w.row_tile(), whole(mask)],
        [
            out_cols((f.rows, k), BF16, tile),
            out_cols((f.rows, k), F32, tile),
            out_whole((f.rows, n), F32),
            out_whole((2, n), F32),
        ],
        us=8,
        after=after,
    )


def pool_kernel(
    f, count, wide_ref, pre_ref, stats_ref, affine_ref, mask_ref,
    pooled_ref, slope_ref, view_ref,
):
    mask = spread(mask_ref[...], wide_ref.shape[1])
    norm = Norm(stats_ref, affine_ref, count)
    hat = norm.hat(wide_ref[...])
    before = pre_ref[...]
    v = norm.scaled(hat) + before * sigmoid(before)
    s = sigmoid(v)
    d = s * (1.0 + v * (1.0 - s)) * mask
    slope_ref[...] = d

    def put(ref, at, pair, scale=(1.0, 1.0)):
        ref[at : at + f.large, :] = pair[0] * scale[0]
        ref[at + f.large : at + f.views, :] = pair[1] * scale[1]
        if f.views < SLOT:
            ref[at + f.views : at + SLOT, :] = jnp.zeros((SLOT - f.views, ref.shape[1]), F32)

    put(pooled_ref, 0, f.per_view(v * s * mask), (1.0 / f.lo**2, 1.0 / f.so**2))
    put(view_ref, 0, f.per_view(d))
    put(view_ref, SLOT, f.per_view(d * hat))


def pool(f, count, wide, pre, stats, affine, mask, tile=512, after=()):
    n = wide.shape[1]
    return call(
        functools.partial(pool_kernel, f, count),
        (n // tile,),
        [cols(a, tile) for a in (wide, pre, stats, affine)] + [whole(mask)],
        [
            out_cols((SLOT, n), F32, tile),
            out_cols((f.rows, n), F32, tile),
            out_cols((2 * SLOT, n), F32, tile),
        ],
        us=6.7,
        after=after,
    )


def head_kernel(
    f, devices, shard, place_ref, mine_ref, other_ref, h_ref, e_ref, affine_ref, view_ref, cells_ref,
    loss_ref, hidden_ref, embed_ref, gain_ref, back_ref, sums_ref,
    hat, low, emb, grad, own, factors, pooled_grad, rows_ref, sems,
):
    step = pl.program_id(0)
    tiles = pl.num_programs(0) // 2
    p_ref = rows_ref.at[:, 0 : view_ref.shape[1]]
    digit_ref = rows_ref.at[:, view_ref.shape[1] :]

    @pl.when(step == 0)
    def _():
        copies = []
        for m in range(32):
            c, j, k = m & 1, (m >> 1) & 3, m >> 3
            at = pl.ds(pl.multiple_of((place_ref[2] ^ m) * SLOT, SLOT), SLOT)
            src = (other_ref if c else mine_ref).at[j, k]
            copies.append(pltpu.make_async_copy(src, rows_ref.at[at, :], sems.at[m]))
        for copy in copies:
            copy.start()
        for copy in copies:
            copy.wait()

    v = rows_ref.shape[0]
    tile = h_ref.shape[1]
    number = devices * f.views
    row_id = lax.broadcasted_iota(jnp.int32, (v, 128), 0)
    row_ok = (row_id % SLOT < f.views).astype(F32)
    mask = spread(row_ok, tile)
    gain, offset = affine_ref[0:1, :], affine_ref[1:2, :]

    @pl.when(step < tiles)
    def _():
        t = dot(p_ref[...], h_ref[...])
        center = column_sum(t * mask) / number
        t = (t - center) * mask
        factor = lax.rsqrt(column_sum(t * t) / number + EPSILON)
        t = t * factor
        hat[step] = t
        factors[step, 0:1, :] = factor
        t = t * gain + offset
        lowered = (t * sigmoid(t) * mask).astype(BF16)
        low[step] = lowered
        part = dot(lowered, e_ref[...])

        @pl.when(step == 0)
        def _():
            emb[...] = part

        @pl.when(step > 0)
        def _():
            emb[...] += part

    @pl.when(step == tiles - 1)
    def _():
        e = emb[...]
        inverse = lax.rsqrt(jnp.sum(e * e, 1, keepdims=True) + NORM_EPSILON)
        unit = e * inverse
        lowered = unit.astype(BF16)
        scores = dot(lowered, lowered, NT) / SOFTMAX_TEMP
        i = lax.broadcasted_iota(jnp.int32, (v, v), 0)
        j = lax.broadcasted_iota(jnp.int32, (v, v), 1)
        i_ok = i % SLOT < f.views
        j_ok = j % SLOT < f.views
        use = (i != j) & i_ok & j_ok
        digits = digit_ref[...].astype(F32)
        across = digits.T
        paired = use & (digits[:, 0:1] * 256.0 + digits[:, 1:2] == across[0:1, :] * 256.0 + across[1:2, :])
        weight = paired.astype(F32) / POSITIVES
        masked = jnp.where(use, scores, MASKED)

        def log_total(axis):
            top = jnp.max(masked, axis, keepdims=True)
            terms = jnp.where(use, jnp.exp(masked - top), 0.0)
            total = jnp.sum(terms, axis, keepdims=True)
            return top + jnp.log(jnp.where(total > 0.0, total, 1.0))

        by_row = log_total(1)
        by_col = log_total(0)
        positive = jnp.sum(jnp.where(paired, scores, 0.0), 1, keepdims=True)
        fine = lax.broadcasted_iota(jnp.int32, (v, 1), 0) % SLOT < f.views
        per_row = jnp.where(fine, by_row - positive / POSITIVES, 0.0)
        loss_ref[...] = jnp.broadcast_to(
            jnp.sum(per_row, 0, keepdims=True) / number, loss_ref.shape
        )

        def pair_grad(logs):
            chance = jnp.where(use, jnp.exp(masked - logs), 0.0)
            return ((chance - weight) / number).astype(BF16)

        unit_grad = (dot(pair_grad(by_row), lowered) + dot(pair_grad(by_col), lowered)) / SOFTMAX_TEMP
        along = jnp.sum(unit * unit_grad, 1, keepdims=True)
        g = inverse * (unit_grad - unit * along)
        grad[...] = jnp.where(fine, g, 0.0).astype(BF16)

    @pl.when(step >= tiles)
    def _():
        now = step - tiles
        t = hat[now]
        d = dot(grad[...], e_ref[...], NT) * slope(t * gain + offset)
        shift_grad = column_sum(d)
        gain_grad = column_sum(d * t)
        gain_ref[0:1, :] = gain_grad
        gain_ref[1:2, :] = shift_grad
        d = (factors[now, 0:1, :] * gain) * (d - shift_grad / number - t * (gain_grad / number))
        lowered = (d * mask).astype(BF16)
        own[...] = lowered
        mine = pl.multiple_of(place_ref[0] * shard, 128)
        hidden_ref[...] = dot(p_ref[:, pl.ds(mine, shard)], lowered, TN)
        here = pl.multiple_of(place_ref[2] * SLOT, SLOT)
        part = dot(own[pl.ds(here, SLOT), :], h_ref[...], NT)

        @pl.when(now == 0)
        def _():
            pooled_grad[...] = part

        @pl.when(now > 0)
        def _():
            pooled_grad[...] += part

    @pl.when(step == 2 * tiles - 1)
    def _():
        per = tile // shard if tile > shard else 1
        at = place_ref[0] // per
        inner = pl.multiple_of((place_ref[0] % per) * shard, 128)
        embed_ref[...] = dot(low[at, :, pl.ds(inner, shard)], grad[...], TN)
        b = pooled_grad[...] * cells_ref[...]
        back_ref[...] = b
        sums_ref[0:1, :] = column_sum(b * view_ref[0:SLOT, :])
        sums_ref[1:2, :] = column_sum(b * view_ref[SLOT:, :])


def head(f, devices, shard, place, pooled, weight, affine, view_sums, tile=512):
    v, c = devices * SLOT, weight.shape[0]
    n, w = affine.shape[1], weight.shape[1] - affine.shape[1]
    tiles = n // tile
    cells = jnp.asarray(np.repeat(f.cells(), c, 1))
    late = lambda i: (0, jnp.maximum(i - tiles, 0))
    inputs = [
        (weight, (c, tile), lambda i: (0, i % tiles)),
        (weight, (tile, w), lambda i: (i % tiles, n // w)),
        (affine, (2, tile), lambda i: (0, i % tiles)),
        whole(view_sums),
        whole(cells),
    ]
    outputs = [
        out_whole((8, 128), F32),
        ((shard, n), F32, (shard, tile), late),
        out_whole((shard, w), F32),
        ((2, n), F32, (2, tile), late),
        out_whole((SLOT, c), F32),
        out_whole((2, c), F32),
    ]
    return pl.pallas_call(
        functools.partial(head_kernel, f, devices, shard),
        name="head",
        grid=(2 * tiles,),
        in_specs=[IN_SMEM, IN_PLACE, IN_PLACE] + [pl.BlockSpec(b, m) for _, b, m in inputs],
        out_specs=[pl.BlockSpec(b, m) for _, _, b, m in outputs],
        out_shape=[jax.ShapeDtypeStruct(s, d) for s, d, _, _ in outputs],
        scratch_shapes=[
            pltpu.VMEM((tiles, v, tile), F32),
            pltpu.VMEM((tiles, v, tile), BF16),
            pltpu.VMEM((v, w), F32),
            pltpu.VMEM((v, w), BF16),
            pltpu.VMEM((v, tile), BF16),
            pltpu.VMEM((tiles, 8, tile), F32),
            pltpu.VMEM((SLOT, c), F32),
            pltpu.VMEM((v, pooled[0].shape[-1]), BF16),
            pltpu.SemaphoreType.DMA((32,)),
        ],
        compiler_params=pltpu.CompilerParams(vmem_limit_bytes=VMEM_LIMIT),
        cost_estimate=cost(22),
    )(place, *pooled, *[a for a, _, _ in inputs])


def widen_back_kernel(
    f, count, wide_ref, slope_ref, back_ref, stats_ref, affine_ref, sums_ref, w_ref,
    turn_ref, turn_stats, turn_affine, mask_ref,
    low_ref, out_ref, new_ref,
):
    step = pl.program_id(0)
    norm = Norm(stats_ref, affine_ref, count)
    hat = norm.hat(wide_ref[...])
    d = f.to_rows(back_ref[...]) * slope_ref[...]
    low = (norm.backward(d, hat, sums_ref) * spread(mask_ref[...], hat.shape[1])).astype(BF16)
    low_ref[...] = low
    finish_back(step, dot(low, flat(w_ref), NT), turn_ref, turn_stats, turn_affine, count, mask_ref, out_ref, new_ref)


def finish_back(step, part, pre_ref, stats, affine, count, mask_ref, out_ref, new_ref):
    @pl.when(step == 0)
    def _():
        out_ref[...] = part

    @pl.when(step > 0)
    def _():
        out_ref[...] += part

    @pl.when(step == pl.num_programs(0) - 1)
    def _():
        norm = Norm(stats, affine, count)
        hat = norm.hat(pre_ref[...])
        d = out_ref[...] * slope(norm.scaled(hat)) * spread(mask_ref[...], hat.shape[1])
        out_ref[...] = d
        new_ref[0:1, :] = column_sum(d)
        new_ref[1:2, :] = column_sum(d * hat)


def widen_back(f, count, wide, slopes, back, stats, affine, sums, w, turn, tstats, taffine, mask, tile=512, after=()):
    c, n = turn.shape[1], w.steps * tile
    return call(
        functools.partial(widen_back_kernel, f, count),
        (n // tile,),
        [cols(a, tile) for a in (wide, slopes, back, stats, affine, sums)]
        + [w.column_tile()]
        + [whole(a) for a in (turn, tstats, taffine, mask)],
        [
            out_cols((f.rows, n), BF16, tile),
            out_whole((f.rows, c), F32),
            out_whole((2, c), F32),
        ],
        us=7.4,
        after=after,
    )


def conv_back_kernel(
    f, stride, count, in_count, d_ref, pre_ref, stats_ref, affine_ref, sums_ref, w_ref,
    in_ref, in_stats, in_affine, mask_ref,
    low_ref, out_ref, new_ref, act, moved,
):
    width = d_ref.shape[1]
    steps = [(a, b) for a in (0, 1) for b in (0, 1)] if stride == 2 else [(1 - p, 1 - q) for p, q in TAPS]

    @pl.when(pl.program_id(0) == 0)
    def _():
        norm = Norm(stats_ref, affine_ref, count)
        hat = norm.hat(pre_ref[...])
        low = (norm.backward(d_ref[...], hat, sums_ref) * spread(mask_ref[...], width)).astype(BF16)
        low_ref[...] = low
        act[0:GUARD, :] = jnp.zeros((GUARD, width), F32)
        act[GUARD + f.rows :, :] = jnp.zeros((GUARD, width), F32)
        act[GUARD : GUARD + f.rows, :] = low.astype(F32)
        for k, step in enumerate(steps):
            moved[k] = f.shifted(act, *step).astype(BF16)

    tile = out_ref.shape[1]
    mask = spread(mask_ref[...], tile)
    norm = Norm(in_stats, in_affine, in_count)
    total = jnp.zeros((1, tile), F32)
    total_hat = jnp.zeros((1, tile), F32)
    for phase in range(stride * stride):
        acc = None
        for tap, (p, q) in enumerate(TAPS):
            if stride == 2:
                if phase != 2 * (p != 1) + (q != 1):
                    continue
                step = (int(p == 0), int(q == 0))
            else:
                step = (1 - p, 1 - q)
            part = dot(moved[steps.index(step)], tap_of(w_ref, tap), NT)
            acc = part if acc is None else acc + part
        at = phase * f.rows
        hat = norm.hat(in_ref[at : at + f.rows, :])
        d = acc * slope(norm.scaled(hat)) * mask
        out_ref[at : at + f.rows, :] = d
        total += column_sum(d)
        total_hat += column_sum(d * hat)
    new_ref[0:1, :] = total
    new_ref[1:2, :] = total_hat


def conv_back(f, stride, count, in_count, d, pre, stats, affine, sums, w, inside, istats, iaffine, mask, tile=256, after=()):
    c = n = d.shape[1]
    phases = stride * stride
    return call(
        functools.partial(conv_back_kernel, f, stride, count, in_count),
        (c // tile,),
        [whole(a) for a in (d, pre, stats, affine, sums)]
        + [w.taps_by_row(tile)]
        + [cols(a, tile) for a in (inside, istats, iaffine)]
        + [whole(mask)],
        [
            out_whole((f.rows, n), BF16),
            out_cols((phases * f.rows, c), F32, tile),
            out_cols((2, c), F32, tile),
        ],
        [
            pltpu.VMEM((f.rows + 2 * GUARD, n), F32),
            pltpu.VMEM((4 if stride == 2 else 9, f.rows, n), BF16),
        ],
        us=7.2,
        after=after,
    )


def mix_back_kernel(
    f, count, d_ref, mix_ref, stats_ref, affine_ref, sums_ref, w_ref, back_ref, slope_ref,
    pre_ref, exp_ref, exp_stats, exp_affine, skip_ref, skip_stats, skip_affine, mask_ref,
    low_ref, out_ref, new_ref,
):
    @pl.when(pl.program_id(0) == 0)
    def _():
        norm = Norm(stats_ref, affine_ref, count)
        hat = norm.hat(mix_ref[...])
        d = norm.backward(d_ref[...], hat, sums_ref)
        low_ref[...] = (d * spread(mask_ref[...], hat.shape[1])).astype(BF16)

    g = f.to_rows(back_ref[...]) * slope_ref[...] + dot(low_ref[...], flat(w_ref), NT)
    g = g * slope(pre_ref[...]) * spread(mask_ref[...], g.shape[1])
    out_ref[...] = g
    first = Norm(exp_stats, exp_affine, count)
    second = Norm(skip_stats, skip_affine, count)
    new_ref[0:1, :] = column_sum(g)
    new_ref[1:2, :] = column_sum(g * first.hat(exp_ref[...]))
    new_ref[2:3, :] = column_sum(g * second.hat(skip_ref[...]))


def mix_back(
    f, count, d, mixing, stats, affine, sums, w, back, slopes, pre,
    expanded, estats, eaffine, skipped, sstats, saffine, mask, tile=512, after=()):
    n, c = expanded.shape[1], d.shape[1]
    return call(
        functools.partial(mix_back_kernel, f, count),
        (n // tile,),
        [whole(a) for a in (d, mixing, stats, affine, sums)]
        + [w.row_tile()]
        + [cols(a, tile) for a in (back, slopes, pre, expanded, estats, eaffine, skipped, sstats, saffine)]
        + [whole(mask)],
        [
            out_whole((f.rows, c), BF16),
            out_cols((f.rows, n), F32, tile),
            out_cols((3, n), F32, tile),
        ],
        us=9.8,
        after=after,
    )


def block_back_kernel(
    f, count, g_ref, exp_ref, exp_stats, exp_affine, skip_ref, skip_stats, skip_affine,
    sums_ref, w_ref, turn_ref, turn_stats, turn_affine, mask_ref,
    exp_low, skip_low, out_ref, new_ref,
):
    g = g_ref[...]
    mask = spread(mask_ref[...], g.shape[1])
    sums = sums_ref[...]
    first = Norm(exp_stats, exp_affine, count)
    low = (first.backward(g, first.hat(exp_ref[...]), sums[0:2]) * mask).astype(BF16)
    exp_low[...] = low
    second = Norm(skip_stats, skip_affine, count)
    other = jnp.concatenate([sums[0:1], sums[2:3]], 0)
    skip_low[...] = (second.backward(g, second.hat(skip_ref[...]), other) * mask).astype(BF16)
    finish_back(
        pl.program_id(0), dot(low, flat(w_ref), NT), turn_ref, turn_stats, turn_affine,
        count, mask_ref, out_ref, new_ref,
    )


def block_back(
    f, count, g, expanded, estats, eaffine, skipped, sstats, saffine, sums, w,
    turned, tstats, taffine, mask, tile=512, after=()):
    c, n = turned.shape[1], w.steps * tile
    return call(
        functools.partial(block_back_kernel, f, count),
        (n // tile,),
        [cols(a, tile) for a in (g, expanded, estats, eaffine, skipped, sstats, saffine, sums)]
        + [w.column_tile()]
        + [whole(a) for a in (turned, tstats, taffine, mask)],
        [
            out_cols((f.rows, n), BF16, tile),
            out_cols((f.rows, n), BF16, tile),
            out_whole((f.rows, c), F32),
            out_whole((2, c), F32),
        ],
        us=8.8,
        after=after,
    )


def sub_kernel(low_ref, w_ref, out_ref):
    part = dot(low_ref[...], flat(w_ref), NT)

    @pl.when(pl.program_id(0) == 0)
    def _():
        out_ref[...] = part

    @pl.when(pl.program_id(0) > 0)
    def _():
        out_ref[...] += part


def sub_back(low, w, c, tile=512, after=()):
    return call(
        functools.partial(sub_kernel),
        (w.steps,),
        [cols(low, tile), w.column_tile()],
        [out_whole((low.shape[0], c), F32)],
        us=0.1,
        after=after,
    )[0]


def input_low_kernel(f, count, d_ref, pre_ref, stats_ref, affine_ref, sums_ref, mask_ref, low_ref):
    norm = Norm(stats_ref, affine_ref, count)
    mask = spread(mask_ref[...], d_ref.shape[1])
    for phase in range(4):
        at = phase * f.rows
        hat = norm.hat(pre_ref[at : at + f.rows, :])
        d = norm.backward(d_ref[at : at + f.rows, :], hat, sums_ref)
        low_ref[at : at + f.rows, :] = (d * mask).astype(BF16)


def input_low(f, count, d, pre, stats, affine, sums, mask, tile=256, after=()):
    return call(
        functools.partial(input_low_kernel, f, count),
        (d.shape[1] // tile,),
        [cols(a, tile) for a in (d, pre, stats, affine, sums)] + [whole(mask)],
        [out_cols(d.shape, BF16, tile)],
        us=0.1,
        after=after,
    )[0]


def input_back_kernel(f, low_ref, w_ref, sub_ref, large_ref, small_ref, lt, st, acc):
    for phase in range(4):
        at = phase * f.rows
        part = dot(low_ref[at : at + f.rows, :], w_ref[...], NT)
        if phase == 0:
            part = part + sub_ref[...]
        acc[at : at + f.rows, :] = part
    for k, lane in enumerate(lanes(acc.shape[1])):
        for large, n, row, pw, at, pitch in parity_pieces(f):
            t = lt if large else st
            t[k, n, row, pl.ds(pw, pitch, stride=2), :] = acc[at : at + pitch, lane]
        large_ref[:, :, :, lane] = lt[k, :, :, 0 : f.large_in, :].astype(BF16)
        small_ref[:, :, :, lane] = st[k, :, :, 0 : f.small_in, :].astype(BF16)


def input_back(f, low, w, sub, tile=256, after=()):
    n, c = w.shape
    return call(
        functools.partial(input_back_kernel, f),
        (n // tile,),
        [whole(low), rows(w, tile), cols(sub, tile)],
        [
            out_cols((f.large, f.large_in, f.large_in, n), BF16, tile),
            out_cols((f.small, f.small_in, f.small_in, n), BF16, tile),
        ],
        parity_scratch(f, tile),
        us=0.1,
        after=after,
    )


def assemble_kernel(axis, rows, place_ref, own_ref, other_ref, out_ref, sems):
    copies = []
    for m in range(32):
        c, j, k = m & 1, (m >> 1) & 3, m >> 3
        src = (other_ref if c else own_ref).at[j, k]
        at = pl.ds(pl.multiple_of((place_ref[2] ^ m) * rows, 16), rows)
        dst = out_ref.at[at, :] if axis == 0 else out_ref.at[:, at, :]
        copies.append(pltpu.make_async_copy(src, dst, sems.at[m]))
    for copy in copies:
        copy.start()
    for copy in copies:
        copy.wait()


def assemble(place, own, other, after=()):
    block = own.shape[2:]
    axis = len(block) - 2
    shape = block[:axis] + (32 * block[axis],) + block[axis + 1 :]
    return pl.pallas_call(
        skipping(functools.partial(assemble_kernel, axis, block[axis]), 3, len(after)),
        name="assemble",
        in_specs=[IN_SMEM] + [IN_PLACE] * (2 + len(after)),
        out_specs=IN_PLACE,
        out_shape=jax.ShapeDtypeStruct(shape, own.dtype),
        scratch_shapes=[pltpu.SemaphoreType.DMA((32,))],
        compiler_params=pltpu.CompilerParams(vmem_limit_bytes=4 * 1024 * 1024),
        cost_estimate=cost(3.5),
    )(place, own, other, *after)


def pack_kernel(bases, place_ref, *refs):
    shards, out_ref = refs[:-1], refs[-1]
    out_ref[...] = jnp.zeros_like(out_ref)
    for base, shard in zip(bases, shards):
        rows = shard.shape[-2] // 4
        at = pl.ds(pl.multiple_of(place_ref[1] * rows, 16), rows)
        by_tap = len(shard.shape) == 3
        for k in range(shard.shape[0] if by_tap else shard.shape[1] // out_ref.shape[1]):
            width = out_ref.shape[1]
            value = shard[k, at, :] if by_tap else shard[at, k * width : (k + 1) * width]
            out_ref[base + k * rows : base + (k + 1) * rows, :] = value


def pack(place, shards, bases, shape, after=()):
    in_vmem = pl.BlockSpec(memory_space=pltpu.VMEM)
    return pl.pallas_call(
        skipping(functools.partial(pack_kernel, bases), 1 + len(shards), len(after)),
        name="pack",
        in_specs=[IN_SMEM] + [in_vmem] * len(shards) + [IN_PLACE] * len(after),
        out_specs=in_vmem,
        out_shape=jax.ShapeDtypeStruct(shape, BF16),
        compiler_params=pltpu.CompilerParams(vmem_limit_bytes=VMEM_LIMIT),
        cost_estimate=cost(2),
    )(place, *shards, *after)


def cut_kernel(number, place_ref, *refs):
    ins, outs, sems = refs[:number], refs[number : 2 * number], refs[2 * number]
    copies = []
    for k in range(number):
        rows = outs[k].shape[-2]
        at = pl.ds(pl.multiple_of(place_ref[1] * rows, 16), rows)
        src = ins[k].at[at, :] if len(ins[k].shape) == 2 else ins[k].at[:, at, :]
        copies.append(pltpu.make_async_copy(src, outs[k], sems.at[k]))
    for copy in copies:
        copy.start()
    for copy in copies:
        copy.wait()


def cut(place, shards, after=()):
    shapes = [s.shape[:-2] + (s.shape[-2] // 4, s.shape[-1]) for s in shards]
    number = len(shards)
    return pl.pallas_call(
        skipping(functools.partial(cut_kernel, number), 1 + number, len(after)),
        name="cut",
        in_specs=[IN_SMEM] + [IN_PLACE] * (number + len(after)),
        out_specs=[IN_PLACE] * number,
        out_shape=[jax.ShapeDtypeStruct(s, BF16) for s in shapes],
        scratch_shapes=[pltpu.SemaphoreType.DMA((number,))],
        compiler_params=pltpu.CompilerParams(vmem_limit_bytes=4 * 1024 * 1024),
        cost_estimate=cost(0.7),
    )(place, *shards, *after)


def unpack_kernel(kinds, place_ref, own_ref, other_ref, *outs):
    core = place_ref[1] % 2
    for ref, c in ((own_ref, core), (other_ref, 1 - core)):
        at = 0
        for (steps, rows, by_tap), out in zip(kinds, outs):
            there = pl.ds(pl.multiple_of(c * rows, 16), rows)
            for k in range(steps):
                value = ref[at : at + rows, :].astype(F32)
                if by_tap:
                    out[k, there, :] = value
                else:
                    out[there, k * 512 : (k + 1) * 512] = value
                at += rows


def unpack(place, own, other, kinds):
    in_vmem = pl.BlockSpec(memory_space=pltpu.VMEM)
    shapes = [(n, 2 * r, 512) if by_tap else (2 * r, n * 512) for n, r, by_tap in kinds]
    return pl.pallas_call(
        functools.partial(unpack_kernel, kinds),
        name="unpack",
        in_specs=[IN_SMEM, in_vmem, in_vmem],
        out_specs=[in_vmem] * len(kinds),
        out_shape=[jax.ShapeDtypeStruct(s, F32) for s in shapes],
        compiler_params=pltpu.CompilerParams(vmem_limit_bytes=VMEM_LIMIT),
        cost_estimate=cost(0.1),
    )(place, own, other)


def local_kernel(function, number, *refs):
    ins, outs = refs[:number], refs[number:]
    for out, value in zip(outs, function(*[r[...] for r in ins])):
        out[...] = value


def local(function, arrays, after=(), name="local", us=0.1):
    shapes = jax.eval_shape(function, *arrays)
    in_vmem = pl.BlockSpec(memory_space=pltpu.VMEM)
    kernel = functools.partial(local_kernel, function, len(arrays))
    return pl.pallas_call(
        skipping(kernel, len(arrays), len(after)),
        name=name,
        in_specs=[in_vmem] * len(arrays) + [IN_PLACE] * len(after),
        out_specs=[in_vmem] * len(shapes),
        out_shape=list(shapes),
        compiler_params=pltpu.CompilerParams(vmem_limit_bytes=VMEM_LIMIT),
        cost_estimate=cost(us),
    )(*arrays, *after)


def nothing(*refs):
    del refs


def pin(v, after):
    if not after:
        return v
    return pl.pallas_call(
        nothing,
        name="pin",
        in_specs=[IN_PLACE] * (1 + len(after)),
        out_specs=IN_PLACE,
        out_shape=jax.ShapeDtypeStruct(v.shape, v.dtype),
        input_output_aliases={0: 0},
        compiler_params=pltpu.CompilerParams(vmem_limit_bytes=4 * 1024 * 1024),
        cost_estimate=cost(0.5),
    )(v, *after)


def weight_kernel(by_tap, rows, halves, place_ref, left_ref, right_ref, keep_ref, send_ref, acc):
    acc[...] = dot(left_ref[...], right_ref[...], TN)
    for m in range(32):
        if halves:
            if m >= 16:
                break
            img, c = m >> 1, m & 1
            at, place = img * 2 + ((place_ref[1] % 2) ^ c), (img,)
        else:
            at, c, place = place_ref[2] ^ m, m & 1, ((m >> 1) & 3, m >> 3)
            place = place + (0,) if by_tap else place
        block = acc[pl.ds(pl.multiple_of(at * rows, 16), rows), :].astype(BF16)
        (send_ref if c else keep_ref)[place] = block


def weight_grad(place, left, right, taps=1, halves=False, us=None, tile=512):
    k, n = left.shape[1] // taps, right.shape[1]
    rows = k // (16 if halves else 32)
    if taps == 1:
        steps = n // tile
        left_in = (right.shape[0], k), lambda i: (0, 0)
        right_in = (right.shape[0], tile), lambda i: (0, i)
        shape, block = (4, 4, rows, n), (4, 4, rows, tile)
        out_map = lambda i: (0, 0, 0, i)
    else:
        steps, tile = taps, n
        left_in = (right.shape[0], k), lambda i: (0, i)
        right_in = right.shape, lambda i: (0, 0)
        shape, block = (4, 4, taps, rows, n), (4, 4, 1, rows, n)
        out_map = lambda i: (0, 0, i, 0, 0)
    if halves:
        shape, block = (8, steps * rows, tile), (8, rows, tile)
        out_map = lambda i: (0, i, 0)
    return pl.pallas_call(
        functools.partial(weight_kernel, taps > 1, rows, halves),
        name="weight_grad",
        grid=(steps,),
        in_specs=[IN_SMEM, pl.BlockSpec(*left_in), pl.BlockSpec(*right_in)],
        out_specs=[pl.BlockSpec(block, out_map)] * 2,
        out_shape=[jax.ShapeDtypeStruct(shape, BF16)] * 2,
        scratch_shapes=[pltpu.VMEM((k, tile), F32)],
        compiler_params=pltpu.CompilerParams(vmem_limit_bytes=VMEM_LIMIT),
        cost_estimate=cost(us or (10 if taps > 1 else 5)),
    )(place, left, right)


class Links:
    def __init__(self):
        self.img, self.blk = lax.axis_size("img"), lax.axis_size("blk")
        self.size = self.img * self.blk
        self.me = lax.axis_index("img") * self.blk + lax.axis_index("blk")
        low, high = self.blk.bit_length() - 1, self.img.bit_length() - 1
        self.low, self.high = low, high

    def swap(self, v, bits):
        return lax.ppermute(v, AXES, [(i, i ^ bits) for i in range(self.size)])

    def stages(self):
        found = []

        def cut(start, number):
            if number % 2 and number > 1:
                found.append([1 << start])
                start, number = start + 1, number - 1
            while number > 0:
                take = min(2, number)
                found.append([1 << (start + k) for k in range(take)])
                start, number = start + take, number - take

        cut(0, self.low)
        cut(self.low, self.high)
        return found

    def partners(self, v, stage):
        if len(stage) == 1:
            return [self.swap(v, stage[0])]
        a, b = stage
        return [self.swap(v, a), self.swap(v, b), self.swap(v, a | b)]

    def total(self, v):
        return self.end_total(self.begin_total(v))

    def begin_total(self, v):
        return self.add_stages(v, self.stages()[:1])

    def end_total(self, v):
        return self.add_stages(v, self.stages()[1:])

    def add_stages(self, v, stages):
        for stage in stages:
            got = self.partners(v, stage)
            if len(got) == 1:
                v = v + got[0]
            else:
                v = (v + got[0]) + (got[1] + got[2])
        return v

    def moments(self, v, count):
        for stage in self.stages():
            got = [v] + self.partners(v, stage)
            if len(got) == 2:
                a, b = got
                center = (a[0] + b[0]) * 0.5
                square = (a[1] + b[1]) + count * (
                    jnp.square(a[0] - center) + jnp.square(b[0] - center)
                )
            else:
                a, b, c, d = got
                center = ((a[0] + b[0]) + (c[0] + d[0])) * 0.25
                square = ((a[1] + b[1]) + (c[1] + d[1])) + count * (
                    (jnp.square(a[0] - center) + jnp.square(b[0] - center))
                    + (jnp.square(c[0] - center) + jnp.square(d[0] - center))
                )
            count = count * len(got)
            v = jnp.stack([center, square])
        return v

    def from_each(self, v, bits):
        return [v] + [self.swap(v, b) for b in bits]

    def across(self, own):
        return self.swap(own, 1)

    def joined(self, parts):
        a, b, c, d = parts
        core, y = self.me & 1, (self.me >> 1) & 1
        pick = lambda bit, p, q: (jnp.where(bit == 0, p, q), jnp.where(bit == 0, q, p))
        a, b = pick(core, a, b)
        c, d = pick(core, c, d)
        a, c = pick(y, a, c)
        b, d = pick(y, b, d)
        return jnp.concatenate([a, b, c, d], a.ndim - 2).astype(F32)

    def scatter_plain(self, left, right, taps=1):
        g = dot(left[: right.shape[0]], right, TN).astype(BF16)
        if taps > 1:
            g = g.reshape(taps, left.shape[1] // taps, -1)
        g = lax.psum_scatter(g, "img", scatter_dimension=int(taps > 1), tiled=True)
        return lax.psum(g, "blk").astype(F32)

    def gather(self, v):
        depth = 0
        for bit in reversed(range(self.low + self.high)):
            got = self.swap(v, 1 << bit)
            upper = (self.me >> bit) & 1
            v = jnp.stack(
                [jnp.where(upper == 0, v, got), jnp.where(upper == 0, got, v)], depth
            )
            depth += 1
        return v.reshape((self.size,) + v.shape[depth:])


class Weights:
    def __init__(self, links, place, staged, shards):
        self.links, self.place, self.staged, self.shards = links, place, staged, shards
        self.now = {}

    def whole(self, name):
        shard = self.shards[name]
        return lax.all_gather(shard, "img", axis=shard.ndim - 2, tiled=True)

    def first(self, name, during):
        if not self.staged:
            return self.whole(name), during(())
        (block,) = cut(self.place, [self.shards[name]])
        z = self.links.from_each(block, (8, 16, 24))
        x = during((block,))
        (z,) = local(lambda *v: [jnp.stack(v)], z, (x,), "stack")
        plane = self.links.from_each(z, (2, 4, 6))
        (own,) = local(lambda *v: [jnp.stack(v)], plane, (), "stack")
        return assemble(self.place, own, self.links.across(own)), x

    def fetch(self, bases, height, after=()):
        names = list(bases)
        if self.staged:
            shards = [self.shards[n] for n in names]
            own = pack(self.place, shards, list(bases.values()), (height, 512), after)
            buffer = lax.all_gather(own, AXES)
        else:
            own, at, blocks = None, 0, []
            for n in names:
                w = self.whole(n)
                if w.ndim == 2:
                    w = w.reshape(w.shape[0], -1, 512).transpose(1, 0, 2)
                w = w.reshape(w.shape[0], 32, -1, 512).transpose(1, 0, 2, 3).reshape(32, -1, 512)
                blocks += [jnp.zeros((32, bases[n] - at, 512), BF16), w]
                at = bases[n] + w.shape[1]
            blocks.append(jnp.zeros((32, height - at, 512), BF16))
            buffer = jnp.concatenate(blocks, 1)
        for n in names:
            shard = self.shards[n]
            rows = shard.shape[-2] * self.links.img // 32
            steps = shard.shape[0] if shard.ndim == 3 else shard.shape[1] // 512
            self.now[n] = Packed(buffer, bases[n], rows, steps)
        return () if own is None else (own,)

    def fetch_rows(self, name, after=()):
        if not self.staged:
            self.now[name] = self.whole(name)
            return ()
        (own,) = cut(self.place, [self.shards[name]], after)
        self.now[name] = lax.all_gather(own, AXES, axis=0, tiled=True)
        return (own,)


class Sums:
    def __init__(self, links, place, staged):
        self.links, self.place, self.staged = links, place, staged
        self.now = {}

    def start(self, name, left, right, taps=1, halves=False, us=None):
        if self.staged:
            self.now[name] = weight_grad(self.place, left, right, taps, halves, us)
        else:
            self.now[name] = self.links.scatter_plain(left, right, taps)

    def swap(self, name):
        if self.staged:
            keep, send = self.now[name]
            self.now[name] = keep, self.links.across(send)

    def in_plane(self, name, after=()):
        if self.staged:
            fold = lambda keep, got: [add2(keep[j], got[j]) for j in range(4)]
            part = local(fold, self.now[name], after, "fold")
            self.now[name] = [part[0]] + [self.links.swap(part[j], 2 * j) for j in (1, 2, 3)]

    def along_z(self, name, after=()):
        if self.staged:
            fold = lambda *got: [sum4([g[k] for g in got]) for k in range(4)]
            part = local(fold, self.now[name], after, "fold")
            self.now[name] = [part[0]] + [self.links.swap(part[k], 8 * k) for k in (1, 2, 3)]

    def join(self, name, after=()):
        if self.staged:
            (part,) = local(lambda *got: [sum4(got)], self.now[name], after, "fold")
            self.now[name] = self.links.from_each(part, (1, 2, 3))

    def scatter(self, *names, after=()):
        if self.staged:
            parts = [p for n in names for p in self.now[n]]
            join = lambda *v: [jnp.concatenate([add2(a, b) for a, b in zip(v[::2], v[1::2])], 1)]
            (part,) = local(join, parts, after, "fold", 4)
            self.now[names] = lax.psum_scatter(part, "img", scatter_dimension=0, tiled=False)
            return (part,)
        return ()

    def across_y(self, *names):
        if self.staged:
            own = self.now[names]
            self.now[names] = own, self.links.swap(own, 2)

    def across_cores(self, *names, after=()):
        if self.staged:
            (own,) = local(lambda a, b: [add2(a, b)], self.now[names], after, "fold")
            self.now[names] = own, self.links.across(own)

    def split(self, names, kinds):
        if not self.staged:
            return [self.now[n] for n in names]
        return unpack(self.place, *self.now[names], kinds)

    def state(self, *names):
        return tuple(jax.tree.leaves([self.now[n] for n in names])) if self.staged else ()

    def get(self, name):
        if not self.staged:
            return self.now[name]
        return self.links.joined(self.now[name])


def add2(a, b):
    return (a.astype(F32) + b.astype(F32)).astype(BF16)


def sum4(v):
    a, b, c, d = [x.astype(F32) for x in v]
    return ((a + b) + (c + d)).astype(BF16)


def head_plain(f, links, pooled, hidden, embed, affine, labels):
    number = links.size * f.views
    line = dot(pooled, hidden)
    center = lax.psum(jnp.sum(line, 0), AXES) / number
    line = line - center
    factor = lax.rsqrt(lax.psum(jnp.sum(line * line, 0), AXES) / number + EPSILON)
    hat = line * factor
    v = hat * affine[0] + affine[1]
    low = (v * sigmoid(v)).astype(BF16)
    e = dot(low, embed)
    inverse = lax.rsqrt(jnp.sum(e * e, 1, keepdims=True) + NORM_EPSILON)
    unit = e * inverse
    lowered = unit.astype(BF16)
    every = lax.all_gather(lowered, AXES, axis=0, tiled=True)
    every_label = lax.all_gather(labels, AXES, axis=0, tiled=True)
    scores = dot(lowered, every, NT) / SOFTMAX_TEMP
    anchor = links.me * f.views + jnp.arange(f.views, dtype=jnp.int32)
    itself = anchor[:, None] == jnp.arange(number, dtype=jnp.int32)[None, :]
    paired = (labels[:, None] == every_label[None, :]) & jnp.logical_not(itself)
    masked = jnp.where(itself, MASKED, scores)
    top = jnp.max(masked, 1)
    log_total = top + jnp.log(jnp.sum(jnp.where(itself, 0.0, jnp.exp(masked - top[:, None])), 1))
    positive = jnp.sum(jnp.where(paired, scores, 0.0), 1)
    loss = lax.psum(jnp.sum(log_total - positive / POSITIVES), AXES) / number
    every_log = lax.all_gather(log_total, AXES, axis=0, tiled=True)

    def pair_grad(logs):
        chance = jnp.where(itself, 0.0, jnp.exp(scores - logs))
        return ((chance - paired.astype(F32) / POSITIVES) / number).astype(BF16)

    unit_grad = (
        dot(pair_grad(log_total[:, None]), every) + dot(pair_grad(every_log[None, :]), every)
    ) / SOFTMAX_TEMP
    along = jnp.sum(unit * unit_grad, 1, keepdims=True)
    grad = (inverse * (unit_grad - unit * along)).astype(BF16)
    d = dot(grad, embed, NT) * slope(v)
    shift_grad = lax.psum(jnp.sum(d, 0), AXES)
    gain_grad = lax.psum(jnp.sum(d * hat, 0), AXES)
    back = (affine[0] * factor * (d - shift_grad / number - hat * (gain_grad / number))).astype(BF16)
    return loss, back, low, grad, gain_grad, shift_grad, dot(back, hidden, NT)


def per_device(
    x_large, x_small, large_image, small_image,
    first_reduce, first_spatial, first_expand, first_short,
    second_reduce, second_spatial, second_expand, head_hidden, head_embed,
    norm_gain, norm_shift,
):
    f = Frames(x_large, x_small)
    links = Links()
    mid, wide, proj = first_reduce.shape[1], first_short.shape[1], head_hidden.shape[1]
    widths = [mid, mid, wide, wide, mid, mid, wide, proj]
    starts = np.cumsum([0] + widths)
    both = jnp.stack([norm_gain, norm_shift])
    affine = [both[:, starts[k] : starts[k + 1]] for k in range(8)]
    mask = f.mask()

    place = jnp.stack([lax.axis_index("img"), lax.axis_index("blk"), links.me]).astype(jnp.int32)
    kernel_shape = (9,) + first_spatial.shape[2:]
    shards = {
        "reduce": first_reduce,
        "spatial": first_spatial.reshape(kernel_shape),
        "expand": first_expand,
        "short": first_short,
        "reduce2": second_reduce,
        "spatial2": second_spatial.reshape(kernel_shape),
        "expand2": second_expand,
        "head": jnp.concatenate([head_hidden, head_embed], 1),
    }
    staged = links.img == 8 and links.blk == 4
    staged = staged and all(w.shape[-2] % 64 == 0 for w in shards.values())
    weights = Weights(links, place, staged, shards)
    sums = Sums(links, place, staged)
    n_in, n_out = 4 * f.valid, f.valid
    all_in, all_out = n_in * links.size, n_out * links.size

    first = {"expand": 0, "reduce2": 64, "spatial": 144, "short": 288}
    second = {"spatial2": 0, "expand2": 144}
    weights.fetch(first, 416)
    w = weights.now
    w_reduce, x = weights.first(
        "reduce", lambda after: split_cells(f, x_large, x_small, after=after)
    )
    second_own = weights.fetch(second, 208, after=(x,))
    reduce_in = (w_reduce, (w_reduce.shape[0], 256), lambda i: (0, i))
    reduced, part0 = linear(f, x, reduce_in, mid, mask, 4, 256, after=second_own)
    st0 = links.moments(part0, n_in)
    head_own = weights.fetch_rows("head", after=(part0,))
    patch1, turned, part1 = conv(
        f, 2, all_in, reduced, st0, affine[0], w["spatial"], mask, after=head_own
    )
    st1 = links.moments(part1, n_out)
    turned_low, expanded, part2 = expand(f, all_out, turned, st1, affine[1], w["expand"], mask)
    skipped, part3 = linear(
        f, x, w["short"].column_tile(), wide, mask, 1, 512, after=(part2,)
    )
    joint = links.moments(jnp.concatenate([part2, part3], 1), n_out)
    st2, st3 = joint[:, :wide], joint[:, wide:]
    block_low, block_pre, mixing, part4 = mix(
        f, all_out, expanded, skipped, st2, affine[2], st3, affine[3], w["reduce2"], mask
    )
    st4 = links.moments(part4, n_out)
    patch2, rotated, part5 = conv(f, 1, all_out, mixing, st4, affine[4], w["spatial2"], mask)
    st5 = links.moments(part5, n_out)
    rotated_low, widened, part6 = expand(f, all_out, rotated, st5, affine[5], w["expand2"], mask)
    st6 = links.moments(part6, n_out)
    pooled, slopes, view_sums = pool(f, all_out, widened, block_pre, st6, affine[6], mask)
    pooled = pooled.astype(BF16)
    labels = jnp.concatenate([large_image, small_image], 0)
    w_head = w["head"]

    shard = head_hidden.shape[0]
    if staged:
        digits = jnp.concatenate([labels, jnp.full((SLOT - f.views,), -1, jnp.int32)])
        digits = jnp.stack([digits // 256, digits % 256], 1).astype(BF16)
        pooled = jnp.concatenate([pooled, jnp.pad(digits, ((0, 0), (0, 126)))], 1)
        every = jnp.stack(links.from_each(pooled, (8, 16, 24)))
        every = jnp.stack(links.from_each(every, (2, 4, 6)))
        every = every, links.across(every)
        loss, hidden_grad, embed_grad, gains7, back, sums6 = head(
            f, links.size, shard, place, every, w_head, affine[7], view_sums
        )
        loss = loss[0, 0]
        gain7, shift7 = gains7[0], gains7[1]
    else:
        pooled = pooled[: f.views]
        loss, hidden_back, head_low, embed_back, gain7, shift7, back = head_plain(
            f, links, pooled, w_head[:, :proj], w_head[:, proj:], affine[7], labels
        )
        back = jnp.pad(back, ((0, SLOT - f.views), (0, 0))) * f.cells()
        sums6 = jnp.stack([jnp.sum(back * view_sums[:SLOT], 0), jnp.sum(back * view_sums[SLOT:], 0)])
        hidden_grad = links.scatter_plain(pooled, hidden_back)
        embed_grad = links.scatter_plain(head_low, embed_back)
    sums6 = links.total(sums6)

    widened_back, d5, part5 = widen_back(
        f, all_out, widened, slopes, back, st6, affine[6], sums6, w["expand2"], rotated, st5, affine[5], mask
    )
    sums.start("expand2", rotated_low, widened_back, halves=True)
    started = sums.state("expand2")
    sums.swap("expand2")
    sums5 = links.total(part5)
    rotated_back, d4, part4 = conv_back(
        f, 1, all_out, all_out, d5, rotated, st5, affine[5], sums5, w["spatial2"], mixing, st4, affine[4],
        mask, after=started,
    )
    sums.start("spatial2", patch2, rotated_back, 9, halves=True)
    sums.swap("spatial2")
    first = ("expand2", "spatial2")
    first_own = sums.scatter(*first)
    sums4 = links.total(pin(part4, first_own))
    mixing_back, block_grad, part23 = mix_back(
        f, all_out, d4, mixing, st4, affine[4], sums4, w["reduce2"], back, slopes, block_pre,
        expanded, st2, affine[2], skipped, st3, affine[3], mask, after=first_own,
    )
    sums.start("reduce2", block_low, mixing_back, halves=True)
    started = sums.state("reduce2")
    sums.swap("reduce2")
    sums23 = links.total(part23)
    expanded_back, skipped_back, d1, part1 = block_back(
        f, all_out, block_grad, expanded, st2, affine[2], skipped, st3, affine[3], sums23, w["expand"],
        turned, st1, affine[1], mask, after=started,
    )
    sums.start("expand", turned_low, expanded_back, halves=True)
    sums.swap("expand")
    sums.start("short", x, skipped_back, halves=True)
    sums.swap("short")
    sums1 = links.total(part1)
    second = ("reduce2", "expand", "short")
    second_own = sums.scatter(*second)
    turned_back, d0, part0 = conv_back(
        f, 2, all_out, all_in, d1, turned, st1, affine[1], sums1, w["spatial"], reduced, st0, affine[0], mask,
        after=second_own + sums.state(first),
    )
    sums.start("spatial", patch1, turned_back, 9)
    sums.swap("spatial")
    sums0 = links.total(part0)
    sums.in_plane("spatial")
    reduced_back = input_low(
        f, all_in, d0, reduced, st0, affine[0], sums0, mask, after=sums.state("spatial")[:1]
    )
    sums.start("reduce", x, reduced_back, us=0.1)
    sums.swap("reduce")
    sub = sub_back(skipped_back, w["short"], x.shape[1], after=(reduced_back,))
    grad_large, grad_small = input_back(f, reduced_back, w_reduce, sub)
    sums.along_z("spatial", after=(grad_small,))
    sums.in_plane("reduce", after=sums.state("spatial")[:1])
    sums.across_y(*first)
    sums.across_y(*second)
    sums.along_z("reduce")
    sums.across_cores(*second)
    sums.join("spatial", after=sums.state(second)[:1])
    sums.across_cores(*first)
    sums.join("reduce")
    part = lambda n: n // 16
    expand2_grad, spatial2_grad = sums.split(
        first, [(wide // 512, part(mid), False), (9, part(mid), True)]
    )
    reduce2_grad, expand_grad, short_grad = sums.split(
        second, [(1, part(wide), False), (wide // 512, part(mid), False), (wide // 512, part(2 * mid), False)]
    )
    reduce_grad, spatial_grad = sums.get("reduce"), sums.get("spatial")

    gain_grads = jnp.concatenate(
        [sums0[1], sums1[1], sums23[1], sums23[2], sums4[1], sums5[1], sums6[1], gain7]
    )
    shift_grads = jnp.concatenate(
        [sums0[0], sums1[0], sums23[0], sums23[0], sums4[0], sums5[0], sums6[0], shift7]
    )
    return (
        loss, grad_large, grad_small, reduce_grad, spatial_grad.reshape(first_spatial.shape), expand_grad, short_grad,
        reduce2_grad, spatial2_grad.reshape(first_spatial.shape), expand2_grad, hidden_grad, embed_grad, gain_grads, shift_grads,
    )


def solution(mesh):
    image = P(("img", "blk"), None, None, None)
    label = P(("img", "blk"))
    matrix = P("img", None)
    kernel = P(None, None, "img", None)
    weights = (matrix, kernel, matrix, matrix, matrix, kernel, matrix, matrix, matrix)
    return jax.shard_map(
        per_device,
        mesh=mesh,
        in_specs=(image, image, label, label) + weights + (P(), P()),
        out_specs=(P(), image, image) + weights + (P(), P()),
        check_vma=False,
    )
```
